32 devices in a mesh: scene: 2 (over y), row: 16 (over z, x, core).
Axes of the slice: x: 2, y: 2, z: 4, core: 2. Of those that a mesh axis runs over, the one named last changes fastest.
Arguments:
- adjoint_seed: float32 [64, 8192], P(None, ('scene', 'row')), parts along dimension 1, may hold values from -1 to 1
- radiosity: bfloat16 [64, 8192], P(None, ('scene', 'row')), parts along dimension 1, may hold values from -6 to 6
- emission: bfloat16 [64, 8192], P(None, ('scene', 'row')), parts along dimension 1, may hold values from -6 to 6
- reflectance: float32 [8192], P(('scene', 'row')), parts along dimension 0, may hold values from 0.2 to 0.9
- area: float32 [8192], P(('scene', 'row')), parts along dimension 0, may hold values from 0.5 to 4
- position: float32 [3, 8192], P(None, ('scene', 'row')), parts along dimension 1, may hold values from -4 to 4
- visibility: int32 [64, 32], P(('scene', 'row')), parts along dimension 0, may hold values from -2147483648 to 2147483647, as said below
Outputs:
- adjoint_field: float32 [64, 8192], P(None, ('scene', 'row')), parts along dimension 1
- reflect_grad: float32 [8192], P(('scene', 'row')), parts along dimension 0
The draws below stay inside these ranges and needn't reach their ends.
There are 2 independent parts, one for each index of `scene`. The reference program is written for one: setup_inputs(seed, part) draws one part's arguments, and reference() takes and returns one part's arrays. A program takes and returns all parts, laid end to end along the dimension named above; each array names one. Nothing has to cross between parts.
Inputs may be any that keep to these rules, and one draw needn't show every extreme that they name: visibility is symmetric: visibility[I, J] equals visibility[J, I]; its words use all 32 bits.
All inputs are finite; a program needn't handle non-finite values.
Results may differ from the reference program's by a relative error of at most 0.0026.
Values may be sent and summed in bfloat16 or wider, within the bound.
No kernel may reach another device: no remote copies, remote signals or barrier semaphores. Data moves between devices by JAX's collectives and lax.ppermute only.
A program may use at most 64 MiB of HBM per device.

```python
import math
import jax
import jax.numpy as jnp
from jax import lax

RHS = 64
TILE = 128
SWEEPS = 2
NBLOCK = 32
PATCHES = 4096


def draw_visibility(key, part):
    key = jax.random.fold_in(key, 7)
    raw_words = jax.random.randint(key, (NBLOCK, NBLOCK), -2147483648, 2147483647, dtype=jnp.int32)
    row_ids = jnp.arange(NBLOCK, dtype=jnp.int32)[:, None]
    col_ids = jnp.arange(NBLOCK, dtype=jnp.int32)[None, :]
    words = jnp.where(row_ids <= col_ids, raw_words, raw_words.T)
    lowest = jnp.full((NBLOCK, NBLOCK), -2147483648, dtype=jnp.int32)
    highest = jnp.full((NBLOCK, NBLOCK), 2147483647, dtype=jnp.int32)
    words = jnp.where((row_ids == 0) & (col_ids == 0), lowest, words)
    words = jnp.where((row_ids == 1) & (col_ids == 1), highest, words)
    return words


def draw_adjoint_seed(key, part):
    key = jax.random.fold_in(key, 11)
    value_key = jax.random.fold_in(key, 0)
    values = jax.random.uniform(value_key, (RHS, PATCHES), jnp.float32, -1.0, 1.0)
    return values


def level_of(own_key, extent, cuts, least, top_value):
    def one(dim, shards_of):
        steps = jax.random.uniform(jax.random.fold_in(jax.random.fold_in(own_key, 6), dim), (shards_of,), jnp.float32, least / len(cuts), top_value / len(cuts))
        return jnp.repeat(jnp.exp(steps), extent[dim] // shards_of).reshape((-1,) + (1,) * (len(extent) - dim - 1))

    loudness = one(*cuts[0])
    for cut in cuts[1:]:
        loudness = loudness * one(*cut)
    return loudness


def centred(key, shape, deviation, reach, shards=(), held_as=jnp.bfloat16):
    array = jax.random.normal(key, shape, jnp.float32) * deviation
    if len(shards) > 0:
        array = level_of(key, shape, shards, -0.22, 0.18) * array
    return jnp.clip(array, min=-reach, max=reach).astype(held_as)


def setup_inputs(seed: int = 0, part: int = 0) -> dict:
    key_list = jax.random.split(jax.random.key(seed), 8)
    part_splits = jax.random.split(jax.random.fold_in(key_list[7], part), 8)
    return {
        "adjoint_seed": draw_adjoint_seed(jax.random.fold_in(jax.random.fold_in(key_list[7], part), 71), part),
        "radiosity": centred(part_splits[1], (RHS, PATCHES), 1.0, 6.0, ((1, 16),)),
        "emission": centred(part_splits[2], (RHS, PATCHES), 1.0, 6.0, ((1, 16),)),
        "reflectance": jnp.clip(jnp.exp(math.log(0.9) - 1.50407736 * jax.random.uniform(part_splits[3], (PATCHES,), jnp.float32) ** level_of(part_splits[3], (PATCHES,), ((0, 16),), -0.2, 0.2)), 0.2, 0.9),
        "area": jnp.clip(jnp.exp(math.log(4.0) - 2.0794415 * jax.random.uniform(part_splits[4], (PATCHES,), jnp.float32) ** level_of(part_splits[4], (PATCHES,), ((0, 16),), -0.2, 0.2)), 0.5, 4.0),
        "position": centred(part_splits[5], (3, PATCHES), 1.0, 4.0, ((1, 16),), jnp.float32),
        "visibility": draw_visibility(jax.random.fold_in(jax.random.fold_in(key_list[7], part), 71), part),
    }


def form_kernel(row_pos, col_pos, mask_words, row_block, col_block, tile_size):
    row_ids = (jnp.arange(row_pos.shape[1], dtype=jnp.int32) % tile_size)[:, None]
    col_ids = (jnp.arange(col_pos.shape[1], dtype=jnp.int32) % tile_size)[None, :]
    quarter = tile_size // 4
    eighth = tile_size // 8
    col_block = col_block.reshape(1, -1)
    direct = (row_block < col_block) | (row_block == col_block) & (row_ids <= col_ids)
    bit_index = jnp.where(direct, 8 * (row_ids // quarter) + col_ids // eighth, 8 * (col_ids // quarter) + row_ids // eighth).astype(jnp.int32)
    visible = jnp.right_shift(mask_words.reshape(1, -1), bit_index) & 1
    delta = row_pos[:, :, None] - col_pos[:, None, :]
    distance = lax.optimization_barrier(jnp.sum(delta * delta, axis=0))
    return (visible.astype(jnp.float32) / (1.0 + distance)).astype(jnp.bfloat16)

def reference(adjoint_seed, radiosity, emission, reflectance, area, position, visibility):
    col_block = (jnp.arange(PATCHES, dtype=jnp.int32) // TILE).astype(jnp.int32)
    adjoint = adjoint_seed
    for sweep in range(SWEEPS):
        scaled = (reflectance[None, :] * adjoint).astype(jnp.bfloat16)

        def strip(row_block):
            row_pos = lax.dynamic_slice_in_dim(position, row_block * TILE, TILE, 1)
            words_row = lax.dynamic_index_in_dim(visibility, row_block, 0, keepdims=False)
            mask_words = jnp.repeat(words_row, TILE)
            kernel = form_kernel(row_pos, position, mask_words, row_block, col_block, TILE)
            return lax.dot_general(scaled, kernel, (((1,), (1,)), ((), ())), preferred_element_type=jnp.float32)
        strips = lax.map(strip, jnp.arange(NBLOCK, dtype=jnp.int32))
        summed = jnp.transpose(strips, (1, 0, 2)).reshape(RHS, PATCHES)
        adjoint = adjoint_seed + (area / math.sqrt(PATCHES))[None, :] * summed
    change = radiosity.astype(jnp.float32) - emission.astype(jnp.float32)
    reflect_grad = lax.optimization_barrier(jnp.sum(adjoint * change, axis=0)) / reflectance
    return (adjoint, reflect_grad)
```

```python
import functools
import math

import jax
import jax.numpy as jnp
from jax import lax
from jax.experimental import pallas as pl
from jax.experimental.pallas import tpu as pltpu
from jax.sharding import PartitionSpec as P

TILE = 128
SWEEPS = 2
GROUP = 16
VMEM_BYTES = 48 * 1024 * 1024


def lane_ids(rows):
    return lax.broadcasted_iota(jnp.int32, (rows, TILE), 1)


def spread_rows(pos_ref, spread):
    for coord in range(3):
        for block in range(spread.shape[1]):
            line = pos_ref[coord : coord + 1, block * TILE : (block + 1) * TILE]
            spread[coord, block] = jnp.transpose(jnp.broadcast_to(line, (TILE, TILE)))


def inverse_square(spread, pos_ref, at, own_block, rows, other_block):
    lanes = pl.ds(other_block * TILE, TILE)
    total = 1.0
    for coord in range(3):
        delta = spread[coord, own_block, rows, :] - pos_ref[at, coord : coord + 1, lanes]
        total = total + delta * delta
    return 1.0 / total


def form_part(me, at, part, words_ref, pos_ref, spread, kernel_ref):
    blocks = spread.shape[1]
    lane = lane_ids(GROUP)
    for own_block in range(blocks):
        row_block = me * blocks + own_block
        for other_block in range(blocks):
            col_block = part * blocks + other_block
            word = words_ref[own_block, col_block]
            direct = row_block < col_block
            for group in range(TILE // GROUP):
                rows = slice(group * GROUP, (group + 1) * GROUP)
                bit = jnp.where(direct, 8 * (group // 2) + lane // 16, 8 * (lane // 32) + group)
                seen = (jnp.right_shift(word, bit) & 1) != 0
                value = inverse_square(spread, pos_ref, at, own_block, rows, other_block)
                value = jnp.where(seen, value, 0.0).astype(jnp.bfloat16)
                kernel_ref[
                    at,
                    own_block * TILE + group * GROUP : own_block * TILE + (group + 1) * GROUP,
                    other_block * TILE : (other_block + 1) * TILE,
                ] = value


def form_diagonal(me, at, words_ref, pos_ref, spread, kernel_ref):
    blocks = spread.shape[1]
    lane = lane_ids(TILE)
    row = lax.broadcasted_iota(jnp.int32, (TILE, TILE), 0)
    low, high = jnp.minimum(row, lane), jnp.maximum(row, lane)
    bit = 8 * (low // 32) + high // 16
    for block in range(blocks):
        word = words_ref[block, me * blocks + block]
        seen = (jnp.right_shift(word, bit) & 1) != 0
        value = inverse_square(spread, pos_ref, at, block, slice(0, TILE), block)
        value = jnp.where(seen, value, 0.0).astype(jnp.bfloat16)
        kernel_ref[
            at, block * TILE : (block + 1) * TILE, block * TILE : (block + 1) * TILE
        ] = value


def times_transpose(values, kernel):
    return lax.dot_general(
        values, kernel, (((1,), (1,)), ((), ())), preferred_element_type=jnp.float32
    )


def gather_sum(every_ref, kernel_ref):
    total = times_transpose(every_ref[0], kernel_ref[0])
    for at in range(1, every_ref.shape[0]):
        total += times_transpose(every_ref[at], kernel_ref[at])
    return total


def first_sweep(
    scale,
    me_ref,
    words_ref,
    own_pos_ref,
    pos_ref,
    every_ref,
    seed_ref,
    area_ref,
    reflectance_ref,
    kernel_ref,
    scaled_ref,
    spread,
    total,
):
    step = pl.program_id(0)
    chunk = pos_ref.shape[0]
    me = me_ref[0]

    @pl.when(step == 0)
    def _():
        spread_rows(own_pos_ref, spread)
        total[...] = jnp.zeros_like(total)

    def form(at, carry):
        form_part(me, at, step * chunk + at, words_ref, pos_ref, spread, kernel_ref)
        return carry

    lax.fori_loop(0, chunk, form, 0)

    @pl.when((me >= step * chunk) & (me < (step + 1) * chunk))
    def _():
        form_diagonal(me, me - step * chunk, words_ref, pos_ref, spread, kernel_ref)

    total[...] += gather_sum(every_ref, kernel_ref)

    @pl.when(step == pl.num_programs(0) - 1)
    def _():
        adjoint = seed_ref[...] + (area_ref[...] * scale) * total[...]
        scaled_ref[...] = (reflectance_ref[...] * adjoint).astype(jnp.bfloat16)


def last_sweep(
    scale,
    kernel_ref,
    every_ref,
    seed_ref,
    area_ref,
    reflectance_ref,
    radiosity_ref,
    emission_ref,
    adjoint_ref,
    grad_ref,
    total,
):
    step = pl.program_id(0)

    @pl.when(step == 0)
    def _():
        total[...] = jnp.zeros_like(total)

    total[...] += gather_sum(every_ref, kernel_ref)

    @pl.when(step == pl.num_programs(0) - 1)
    def _():
        adjoint = seed_ref[...] + (area_ref[...] * scale) * total[...]
        adjoint_ref[...] = adjoint
        change = radiosity_ref[...].astype(jnp.float32) - emission_ref[...].astype(jnp.float32)
        grad = jnp.sum(adjoint * change, axis=0, keepdims=True) / reflectance_ref[...]
        grad_ref[...] = grad


def whole(shape):
    return pl.BlockSpec(shape, lambda step: (0,) * len(shape))


def parts(chunk, shape):
    return pl.BlockSpec((chunk,) + shape, lambda step: (step,) + (0,) * len(shape))


def on_device(adjoint_seed, radiosity, emission, reflectance, area, position, visibility):
    rhs_count, own_width = adjoint_seed.shape
    devices = lax.axis_size("row")
    my_index = lax.axis_index("row").astype(jnp.int32).reshape(1)
    local_blocks = own_width // TILE
    scale = 1.0 / math.sqrt(own_width * devices)
    chunk = math.gcd(devices, 16)
    area = area.reshape(1, own_width)
    reflectance = reflectance.reshape(1, own_width)
    smem = pl.BlockSpec(memory_space=pltpu.SMEM)
    params = pltpu.CompilerParams(
        dimension_semantics=("arbitrary",), vmem_limit_bytes=VMEM_BYTES
    )

    all_pos = lax.all_gather(position, "row")
    every = lax.all_gather((reflectance * adjoint_seed).astype(jnp.bfloat16), "row")
    kernel, scaled = pl.pallas_call(
        functools.partial(first_sweep, scale),
        grid=(devices // chunk,),
        in_specs=[
            smem,
            smem,
            whole((3, own_width)),
            parts(chunk, (3, own_width)),
            parts(chunk, (rhs_count, own_width)),
            whole((rhs_count, own_width)),
            whole((1, own_width)),
            whole((1, own_width)),
        ],
        out_specs=[parts(chunk, (own_width, own_width)), whole((rhs_count, own_width))],
        out_shape=[
            jax.ShapeDtypeStruct((devices, own_width, own_width), jnp.bfloat16),
            jax.ShapeDtypeStruct((rhs_count, own_width), jnp.bfloat16),
        ],
        scratch_shapes=[
            pltpu.VMEM((3, local_blocks, TILE, TILE), jnp.float32),
            pltpu.VMEM((rhs_count, own_width), jnp.float32),
        ],
        compiler_params=params,
        name="first_sweep",
    )(my_index, visibility, position, all_pos, every, adjoint_seed, area, reflectance)

    every = lax.all_gather(scaled, "row")
    adjoint, grad = pl.pallas_call(
        functools.partial(last_sweep, scale),
        grid=(devices // chunk,),
        in_specs=[
            parts(chunk, (own_width, own_width)),
            parts(chunk, (rhs_count, own_width)),
            whole((rhs_count, own_width)),
            whole((1, own_width)),
            whole((1, own_width)),
            whole((rhs_count, own_width)),
            whole((rhs_count, own_width)),
        ],
        out_specs=[whole((rhs_count, own_width)), whole((1, own_width))],
        out_shape=[
            jax.ShapeDtypeStruct((rhs_count, own_width), jnp.float32),
            jax.ShapeDtypeStruct((1, own_width), jnp.float32),
        ],
        scratch_shapes=[pltpu.VMEM((rhs_count, own_width), jnp.float32)],
        compiler_params=params,
        name="last_sweep",
    )(kernel, every, adjoint_seed, area, reflectance, radiosity, emission)
    return adjoint, grad.reshape(own_width)


def solution(mesh):
    placed = (
        P(None, ("scene", "row")),
        P(None, ("scene", "row")),
        P(None, ("scene", "row")),
        P(("scene", "row")),
        P(("scene", "row")),
        P(None, ("scene", "row")),
        P(("scene", "row"), None),
    )
    return jax.shard_map(
        on_device,
        mesh=mesh,
        in_specs=placed,
        out_specs=(P(None, ("scene", "row")), P(("scene", "row"))),
        check_vma=False,
    )
```

```python
import functools
import math

import jax
import jax.numpy as jnp
from jax import lax
from jax.experimental import pallas as pl
from jax.experimental.pallas import tpu as pltpu
from jax.sharding import PartitionSpec as P

TILE = 128
SWEEPS = 2
GROUP = 16
EXTRA = 16
DIRECT = 16
VMEM_BYTES = 48 * 1024 * 1024


def position_rows(pos):
    high = pos.astype(jnp.bfloat16).astype(jnp.float32)
    rest = pos - high
    middle = rest.astype(jnp.bfloat16).astype(jnp.float32)
    return high, middle, rest - middle


def spread_rows(pos_ref, spread):
    for coord in range(3):
        for block in range(spread.shape[1]):
            line = pos_ref[coord : coord + 1, block * TILE : (block + 1) * TILE]
            spread[coord, block] = jnp.transpose(jnp.broadcast_to(line, (TILE, TILE)))


def inverse_square(spread, lines, own_block, rows, other_block):
    lanes = slice(other_block * TILE, (other_block + 1) * TILE)
    total = 1.0
    for coord in range(3):
        delta = spread[coord, own_block, rows, :] - lines[coord][:, lanes]
        total = total + delta * delta
    return 1.0 / total


def form_part(me, part, at, words_ref, lines, spread, kernel_ref):
    blocks = spread.shape[1]
    lane = lax.broadcasted_iota(jnp.int32, (GROUP, TILE), 1)
    for own_block in range(blocks):
        row_block = me * blocks + own_block
        for other_block in range(blocks):
            col_block = part * blocks + other_block
            word = words_ref[own_block, col_block]
            direct = row_block < col_block
            for group in range(TILE // GROUP):
                rows = slice(group * GROUP, (group + 1) * GROUP)
                bit = jnp.where(direct, 8 * (group // 2) + lane // 16, 8 * (lane // 32) + group)
                seen = (jnp.right_shift(word, bit) & 1) != 0
                value = inverse_square(spread, lines, own_block, rows, other_block)
                value = jnp.where(seen, value, 0.0).astype(jnp.bfloat16)
                kernel_ref[
                    at,
                    own_block * TILE + group * GROUP : own_block * TILE + (group + 1) * GROUP,
                    other_block * TILE : (other_block + 1) * TILE,
                ] = value


def form_diagonal(me, at, words_ref, lines, spread, kernel_ref):
    blocks = spread.shape[1]
    lane = lax.broadcasted_iota(jnp.int32, (TILE, TILE), 1)
    row = lax.broadcasted_iota(jnp.int32, (TILE, TILE), 0)
    low, high = jnp.minimum(row, lane), jnp.maximum(row, lane)
    bit = 8 * (low // 32) + high // 16
    for block in range(blocks):
        word = words_ref[block, me * blocks + block]
        seen = (jnp.right_shift(word, bit) & 1) != 0
        value = inverse_square(spread, lines, block, slice(0, TILE), block)
        value = jnp.where(seen, value, 0.0).astype(jnp.bfloat16)
        span = slice(block * TILE, (block + 1) * TILE)
        kernel_ref[at, span, span] = value


def times_transpose(values, kernel):
    return lax.dot_general(
        values, kernel, (((1,), (1,)), ((), ())), preferred_element_type=jnp.float32
    )


def prepare(pos_ref, seed_ref, reflectance_ref, out_ref, rows):
    rhs_count = seed_ref.shape[0]
    rows[...] = jnp.zeros_like(rows)
    for term, value in enumerate(position_rows(pos_ref[...])):
        rows[3 * term : 3 * term + 3, :] = value
    scaled = (reflectance_ref[...] * seed_ref[...]).astype(jnp.bfloat16)
    extra = rows[...].astype(jnp.bfloat16)
    for copy in range(out_ref.shape[0]):
        out_ref[copy, :rhs_count] = scaled
        out_ref[copy, rhs_count:] = extra


def lines_of(extra):
    extra = extra.astype(jnp.float32)
    return [
        extra[coord : coord + 1] + extra[3 + coord : 4 + coord] + extra[6 + coord : 7 + coord]
        for coord in range(3)
    ]


def first_sweep(
    scale,
    me_ref,
    words_ref,
    own_pos_ref,
    packed_ref,
    seed_ref,
    area_ref,
    reflectance_ref,
    kernel_ref,
    scaled_ref,
    spread,
    total,
):
    step = pl.program_id(0)
    chunk = packed_ref.shape[0]
    rhs_count = seed_ref.shape[0]
    me = me_ref[0]

    @pl.when(step == 0)
    def _():
        spread_rows(own_pos_ref, spread)
        total[...] = jnp.zeros_like(total)

    def form(at, carry):
        lines = lines_of(packed_ref[at, rhs_count:])
        form_part(me, step * chunk + at, at, words_ref, lines, spread, kernel_ref)
        return carry

    lax.fori_loop(0, chunk, form, 0)

    @pl.when((me >= step * chunk) & (me < (step + 1) * chunk))
    def _():
        lines = [own_pos_ref[coord : coord + 1, :] for coord in range(3)]
        form_diagonal(me, me - step * chunk, words_ref, lines, spread, kernel_ref)

    held = total[...]
    for at in range(chunk):
        held += times_transpose(packed_ref[at, :rhs_count], kernel_ref[at])
    total[...] = held

    @pl.when(step == pl.num_programs(0) - 1)
    def _():
        adjoint = seed_ref[...] + (area_ref[...] * scale) * total[...]
        scaled_ref[...] = (reflectance_ref[...] * adjoint).astype(jnp.bfloat16)


def finish(
    scale, total, seed_ref, area_ref, reflectance_ref, radiosity_ref, emission_ref, adjoint_ref, grad_ref
):
    adjoint = seed_ref[...] + (area_ref[...] * scale) * total
    adjoint_ref[...] = adjoint
    change = radiosity_ref[...].astype(jnp.float32) - emission_ref[...].astype(jnp.float32)
    grad_ref[...] = jnp.sum(adjoint * change, axis=0, keepdims=True) / reflectance_ref[...]


def last_sweep(scale, kernel_ref, every_ref, *rest):
    step = pl.program_id(0)
    total = rest[-1]

    @pl.when(step == 0)
    def _():
        total[...] = jnp.zeros_like(total)

    held = total[...]
    for at in range(every_ref.shape[0]):
        held += times_transpose(every_ref[at], kernel_ref[at])
    total[...] = held

    @pl.when(step == pl.num_programs(0) - 1)
    def _():
        finish(scale, total[...], *rest[:-1])


def last_sweep_direct(scale, pieces, me_ref, kernel_ref, *rest):
    me = me_ref[0]
    held = times_transpose(rest[0][...], kernel_ref[me])
    for step in range(1, pieces):
        held += times_transpose(rest[step][...], kernel_ref[jnp.bitwise_xor(me, step)])
    finish(scale, held, *rest[pieces:])


def whole(shape):
    return pl.BlockSpec(shape, lambda step: (0,) * len(shape))


def parts(chunk, shape):
    return pl.BlockSpec((chunk,) + shape, lambda step: (step,) + (0,) * len(shape))


def on_device(adjoint_seed, radiosity, emission, reflectance, area, position, visibility):
    rhs_count, own_width = adjoint_seed.shape
    devices = lax.axis_size("row")
    my_index = lax.axis_index("row").astype(jnp.int32).reshape(1)
    local_blocks = own_width // TILE
    scale = 1.0 / math.sqrt(own_width * devices)
    chunk = math.gcd(devices, 16)
    direct = devices <= DIRECT and devices & (devices - 1) == 0
    area = area.reshape(1, own_width)
    reflectance = reflectance.reshape(1, own_width)
    smem = pl.BlockSpec(memory_space=pltpu.SMEM)
    vmem = pl.BlockSpec(memory_space=pltpu.VMEM)
    params = pltpu.CompilerParams(
        dimension_semantics=("arbitrary",), vmem_limit_bytes=VMEM_BYTES
    )
    packed_rows = rhs_count + EXTRA

    packed = pl.pallas_call(
        prepare,
        in_specs=[vmem] * 3,
        out_specs=vmem,
        out_shape=jax.ShapeDtypeStruct(
            (devices if direct else 1, packed_rows, own_width), jnp.bfloat16
        ),
        scratch_shapes=[pltpu.VMEM((EXTRA, own_width), jnp.float32)],
        name="prepare",
    )(position, adjoint_seed, reflectance)
    if direct:
        packed = lax.all_to_all(packed, "row", 0, 0)
    else:
        packed = lax.all_gather(packed[0], "row")
    kernel, scaled = pl.pallas_call(
        functools.partial(first_sweep, scale),
        grid=(devices // chunk,),
        in_specs=[
            smem,
            smem,
            whole((3, own_width)),
            parts(chunk, (packed_rows, own_width)),
            whole((rhs_count, own_width)),
            whole((1, own_width)),
            whole((1, own_width)),
        ],
        out_specs=[parts(chunk, (own_width, own_width)), whole((rhs_count, own_width))],
        out_shape=[
            jax.ShapeDtypeStruct((devices, own_width, own_width), jnp.bfloat16),
            jax.ShapeDtypeStruct((rhs_count, own_width), jnp.bfloat16),
        ],
        scratch_shapes=[
            pltpu.VMEM((3, local_blocks, TILE, TILE), jnp.float32),
            pltpu.VMEM((rhs_count, own_width), jnp.float32),
        ],
        compiler_params=params,
        name="first_sweep",
    )(my_index, visibility, position, packed, adjoint_seed, area, reflectance)

    out_shape = [
        jax.ShapeDtypeStruct((rhs_count, own_width), jnp.float32),
        jax.ShapeDtypeStruct((1, own_width), jnp.float32),
    ]
    own = (adjoint_seed, area, reflectance, radiosity, emission)
    if direct:
        pieces = [scaled]
        for step in range(1, devices):
            pairs = [(device, device ^ step) for device in range(devices)]
            pieces.append(lax.ppermute(scaled, "row", pairs))
        adjoint, grad = pl.pallas_call(
            functools.partial(last_sweep_direct, scale, devices),
            in_specs=[smem] + [vmem] * (devices + 6),
            out_specs=[vmem, vmem],
            out_shape=out_shape,
            compiler_params=pltpu.CompilerParams(vmem_limit_bytes=VMEM_BYTES),
            name="last_sweep",
        )(my_index, kernel, *pieces, *own)
        return adjoint, grad.reshape(own_width)

    every = lax.all_gather(scaled, "row")
    adjoint, grad = pl.pallas_call(
        functools.partial(last_sweep, scale),
        grid=(devices // chunk,),
        in_specs=[
            parts(chunk, (own_width, own_width)),
            parts(chunk, (rhs_count, own_width)),
            whole((rhs_count, own_width)),
            whole((1, own_width)),
            whole((1, own_width)),
            whole((rhs_count, own_width)),
            whole((rhs_count, own_width)),
        ],
        out_specs=[whole((rhs_count, own_width)), whole((1, own_width))],
        out_shape=out_shape,
        scratch_shapes=[pltpu.VMEM((rhs_count, own_width), jnp.float32)],
        compiler_params=params,
        name="last_sweep",
    )(kernel, every, *own)
    return adjoint, grad.reshape(own_width)


def solution(mesh):
    placed = (
        P(None, ("scene", "row")),
        P(None, ("scene", "row")),
        P(None, ("scene", "row")),
        P(("scene", "row")),
        P(("scene", "row")),
        P(None, ("scene", "row")),
        P(("scene", "row"), None),
    )
    return jax.shard_map(
        on_device,
        mesh=mesh,
        in_specs=placed,
        out_specs=(P(None, ("scene", "row")), P(("scene", "row"))),
        check_vma=False,
    )
```

```python
import functools
import math

import jax
import jax.numpy as jnp
from jax import lax
from jax.experimental import pallas as pl
from jax.experimental.pallas import tpu as pltpu
from jax.sharding import PartitionSpec as P

TILE = 128
SWEEPS = 2
GROUP = 16
EXTRA = 16
LINE = 4
VMEM_BYTES = 48 * 1024 * 1024


def position_rows(pos):
    high = pos.astype(jnp.bfloat16).astype(jnp.float32)
    rest = pos - high
    middle = rest.astype(jnp.bfloat16).astype(jnp.float32)
    return high, middle, rest - middle


def spread_rows(pos_ref, spread):
    for coord in range(3):
        for block in range(spread.shape[1]):
            line = pos_ref[coord : coord + 1, block * TILE : (block + 1) * TILE]
            spread[coord, block] = jnp.transpose(jnp.broadcast_to(line, (TILE, TILE)))


def inverse_square(spread, lines, own_block, rows, other_block):
    lanes = slice(other_block * TILE, (other_block + 1) * TILE)
    total = 1.0
    for coord in range(3):
        delta = spread[coord, own_block, rows, :] - lines[coord][:, lanes]
        total = total + delta * delta
    return 1.0 / total


def form_part(me, part, at, words_ref, lines, spread, kernel_ref):
    blocks = spread.shape[1]
    lane = lax.broadcasted_iota(jnp.int32, (GROUP, TILE), 1)
    for own_block in range(blocks):
        row_block = me * blocks + own_block
        for other_block in range(blocks):
            col_block = part * blocks + other_block
            word = words_ref[own_block, col_block]
            direct = row_block < col_block
            for group in range(TILE // GROUP):
                rows = slice(group * GROUP, (group + 1) * GROUP)
                bit = jnp.where(direct, 8 * (group // 2) + lane // 16, 8 * (lane // 32) + group)
                seen = (jnp.right_shift(word, bit) & 1) != 0
                value = inverse_square(spread, lines, own_block, rows, other_block)
                value = jnp.where(seen, value, 0.0).astype(jnp.bfloat16)
                kernel_ref[
                    at,
                    own_block * TILE + group * GROUP : own_block * TILE + (group + 1) * GROUP,
                    other_block * TILE : (other_block + 1) * TILE,
                ] = value


def form_diagonal(me, at, words_ref, lines, spread, kernel_ref):
    blocks = spread.shape[1]
    lane = lax.broadcasted_iota(jnp.int32, (TILE, TILE), 1)
    row = lax.broadcasted_iota(jnp.int32, (TILE, TILE), 0)
    low, high = jnp.minimum(row, lane), jnp.maximum(row, lane)
    bit = 8 * (low // 32) + high // 16
    for block in range(blocks):
        word = words_ref[block, me * blocks + block]
        seen = (jnp.right_shift(word, bit) & 1) != 0
        value = inverse_square(spread, lines, block, slice(0, TILE), block)
        value = jnp.where(seen, value, 0.0).astype(jnp.bfloat16)
        span = slice(block * TILE, (block + 1) * TILE)
        kernel_ref[at, span, span] = value


def times_transpose(values, kernel):
    return lax.dot_general(
        values, kernel, (((1,), (1,)), ((), ())), preferred_element_type=jnp.float32
    )


def prepare(pos_ref, seed_ref, reflectance_ref, out_ref, rows):
    rhs_count = seed_ref.shape[0]
    rows[...] = jnp.zeros_like(rows)
    for term, value in enumerate(position_rows(pos_ref[...])):
        rows[3 * term : 3 * term + 3, :] = value
    scaled = (reflectance_ref[...] * seed_ref[...]).astype(jnp.bfloat16)
    extra = rows[...].astype(jnp.bfloat16)
    out_ref[:rhs_count] = scaled
    out_ref[rhs_count:] = extra


def lines_of(extra):
    extra = extra.astype(jnp.float32)
    return [
        extra[coord : coord + 1] + extra[3 + coord : 4 + coord] + extra[6 + coord : 7 + coord]
        for coord in range(3)
    ]


def gathered_at(device):
    return device % LINE * LINE + device // LINE


def first_sweep(
    scale,
    two_level,
    me_ref,
    words_ref,
    own_pos_ref,
    packed_ref,
    seed_ref,
    area_ref,
    reflectance_ref,
    kernel_ref,
    scaled_ref,
    spread,
    total,
):
    step = pl.program_id(0)
    chunk = packed_ref.shape[0]
    rhs_count = seed_ref.shape[0]
    me = me_ref[0]

    @pl.when(step == 0)
    def _():
        spread_rows(own_pos_ref, spread)
        total[...] = jnp.zeros_like(total)

    def form(at, carry):
        lines = lines_of(packed_ref[at, rhs_count:])
        part = gathered_at(at) if two_level else step * chunk + at
        form_part(me, part, at, words_ref, lines, spread, kernel_ref)
        return carry

    lax.fori_loop(0, chunk, form, 0)

    @pl.when((me >= step * chunk) & (me < (step + 1) * chunk))
    def _():
        lines = [own_pos_ref[coord : coord + 1, :] for coord in range(3)]
        at = gathered_at(me) if two_level else me - step * chunk
        form_diagonal(me, at, words_ref, lines, spread, kernel_ref)

    held = total[...]
    for at in range(chunk):
        held += times_transpose(packed_ref[at, :rhs_count], kernel_ref[at])
    total[...] = held

    @pl.when(step == pl.num_programs(0) - 1)
    def _():
        adjoint = seed_ref[...] + (area_ref[...] * scale) * total[...]
        scaled_ref[...] = (reflectance_ref[...] * adjoint).astype(jnp.bfloat16)


def finish(
    scale, total, seed_ref, area_ref, reflectance_ref, radiosity_ref, emission_ref, adjoint_ref, grad_ref
):
    adjoint = seed_ref[...] + (area_ref[...] * scale) * total
    adjoint_ref[...] = adjoint
    change = radiosity_ref[...].astype(jnp.float32) - emission_ref[...].astype(jnp.float32)
    grad_ref[...] = jnp.sum(adjoint * change, axis=0, keepdims=True) / reflectance_ref[...]


def last_sweep(scale, kernel_ref, every_ref, *rest):
    step = pl.program_id(0)
    total = rest[-1]

    @pl.when(step == 0)
    def _():
        total[...] = jnp.zeros_like(total)

    held = total[...]
    for at in range(every_ref.shape[0]):
        held += times_transpose(every_ref[at], kernel_ref[at])
    total[...] = held

    @pl.when(step == pl.num_programs(0) - 1)
    def _():
        finish(scale, total[...], *rest[:-1])


def last_sweep_lines(scale, me_ref, kernel_ref, every_ref, *rest):
    line = me_ref[0] // LINE
    held = None
    for at in range(LINE * LINE):
        column = at // LINE % 2 * 2 + at // LINE // 2
        place = column * LINE + (line + (LINE - at % LINE)) % LINE
        term = times_transpose(every_ref[at], kernel_ref[place])
        held = term if held is None else held + term
    finish(scale, held, *rest)


def line_groups(devices, stride, count=LINE):
    span = stride * count
    return [
        [base + offset + stride * at for at in range(count)]
        for base in range(0, devices, span)
        for offset in range(stride)
    ]


def shift_in_line(device, step):
    return (device + LINE * step) % (LINE * LINE)


def whole(shape):
    return pl.BlockSpec(shape, lambda step: (0,) * len(shape))


def parts(chunk, shape):
    return pl.BlockSpec((chunk,) + shape, lambda step: (step,) + (0,) * len(shape))


def on_device(adjoint_seed, radiosity, emission, reflectance, area, position, visibility):
    rhs_count, own_width = adjoint_seed.shape
    devices = lax.axis_size("row")
    my_index = lax.axis_index("row").astype(jnp.int32).reshape(1)
    local_blocks = own_width // TILE
    scale = 1.0 / math.sqrt(own_width * devices)
    chunk = math.gcd(devices, 16)
    two_level = devices == LINE * LINE
    area = area.reshape(1, own_width)
    reflectance = reflectance.reshape(1, own_width)
    smem = pl.BlockSpec(memory_space=pltpu.SMEM)
    vmem = pl.BlockSpec(memory_space=pltpu.VMEM)
    params = pltpu.CompilerParams(
        dimension_semantics=("arbitrary",), vmem_limit_bytes=VMEM_BYTES
    )
    packed_rows = rhs_count + EXTRA

    packed = pl.pallas_call(
        prepare,
        in_specs=[vmem] * 3,
        out_specs=vmem,
        out_shape=jax.ShapeDtypeStruct(
            (packed_rows, own_width), jnp.bfloat16
        ),
        scratch_shapes=[pltpu.VMEM((EXTRA, own_width), jnp.float32)],
        name="prepare",
    )(position, adjoint_seed, reflectance)
    if two_level:
        packed = lax.all_gather(
            packed, "row", axis_index_groups=line_groups(devices, LINE)
        )
        packed = lax.all_gather(
            packed, "row", axis_index_groups=line_groups(devices, 1), tiled=True
        )
    else:
        packed = lax.all_gather(packed, "row")
    kernel, scaled = pl.pallas_call(
        functools.partial(first_sweep, scale, two_level),
        grid=(devices // chunk,),
        in_specs=[
            smem,
            smem,
            whole((3, own_width)),
            parts(chunk, (packed_rows, own_width)),
            whole((rhs_count, own_width)),
            whole((1, own_width)),
            whole((1, own_width)),
        ],
        out_specs=[parts(chunk, (own_width, own_width)), whole((rhs_count, own_width))],
        out_shape=[
            jax.ShapeDtypeStruct((devices, own_width, own_width), jnp.bfloat16),
            jax.ShapeDtypeStruct((rhs_count, own_width), jnp.bfloat16),
        ],
        scratch_shapes=[
            pltpu.VMEM((3, local_blocks, TILE, TILE), jnp.float32),
            pltpu.VMEM((rhs_count, own_width), jnp.float32),
        ],
        compiler_params=params,
        name="first_sweep",
    )(my_index, visibility, position, packed, adjoint_seed, area, reflectance)

    out_shape = [
        jax.ShapeDtypeStruct((rhs_count, own_width), jnp.float32),
        jax.ShapeDtypeStruct((1, own_width), jnp.float32),
    ]
    own = (adjoint_seed, area, reflectance, radiosity, emission)
    if two_level:
        pieces = [scaled]
        for step in range(1, LINE):
            pairs = [(device, shift_in_line(device, step)) for device in range(devices)]
            pieces.append(lax.ppermute(scaled, "row", pairs))
        every = jnp.stack(pieces)
        for stride in (2, 1):
            every = lax.all_gather(
                every, "row", axis_index_groups=line_groups(devices, stride, 2), tiled=True
            )
        adjoint, grad = pl.pallas_call(
            functools.partial(last_sweep_lines, scale),
            in_specs=[smem] + [vmem] * 7,
            out_specs=[vmem, vmem],
            out_shape=out_shape,
            compiler_params=pltpu.CompilerParams(vmem_limit_bytes=VMEM_BYTES),
            name="last_sweep",
        )(my_index, kernel, every, *own)
        return adjoint, grad.reshape(own_width)

    every = lax.all_gather(scaled, "row")
    adjoint, grad = pl.pallas_call(
        functools.partial(last_sweep, scale),
        grid=(devices // chunk,),
        in_specs=[
            parts(chunk, (own_width, own_width)),
            parts(chunk, (rhs_count, own_width)),
            whole((rhs_count, own_width)),
            whole((1, own_width)),
            whole((1, own_width)),
            whole((rhs_count, own_width)),
            whole((rhs_count, own_width)),
        ],
        out_specs=[whole((rhs_count, own_width)), whole((1, own_width))],
        out_shape=out_shape,
        scratch_shapes=[pltpu.VMEM((rhs_count, own_width), jnp.float32)],
        compiler_params=params,
        name="last_sweep",
    )(kernel, every, *own)
    return adjoint, grad.reshape(own_width)


def solution(mesh):
    placed = (
        P(None, ("scene", "row")),
        P(None, ("scene", "row")),
        P(None, ("scene", "row")),
        P(("scene", "row")),
        P(("scene", "row")),
        P(None, ("scene", "row")),
        P(("scene", "row"), None),
    )
    return jax.shard_map(
        on_device,
        mesh=mesh,
        in_specs=placed,
        out_specs=(P(None, ("scene", "row")), P(("scene", "row"))),
        check_vma=False,
    )
```

```python
import functools
import math

import jax
import jax.numpy as jnp
from jax import lax
from jax.experimental import pallas as pl
from jax.experimental.pallas import tpu as pltpu
from jax.sharding import PartitionSpec as P

TILE = 128
SWEEPS = 2
GROUP = 16
LINE = 4
EXTRA = 16
TERMS = 32
VMEM_BYTES = 48 * 1024 * 1024


def three_terms(value):
    high = value.astype(jnp.bfloat16).astype(jnp.float32)
    rest = value - high
    middle = rest.astype(jnp.bfloat16).astype(jnp.float32)
    return high, middle, rest - middle


def times_transpose(values, kernel):
    return lax.dot_general(
        values, kernel, (((1,), (1,)), ((), ())), preferred_element_type=jnp.float32
    )


def times(values, kernel):
    return jnp.dot(values, kernel, preferred_element_type=jnp.float32)


def finish(
    scale, total, seed_ref, area_ref, reflectance_ref, radiosity_ref, emission_ref, adjoint_ref, grad_ref
):
    adjoint = seed_ref[...] + (area_ref[...] * scale) * total
    adjoint_ref[...] = adjoint
    change = radiosity_ref[...].astype(jnp.float32) - emission_ref[...].astype(jnp.float32)
    grad_ref[...] = jnp.sum(adjoint * change, axis=0, keepdims=True) / reflectance_ref[...]


def prepare(
    scale, pos_ref, seed_ref, reflectance_ref, area_ref, words_ref, packed_ref, extra_ref, rows
):
    rhs_count = seed_ref.shape[0]
    rows[...] = jnp.zeros_like(rows)
    for term, value in enumerate(three_terms(pos_ref[...])):
        rows[3 * term : 3 * term + 3, :] = value
    factor = area_ref[...] * scale * reflectance_ref[...]
    for term, value in enumerate(three_terms(factor)):
        rows[9 + term : 10 + term, :] = value
    count = words_ref.shape[1]
    for place in range(4):
        part = (jnp.right_shift(words_ref[...], 8 * place) & 255).astype(jnp.float32)
        for local in range(words_ref.shape[0]):
            start = local * TILE
            rows[12 + place : 13 + place, start : start + count] = part[local : local + 1]
    extra = rows[...].astype(jnp.bfloat16)
    extra_ref[...] = extra
    packed_ref[:rhs_count] = (reflectance_ref[...] * seed_ref[...]).astype(jnp.bfloat16)
    packed_ref[rhs_count:] = extra


def distance_terms(extra, terms, as_rows):
    high, middle, low = extra[0:3], extra[3:6], extra[6:9]
    position = high + middle + low
    norm = jnp.sum(position * position, axis=0, keepdims=True)
    terms[...] = jnp.zeros_like(terms)
    if as_rows:
        for at, value in enumerate((high, high, high, middle, middle, low)):
            terms[3 * at : 3 * at + 3, :] = -2.0 * value
        ones, norms, norm = 21, 18, norm + 1.0
    else:
        terms[0:9, :] = extra[0:9]
        for at, value in enumerate((high, middle, high)):
            terms[9 + 3 * at : 12 + 3 * at, :] = value
        ones, norms = 18, 21
    terms[ones : ones + 3, :] = jnp.ones_like(high)
    for at, value in enumerate(three_terms(norm)):
        terms[norms + at : norms + at + 1, :] = value


def shift_up(direct, group, lane):
    return 31 - jnp.where(direct, 8 * (group // 2) + lane // 16, 8 * (lane // 32) + group)


def form_blocks(line, column, at, distance, words, kernel_ref):
    t, s = at // LINE, at % LINE
    lane = lax.broadcasted_iota(jnp.int32, (8, TILE), 1)
    row_chunk = line * LINE + jnp.bitwise_xor(column, t)
    direct = row_chunk < jnp.bitwise_xor(line, s) * LINE + column
    for row_block in range(2):
        for col_block in range(2):
            word = words[s, col_block * TILE + 2 * row_chunk + row_block]
            lanes = slice(col_block * TILE, (col_block + 1) * TILE)
            for group in range(TILE // GROUP):
                first = row_block * TILE + group * GROUP
                seen = jnp.left_shift(word, shift_up(direct, group, lane)) < 0
                value = 1.0 / distance[first : first + GROUP, lanes]
                halves = [jnp.where(seen, value[:8], 0.0), jnp.where(seen, value[8:], 0.0)]
                kernel_ref[at, first : first + GROUP, lanes] = jnp.concatenate(halves).astype(
                    jnp.bfloat16
                )


def form_own(me, distance, words, kernel_ref):
    lane = lax.broadcasted_iota(jnp.int32, (TILE, TILE), 1)
    row = lax.broadcasted_iota(jnp.int32, (TILE, TILE), 0)
    for row_block in range(2):
        for col_block in range(2):
            i, j = row + row_block * TILE, lane + col_block * TILE
            low, high = jnp.minimum(i, j) % TILE, jnp.maximum(i, j) % TILE
            word = words[0, col_block * TILE + 2 * me + row_block]
            seen = jnp.left_shift(word, 31 - (8 * (low // 32) + high // 16)) < 0
            rows = slice(row_block * TILE, (row_block + 1) * TILE)
            lanes = slice(col_block * TILE, (col_block + 1) * TILE)
            value = jnp.where(seen, 1.0 / distance[rows, lanes], 0.0)
            kernel_ref[0, rows, lanes] = value.astype(jnp.bfloat16)


def grid_first(
    scale,
    me_ref,
    z0_ref,
    z1_ref,
    z2_ref,
    z3_ref,
    c1_ref,
    c2_ref,
    c3_ref,
    seed_ref,
    area_ref,
    kernel_ref,
    partial_ref,
    factor_ref,
    words_vmem,
    words,
    terms,
    row_terms,
    col_terms,
    distance,
    sem,
):
    rhs_count = seed_ref.shape[0]
    me = me_ref[0]
    line, column = me // LINE, me % LINE
    lines = (z0_ref, z1_ref, z2_ref, z3_ref)
    for s in range(LINE):
        extra = lines[s][rhs_count:, :].astype(jnp.float32)
        value = extra[12:16].astype(jnp.int32)
        word = value[0:1]
        for place in range(1, 4):
            word = jnp.bitwise_or(word, jnp.left_shift(value[place : place + 1], 8 * place))
        words_vmem[s : s + 1, :] = word
        distance_terms(extra, terms, False)
        col_terms[s] = terms[...].astype(jnp.bfloat16)
    copy = pltpu.make_async_copy(words_vmem, words, sem)
    copy.start()
    for t, ref in enumerate((None, c1_ref, c2_ref, c3_ref)):
        extra = (z0_ref[rhs_count:, :] if ref is None else ref[...]).astype(jnp.float32)
        factor_ref[t] = extra[9:10] + extra[10:11] + extra[11:12]
        distance_terms(extra, terms, True)
        row_terms[t] = jnp.transpose(terms[...]).astype(jnp.bfloat16)
    copy.wait()

    def form(at, carry):
        distance[...] = times(row_terms[at // LINE], col_terms[at % LINE])
        form_blocks(line, column, at, distance, words, kernel_ref)
        return carry

    lax.fori_loop(1, LINE * LINE, form, 0)
    distance[...] = times(row_terms[0], col_terms[0])
    form_own(me, distance, words, kernel_ref)

    for t in range(LINE):
        held = seed_ref[...] / (area_ref[...] * scale) if t == 0 else None
        for s in range(LINE):
            term = times_transpose(lines[s][:rhs_count, :], kernel_ref[LINE * t + s])
            held = term if held is None else held + term
        partial_ref[t] = held.astype(jnp.bfloat16)


def grid_second(
    kernel_ref, factor_ref, p0_ref, p1_ref, p2_ref, p3_ref, q0_ref, q1_ref, q2_ref, q3_ref
):
    parts = (p0_ref, p1_ref, p2_ref, p3_ref)
    scaled = []
    for t in range(LINE):
        total = parts[0][t].astype(jnp.float32)
        for other in range(1, LINE):
            total = total + parts[other][t ^ other].astype(jnp.float32)
        scaled.append((factor_ref[t] * total).astype(jnp.bfloat16))
    for s, out_ref in enumerate((q0_ref, q1_ref, q2_ref, q3_ref)):
        held = times(scaled[0], kernel_ref[s])
        for t in range(1, LINE):
            held = held + times(scaled[t], kernel_ref[LINE * t + s])
        out_ref[...] = held.astype(out_ref.dtype)


def grid_last(scale, q0_ref, q1_ref, q2_ref, q3_ref, *rest):
    total = q0_ref[...]
    for ref in (q1_ref, q2_ref, q3_ref):
        total = total + ref[...].astype(jnp.float32)
    finish(scale, total, *rest)


def on_grid(adjoint_seed, radiosity, emission, reflectance, area, position, visibility):
    rhs_count, own_width = adjoint_seed.shape
    devices = LINE * LINE
    my_index = lax.axis_index("row").astype(jnp.int32).reshape(1)
    scale = 1.0 / math.sqrt(own_width * devices)
    area = area.reshape(1, own_width)
    reflectance = reflectance.reshape(1, own_width)
    smem = pl.BlockSpec(memory_space=pltpu.SMEM)
    vmem = pl.BlockSpec(memory_space=pltpu.VMEM)
    params = pltpu.CompilerParams(vmem_limit_bytes=VMEM_BYTES)
    shaped = jax.ShapeDtypeStruct
    field = (rhs_count, own_width)

    def send(value, step):
        return lax.ppermute(value, "row", [(at, at ^ step) for at in range(devices)])

    packed, extra = pl.pallas_call(
        functools.partial(prepare, scale),
        in_specs=[vmem] * 5,
        out_specs=[vmem] * 2,
        out_shape=[
            shaped((rhs_count + EXTRA, own_width), jnp.bfloat16),
            shaped((EXTRA, own_width), jnp.bfloat16),
        ],
        scratch_shapes=[pltpu.VMEM((EXTRA, own_width), jnp.float32)],
        name="prepare",
    )(position, adjoint_seed, reflectance, area, visibility)
    lines = [packed] + [send(packed, LINE * step) for step in range(1, LINE)]
    columns = [send(extra, step) for step in range(1, LINE)]
    kernel, partial, factor = pl.pallas_call(
        functools.partial(grid_first, scale),
        in_specs=[smem] + [vmem] * 9,
        out_specs=[vmem] * 3,
        out_shape=[
            shaped((devices, own_width, own_width), jnp.bfloat16),
            shaped((LINE,) + field, jnp.bfloat16),
            shaped((LINE, 1, own_width), jnp.float32),
        ],
        scratch_shapes=[
            pltpu.VMEM((LINE, own_width), jnp.int32),
            pltpu.SMEM((LINE, own_width), jnp.int32),
            pltpu.VMEM((TERMS, own_width), jnp.float32),
            pltpu.VMEM((LINE, own_width, TERMS), jnp.bfloat16),
            pltpu.VMEM((LINE, TERMS, own_width), jnp.bfloat16),
            pltpu.VMEM((own_width, own_width), jnp.float32),
            pltpu.SemaphoreType.DMA,
        ],
        compiler_params=params,
        name="grid_first",
    )(my_index, *lines, *columns, adjoint_seed, area)
    partials = [partial] + [send(partial, step) for step in range(1, LINE)]
    sums = pl.pallas_call(
        grid_second,
        in_specs=[vmem] * 6,
        out_specs=[vmem] * LINE,
        out_shape=[shaped(field, jnp.float32)] + [shaped(field, jnp.bfloat16)] * (LINE - 1),
        compiler_params=params,
        name="grid_second",
    )(kernel, factor, *partials)
    sums = [sums[0]] + [send(sums[step], LINE * step) for step in range(1, LINE)]
    adjoint, grad = pl.pallas_call(
        functools.partial(grid_last, scale),
        in_specs=[vmem] * 9,
        out_specs=[vmem, vmem],
        out_shape=[shaped(field, jnp.float32), shaped((1, own_width), jnp.float32)],
        name="grid_last",
    )(*sums, adjoint_seed, area, reflectance, radiosity, emission)
    return adjoint, grad.reshape(own_width)


def spread_rows(pos_ref, spread):
    for coord in range(3):
        for block in range(spread.shape[1]):
            line = pos_ref[coord : coord + 1, block * TILE : (block + 1) * TILE]
            spread[coord, block] = jnp.transpose(jnp.broadcast_to(line, (TILE, TILE)))


def inverse_square(spread, pos_ref, at, own_block, rows, other_block):
    lanes = pl.ds(other_block * TILE, TILE)
    total = 1.0
    for coord in range(3):
        delta = spread[coord, own_block, rows, :] - pos_ref[at, coord : coord + 1, lanes]
        total = total + delta * delta
    return 1.0 / total


def form_part(me, at, part, words_ref, pos_ref, spread, kernel_ref):
    blocks = spread.shape[1]
    lane = lax.broadcasted_iota(jnp.int32, (GROUP, TILE), 1)
    for own_block in range(blocks):
        row_block = me * blocks + own_block
        for other_block in range(blocks):
            col_block = part * blocks + other_block
            word = words_ref[own_block, col_block]
            direct = row_block < col_block
            for group in range(TILE // GROUP):
                rows = slice(group * GROUP, (group + 1) * GROUP)
                bit = jnp.where(direct, 8 * (group // 2) + lane // 16, 8 * (lane // 32) + group)
                seen = (jnp.right_shift(word, bit) & 1) != 0
                value = inverse_square(spread, pos_ref, at, own_block, rows, other_block)
                value = jnp.where(seen, value, 0.0).astype(jnp.bfloat16)
                kernel_ref[
                    at,
                    own_block * TILE + group * GROUP : own_block * TILE + (group + 1) * GROUP,
                    other_block * TILE : (other_block + 1) * TILE,
                ] = value


def form_diagonal(me, at, words_ref, pos_ref, spread, kernel_ref):
    blocks = spread.shape[1]
    lane = lax.broadcasted_iota(jnp.int32, (TILE, TILE), 1)
    row = lax.broadcasted_iota(jnp.int32, (TILE, TILE), 0)
    low, high = jnp.minimum(row, lane), jnp.maximum(row, lane)
    bit = 8 * (low // 32) + high // 16
    for block in range(blocks):
        word = words_ref[block, me * blocks + block]
        seen = (jnp.right_shift(word, bit) & 1) != 0
        value = inverse_square(spread, pos_ref, at, block, slice(0, TILE), block)
        value = jnp.where(seen, value, 0.0).astype(jnp.bfloat16)
        kernel_ref[
            at, block * TILE : (block + 1) * TILE, block * TILE : (block + 1) * TILE
        ] = value


def gather_sum(every_ref, kernel_ref):
    total = times_transpose(every_ref[0], kernel_ref[0])
    for at in range(1, every_ref.shape[0]):
        total += times_transpose(every_ref[at], kernel_ref[at])
    return total


def first_sweep(
    scale,
    me_ref,
    words_ref,
    own_pos_ref,
    pos_ref,
    every_ref,
    seed_ref,
    area_ref,
    reflectance_ref,
    kernel_ref,
    scaled_ref,
    spread,
    total,
):
    step = pl.program_id(0)
    chunk = pos_ref.shape[0]
    me = me_ref[0]

    @pl.when(step == 0)
    def _():
        spread_rows(own_pos_ref, spread)
        total[...] = jnp.zeros_like(total)

    def form(at, carry):
        form_part(me, at, step * chunk + at, words_ref, pos_ref, spread, kernel_ref)
        return carry

    lax.fori_loop(0, chunk, form, 0)

    @pl.when((me >= step * chunk) & (me < (step + 1) * chunk))
    def _():
        form_diagonal(me, me - step * chunk, words_ref, pos_ref, spread, kernel_ref)

    total[...] += gather_sum(every_ref, kernel_ref)

    @pl.when(step == pl.num_programs(0) - 1)
    def _():
        adjoint = seed_ref[...] + (area_ref[...] * scale) * total[...]
        scaled_ref[...] = (reflectance_ref[...] * adjoint).astype(jnp.bfloat16)


def last_sweep(
    scale,
    kernel_ref,
    every_ref,
    seed_ref,
    area_ref,
    reflectance_ref,
    radiosity_ref,
    emission_ref,
    adjoint_ref,
    grad_ref,
    total,
):
    step = pl.program_id(0)

    @pl.when(step == 0)
    def _():
        total[...] = jnp.zeros_like(total)

    total[...] += gather_sum(every_ref, kernel_ref)

    @pl.when(step == pl.num_programs(0) - 1)
    def _():
        finish(
            scale,
            total[...],
            seed_ref,
            area_ref,
            reflectance_ref,
            radiosity_ref,
            emission_ref,
            adjoint_ref,
            grad_ref,
        )


def whole(shape):
    return pl.BlockSpec(shape, lambda step: (0,) * len(shape))


def parts(chunk, shape):
    return pl.BlockSpec((chunk,) + shape, lambda step: (step,) + (0,) * len(shape))


def on_rows(adjoint_seed, radiosity, emission, reflectance, area, position, visibility):
    rhs_count, own_width = adjoint_seed.shape
    devices = lax.axis_size("row")
    my_index = lax.axis_index("row").astype(jnp.int32).reshape(1)
    local_blocks = own_width // TILE
    scale = 1.0 / math.sqrt(own_width * devices)
    chunk = math.gcd(devices, 16)
    area = area.reshape(1, own_width)
    reflectance = reflectance.reshape(1, own_width)
    smem = pl.BlockSpec(memory_space=pltpu.SMEM)
    params = pltpu.CompilerParams(
        dimension_semantics=("arbitrary",), vmem_limit_bytes=VMEM_BYTES
    )

    all_pos = lax.all_gather(position, "row")
    every = lax.all_gather((reflectance * adjoint_seed).astype(jnp.bfloat16), "row")
    kernel, scaled = pl.pallas_call(
        functools.partial(first_sweep, scale),
        grid=(devices // chunk,),
        in_specs=[
            smem,
            smem,
            whole((3, own_width)),
            parts(chunk, (3, own_width)),
            parts(chunk, (rhs_count, own_width)),
            whole((rhs_count, own_width)),
            whole((1, own_width)),
            whole((1, own_width)),
        ],
        out_specs=[parts(chunk, (own_width, own_width)), whole((rhs_count, own_width))],
        out_shape=[
            jax.ShapeDtypeStruct((devices, own_width, own_width), jnp.bfloat16),
            jax.ShapeDtypeStruct((rhs_count, own_width), jnp.bfloat16),
        ],
        scratch_shapes=[
            pltpu.VMEM((3, local_blocks, TILE, TILE), jnp.float32),
            pltpu.VMEM((rhs_count, own_width), jnp.float32),
        ],
        compiler_params=params,
        name="first_sweep",
    )(my_index, visibility, position, all_pos, every, adjoint_seed, area, reflectance)

    every = lax.all_gather(scaled, "row")
    adjoint, grad = pl.pallas_call(
        functools.partial(last_sweep, scale),
        grid=(devices // chunk,),
        in_specs=[
            parts(chunk, (own_width, own_width)),
            parts(chunk, (rhs_count, own_width)),
            whole((rhs_count, own_width)),
            whole((1, own_width)),
            whole((1, own_width)),
            whole((rhs_count, own_width)),
            whole((rhs_count, own_width)),
        ],
        out_specs=[whole((rhs_count, own_width)), whole((1, own_width))],
        out_shape=[
            jax.ShapeDtypeStruct((rhs_count, own_width), jnp.float32),
            jax.ShapeDtypeStruct((1, own_width), jnp.float32),
        ],
        scratch_shapes=[pltpu.VMEM((rhs_count, own_width), jnp.float32)],
        compiler_params=params,
        name="last_sweep",
    )(kernel, every, adjoint_seed, area, reflectance, radiosity, emission)
    return adjoint, grad.reshape(own_width)


def on_device(adjoint_seed, *rest):
    on_grid_shape = lax.axis_size("row") == LINE * LINE and adjoint_seed.shape[1] == 2 * TILE
    return (on_grid if on_grid_shape else on_rows)(adjoint_seed, *rest)


def solution(mesh):
    placed = (
        P(None, ("scene", "row")),
        P(None, ("scene", "row")),
        P(None, ("scene", "row")),
        P(("scene", "row")),
        P(("scene", "row")),
        P(None, ("scene", "row")),
        P(("scene", "row"), None),
    )
    return jax.shard_map(
        on_device,
        mesh=mesh,
        in_specs=placed,
        out_specs=(P(None, ("scene", "row")), P(("scene", "row"))),
        check_vma=False,
    )
```

```python
import functools
import math

import jax
import jax.numpy as jnp
from jax import lax
from jax.experimental import pallas as pl
from jax.experimental.pallas import tpu as pltpu
from jax.sharding import PartitionSpec as P

TILE = 128
SWEEPS = 2
GROUP = 16
LINE = 4
EXTRA = 16
TERMS = 32
VMEM_BYTES = 48 * 1024 * 1024
GRID_BYTES = 8 * 1024 * 1024


def three_terms(value):
    high = value.astype(jnp.bfloat16).astype(jnp.float32)
    rest = value - high
    middle = rest.astype(jnp.bfloat16).astype(jnp.float32)
    return high, middle, rest - middle


def times_transpose(values, kernel):
    return lax.dot_general(
        values, kernel, (((1,), (1,)), ((), ())), preferred_element_type=jnp.float32
    )


def times(values, kernel):
    return jnp.dot(values, kernel, preferred_element_type=jnp.float32)


def finish(
    scale, total, seed_ref, area_ref, reflectance_ref, radiosity_ref, emission_ref, adjoint_ref, grad_ref
):
    adjoint = seed_ref[...] + (area_ref[...] * scale) * total
    adjoint_ref[...] = adjoint
    change = radiosity_ref[...].astype(jnp.float32) - emission_ref[...].astype(jnp.float32)
    grad_ref[...] = jnp.sum(adjoint * change, axis=0, keepdims=True) / reflectance_ref[...]


def prepare(
    scale,
    pos_ref,
    seed_ref,
    reflectance_ref,
    area_ref,
    words_ref,
    packed_ref,
    boost_ref,
    rows,
):
    rhs_count = seed_ref.shape[0]
    rows[...] = jnp.zeros_like(rows)
    for term, value in enumerate(three_terms(pos_ref[...])):
        rows[3 * term : 3 * term + 3, :] = value
    weight = area_ref[...] * scale
    for term, value in enumerate(three_terms(weight * reflectance_ref[...])):
        rows[9 + term : 10 + term, :] = value
    count = words_ref.shape[1]
    for place in range(4):
        part = (jnp.right_shift(words_ref[...], 8 * place) & 255).astype(jnp.float32)
        for local in range(words_ref.shape[0]):
            start = local * TILE
            rows[12 + place : 13 + place, start : start + count] = part[local : local + 1]
    packed_ref[:rhs_count] = (reflectance_ref[...] * seed_ref[...]).astype(jnp.bfloat16)
    packed_ref[rhs_count:] = rows[...].astype(jnp.bfloat16)
    boost_ref[...] = seed_ref[...] * (1.0 / weight)


def distance_terms(position, terms, as_rows):
    high, middle, low = three_terms(position)
    norm = jnp.sum(position * position, axis=0, keepdims=True)
    terms[...] = jnp.zeros_like(terms)
    if as_rows:
        for at, value in enumerate((high, high, high, middle, middle, low)):
            terms[3 * at : 3 * at + 3, :] = -2.0 * value
        ones, norms, norm = 21, 18, norm + 1.0
    else:
        for at, value in enumerate((high, middle, low, high, middle, high)):
            terms[3 * at : 3 * at + 3, :] = value
        ones, norms = 18, 21
    terms[ones : ones + 3, :] = jnp.ones_like(high)
    for at, value in enumerate(three_terms(norm)):
        terms[norms + at : norms + at + 1, :] = value


def shift_up(direct, group, lane):
    return 31 - jnp.where(direct, 8 * (group // 2) + lane // 16, 8 * (lane // 32) + group)


def form_blocks(line, column, at, distance, words, kernel_ref):
    t, s = at // LINE, at % LINE
    lane = lax.broadcasted_iota(jnp.int32, (8, TILE), 1)
    row_chunk = line * LINE + jnp.bitwise_xor(column, t)
    direct = row_chunk < jnp.bitwise_xor(line, s) * LINE + column
    for row_block in range(2):
        for col_block in range(2):
            word = words[s, col_block * TILE + 2 * row_chunk + row_block]
            lanes = slice(col_block * TILE, (col_block + 1) * TILE)
            for group in range(TILE // GROUP):
                first = row_block * TILE + group * GROUP
                seen = jnp.left_shift(word, shift_up(direct, group, lane)) < 0
                value = 1.0 / distance[first : first + GROUP, lanes]
                halves = [jnp.where(seen, value[:8], 0.0), jnp.where(seen, value[8:], 0.0)]
                kernel_ref[at, first : first + GROUP, lanes] = jnp.concatenate(halves).astype(
                    jnp.bfloat16
                )


def form_own(me, distance, words, kernel_ref):
    lane = lax.broadcasted_iota(jnp.int32, (TILE, TILE), 1)
    row = lax.broadcasted_iota(jnp.int32, (TILE, TILE), 0)
    for row_block in range(2):
        for col_block in range(2):
            i, j = row + row_block * TILE, lane + col_block * TILE
            low, high = jnp.minimum(i, j) % TILE, jnp.maximum(i, j) % TILE
            word = words[0, col_block * TILE + 2 * me + row_block]
            seen = jnp.left_shift(word, 31 - (8 * (low // 32) + high // 16)) < 0
            rows = slice(row_block * TILE, (row_block + 1) * TILE)
            lanes = slice(col_block * TILE, (col_block + 1) * TILE)
            value = jnp.where(seen, 1.0 / distance[rows, lanes], 0.0)
            kernel_ref[0, rows, lanes] = value.astype(jnp.bfloat16)


def grid_first(
    me_ref,
    z0_ref,
    z1_ref,
    z2_ref,
    z3_ref,
    c1_ref,
    c2_ref,
    c3_ref,
    boost_ref,
    kernel_ref,
    partial_ref,
    sent_ref,
    words_vmem,
    words,
    terms,
    row_terms,
    col_terms,
    distance,
    sem,
):
    rhs_count = boost_ref.shape[0]
    me = me_ref[0]
    line, column = me // LINE, me % LINE
    lines = (z0_ref, z1_ref, z2_ref, z3_ref)
    positions = []
    for s in range(LINE):
        extra = lines[s][rhs_count:, :].astype(jnp.float32)
        value = extra[12:16].astype(jnp.int32)
        word = value[0:1]
        for place in range(1, 4):
            word = jnp.bitwise_or(word, jnp.left_shift(value[place : place + 1], 8 * place))
        words_vmem[s : s + 1, :] = word
        positions.append(extra[0:3] + extra[3:6] + extra[6:9])
    copy = pltpu.make_async_copy(words_vmem, words, sem)
    copy.start()
    for s in range(LINE):
        distance_terms(positions[s], terms, False)
        col_terms[s] = terms[...].astype(jnp.bfloat16)
    for t, ref in enumerate((None, c1_ref, c2_ref, c3_ref)):
        distance_terms(positions[0] if ref is None else ref[...], terms, True)
        row_terms[t] = jnp.transpose(terms[...]).astype(jnp.bfloat16)
    copy.wait()

    def form(at, carry):
        distance[...] = times(row_terms[at // LINE], col_terms[at % LINE])
        form_blocks(line, column, at, distance, words, kernel_ref)
        return carry

    lax.fori_loop(1, LINE * LINE, form, 0)
    distance[...] = times(row_terms[0], col_terms[0])
    form_own(me, distance, words, kernel_ref)

    for t in range(LINE):
        held = boost_ref[...] if t == 0 else None
        for s in range(LINE):
            term = times_transpose(lines[s][:rhs_count, :], kernel_ref[LINE * t + s])
            held = term if held is None else held + term
        partial_ref[t] = held
        sent_ref[t * rhs_count : (t + 1) * rhs_count] = held.astype(jnp.bfloat16)
    sent_ref[LINE * rhs_count :] = z0_ref[rhs_count:]


def grid_middle(partial_ref, core_ref, own_ref, both_ref, sent_ref, rows):
    rhs_count = partial_ref.shape[1]
    for t in range(LINE):
        start = (t ^ 1) * rhs_count
        both = partial_ref[t] + core_ref[start : start + rhs_count].astype(jnp.float32)
        both_ref[t] = both
        sent_ref[t * rhs_count : (t + 1) * rhs_count] = both.astype(jnp.bfloat16)
    rows[...] = jnp.zeros_like(rows)
    for at, ref in enumerate((own_ref, core_ref)):
        rows[3 * at : 3 * at + 3, :] = ref[-EXTRA:, :].astype(jnp.float32)[9:12]
    sent_ref[LINE * rhs_count :] = rows[...].astype(jnp.bfloat16)


def grid_second(me_ref, kernel_ref, both_ref, own_ref, x_ref, sum_ref, sent_ref):
    line = me_ref[0] // LINE
    rhs_count = sum_ref.shape[0]
    scaled = []
    for t in range(LINE):
        terms = (own_ref, x_ref)[t // 2][LINE * rhs_count :, :].astype(jnp.float32)
        at = 3 * (t % 2)
        factor = terms[at : at + 1] + terms[at + 1 : at + 2] + terms[at + 2 : at + 3]
        start = (t ^ 2) * rhs_count
        total = both_ref[t] + x_ref[start : start + rhs_count].astype(jnp.float32)
        scaled.append((factor * total).astype(jnp.bfloat16))
    for s in range(LINE):
        held = times(scaled[0], kernel_ref[s])
        for t in range(1, LINE):
            held = held + times(scaled[t], kernel_ref[LINE * t + s])
        if s == 0:
            sum_ref[...] = held
        sent_ref[jnp.bitwise_xor(line, s)] = held.astype(jnp.bfloat16)


def grid_last(scale, me_ref, sum_ref, lines_ref, *rest):
    line = me_ref[0] // LINE
    total = sum_ref[...]
    for s in range(1, LINE):
        total = total + lines_ref[jnp.bitwise_xor(line, s)].astype(jnp.float32)
    finish(scale, total, *rest)


def on_grid(adjoint_seed, radiosity, emission, reflectance, area, position, visibility):
    rhs_count, own_width = adjoint_seed.shape
    devices = LINE * LINE
    my_index = lax.axis_index("row").astype(jnp.int32).reshape(1)
    scale = 1.0 / math.sqrt(own_width * devices)
    area = area.reshape(1, own_width)
    reflectance = reflectance.reshape(1, own_width)
    smem = pl.BlockSpec(memory_space=pltpu.SMEM)
    vmem = pl.BlockSpec(memory_space=pltpu.VMEM)
    params = pltpu.CompilerParams(vmem_limit_bytes=GRID_BYTES)
    shaped = jax.ShapeDtypeStruct
    field = (rhs_count, own_width)

    def send(value, step):
        return lax.ppermute(value, "row", [(at, at ^ step) for at in range(devices)])

    columns = [send(position, step) for step in range(1, LINE)]
    packed, boost = pl.pallas_call(
        functools.partial(prepare, scale),
        in_specs=[vmem] * 5,
        out_specs=[vmem] * 2,
        out_shape=[
            shaped((rhs_count + EXTRA, own_width), jnp.bfloat16),
            shaped(field, jnp.float32),
        ],
        scratch_shapes=[pltpu.VMEM((EXTRA, own_width), jnp.float32)],
        compiler_params=params,
        name="prepare",
    )(position, adjoint_seed, reflectance, area, visibility)
    lines = [packed] + [send(packed, LINE * step) for step in range(1, LINE)]
    sent = shaped((LINE * rhs_count + EXTRA, own_width), jnp.bfloat16)
    kernel, partial, terms = pl.pallas_call(
        grid_first,
        in_specs=[smem] + [vmem] * 8,
        out_specs=[vmem] * 3,
        out_shape=[
            shaped((devices, own_width, own_width), jnp.bfloat16),
            shaped((LINE,) + field, jnp.float32),
            sent,
        ],
        scratch_shapes=[
            pltpu.VMEM((LINE, own_width), jnp.int32),
            pltpu.SMEM((LINE, own_width), jnp.int32),
            pltpu.VMEM((TERMS, own_width), jnp.float32),
            pltpu.VMEM((LINE, own_width, TERMS), jnp.bfloat16),
            pltpu.VMEM((LINE, TERMS, own_width), jnp.bfloat16),
            pltpu.VMEM((own_width, own_width), jnp.float32),
            pltpu.SemaphoreType.DMA,
        ],
        compiler_params=params,
        name="grid_first",
    )(my_index, *lines, *columns, boost)
    both, terms = pl.pallas_call(
        grid_middle,
        in_specs=[vmem] * 3,
        out_specs=[vmem] * 2,
        out_shape=[shaped((LINE,) + field, jnp.float32), sent],
        scratch_shapes=[pltpu.VMEM((EXTRA, own_width), jnp.float32)],
        compiler_params=params,
        name="grid_middle",
    )(partial, send(terms, 1), packed)
    own_sum, sums = pl.pallas_call(
        grid_second,
        in_specs=[smem] + [vmem] * 4,
        out_specs=[vmem] * 2,
        out_shape=[shaped(field, jnp.float32), shaped((LINE,) + field, jnp.bfloat16)],
        compiler_params=params,
        name="grid_second",
    )(my_index, kernel, both, terms, send(terms, 2))
    groups = [[LINE * at + column for at in range(LINE)] for column in range(LINE)]
    sums = lax.all_to_all(sums, "row", 0, 0, axis_index_groups=groups)
    adjoint, grad = pl.pallas_call(
        functools.partial(grid_last, scale),
        in_specs=[smem] + [vmem] * 7,
        out_specs=[vmem, vmem],
        out_shape=[shaped(field, jnp.float32), shaped((1, own_width), jnp.float32)],
        compiler_params=params,
        name="grid_last",
    )(my_index, own_sum, sums, adjoint_seed, area, reflectance, radiosity, emission)
    return adjoint, grad.reshape(own_width)


def spread_rows(pos_ref, spread):
    for coord in range(3):
        for block in range(spread.shape[1]):
            line = pos_ref[coord : coord + 1, block * TILE : (block + 1) * TILE]
            spread[coord, block] = jnp.transpose(jnp.broadcast_to(line, (TILE, TILE)))


def inverse_square(spread, pos_ref, at, own_block, rows, other_block):
    lanes = pl.ds(other_block * TILE, TILE)
    total = 1.0
    for coord in range(3):
        delta = spread[coord, own_block, rows, :] - pos_ref[at, coord : coord + 1, lanes]
        total = total + delta * delta
    return 1.0 / total


def form_part(me, at, part, words_ref, pos_ref, spread, kernel_ref):
    blocks = spread.shape[1]
    lane = lax.broadcasted_iota(jnp.int32, (GROUP, TILE), 1)
    for own_block in range(blocks):
        row_block = me * blocks + own_block
        for other_block in range(blocks):
            col_block = part * blocks + other_block
            word = words_ref[own_block, col_block]
            direct = row_block < col_block
            for group in range(TILE // GROUP):
                rows = slice(group * GROUP, (group + 1) * GROUP)
                bit = jnp.where(direct, 8 * (group // 2) + lane // 16, 8 * (lane // 32) + group)
                seen = (jnp.right_shift(word, bit) & 1) != 0
                value = inverse_square(spread, pos_ref, at, own_block, rows, other_block)
                value = jnp.where(seen, value, 0.0).astype(jnp.bfloat16)
                kernel_ref[
                    at,
                    own_block * TILE + group * GROUP : own_block * TILE + (group + 1) * GROUP,
                    other_block * TILE : (other_block + 1) * TILE,
                ] = value


def form_diagonal(me, at, words_ref, pos_ref, spread, kernel_ref):
    blocks = spread.shape[1]
    lane = lax.broadcasted_iota(jnp.int32, (TILE, TILE), 1)
    row = lax.broadcasted_iota(jnp.int32, (TILE, TILE), 0)
    low, high = jnp.minimum(row, lane), jnp.maximum(row, lane)
    bit = 8 * (low // 32) + high // 16
    for block in range(blocks):
        word = words_ref[block, me * blocks + block]
        seen = (jnp.right_shift(word, bit) & 1) != 0
        value = inverse_square(spread, pos_ref, at, block, slice(0, TILE), block)
        value = jnp.where(seen, value, 0.0).astype(jnp.bfloat16)
        kernel_ref[
            at, block * TILE : (block + 1) * TILE, block * TILE : (block + 1) * TILE
        ] = value


def gather_sum(every_ref, kernel_ref):
    total = times_transpose(every_ref[0], kernel_ref[0])
    for at in range(1, every_ref.shape[0]):
        total += times_transpose(every_ref[at], kernel_ref[at])
    return total


def first_sweep(
    scale,
    me_ref,
    words_ref,
    own_pos_ref,
    pos_ref,
    every_ref,
    seed_ref,
    area_ref,
    reflectance_ref,
    kernel_ref,
    scaled_ref,
    spread,
    total,
):
    step = pl.program_id(0)
    chunk = pos_ref.shape[0]
    me = me_ref[0]

    @pl.when(step == 0)
    def _():
        spread_rows(own_pos_ref, spread)
        total[...] = jnp.zeros_like(total)

    def form(at, carry):
        form_part(me, at, step * chunk + at, words_ref, pos_ref, spread, kernel_ref)
        return carry

    lax.fori_loop(0, chunk, form, 0)

    @pl.when((me >= step * chunk) & (me < (step + 1) * chunk))
    def _():
        form_diagonal(me, me - step * chunk, words_ref, pos_ref, spread, kernel_ref)

    total[...] += gather_sum(every_ref, kernel_ref)

    @pl.when(step == pl.num_programs(0) - 1)
    def _():
        adjoint = seed_ref[...] + (area_ref[...] * scale) * total[...]
        scaled_ref[...] = (reflectance_ref[...] * adjoint).astype(jnp.bfloat16)


def last_sweep(
    scale,
    kernel_ref,
    every_ref,
    seed_ref,
    area_ref,
    reflectance_ref,
    radiosity_ref,
    emission_ref,
    adjoint_ref,
    grad_ref,
    total,
):
    step = pl.program_id(0)

    @pl.when(step == 0)
    def _():
        total[...] = jnp.zeros_like(total)

    total[...] += gather_sum(every_ref, kernel_ref)

    @pl.when(step == pl.num_programs(0) - 1)
    def _():
        finish(
            scale,
            total[...],
            seed_ref,
            area_ref,
            reflectance_ref,
            radiosity_ref,
            emission_ref,
            adjoint_ref,
            grad_ref,
        )


def whole(shape):
    return pl.BlockSpec(shape, lambda step: (0,) * len(shape))


def parts(chunk, shape):
    return pl.BlockSpec((chunk,) + shape, lambda step: (step,) + (0,) * len(shape))


def on_rows(adjoint_seed, radiosity, emission, reflectance, area, position, visibility):
    rhs_count, own_width = adjoint_seed.shape
    devices = lax.axis_size("row")
    my_index = lax.axis_index("row").astype(jnp.int32).reshape(1)
    local_blocks = own_width // TILE
    scale = 1.0 / math.sqrt(own_width * devices)
    chunk = math.gcd(devices, 16)
    area = area.reshape(1, own_width)
    reflectance = reflectance.reshape(1, own_width)
    smem = pl.BlockSpec(memory_space=pltpu.SMEM)
    params = pltpu.CompilerParams(
        dimension_semantics=("arbitrary",), vmem_limit_bytes=VMEM_BYTES
    )

    all_pos = lax.all_gather(position, "row")
    every = lax.all_gather((reflectance * adjoint_seed).astype(jnp.bfloat16), "row")
    kernel, scaled = pl.pallas_call(
        functools.partial(first_sweep, scale),
        grid=(devices // chunk,),
        in_specs=[
            smem,
            smem,
            whole((3, own_width)),
            parts(chunk, (3, own_width)),
            parts(chunk, (rhs_count, own_width)),
            whole((rhs_count, own_width)),
            whole((1, own_width)),
            whole((1, own_width)),
        ],
        out_specs=[parts(chunk, (own_width, own_width)), whole((rhs_count, own_width))],
        out_shape=[
            jax.ShapeDtypeStruct((devices, own_width, own_width), jnp.bfloat16),
            jax.ShapeDtypeStruct((rhs_count, own_width), jnp.bfloat16),
        ],
        scratch_shapes=[
            pltpu.VMEM((3, local_blocks, TILE, TILE), jnp.float32),
            pltpu.VMEM((rhs_count, own_width), jnp.float32),
        ],
        compiler_params=params,
        name="first_sweep",
    )(my_index, visibility, position, all_pos, every, adjoint_seed, area, reflectance)

    every = lax.all_gather(scaled, "row")
    adjoint, grad = pl.pallas_call(
        functools.partial(last_sweep, scale),
        grid=(devices // chunk,),
        in_specs=[
            parts(chunk, (own_width, own_width)),
            parts(chunk, (rhs_count, own_width)),
            whole((rhs_count, own_width)),
            whole((1, own_width)),
            whole((1, own_width)),
            whole((rhs_count, own_width)),
            whole((rhs_count, own_width)),
        ],
        out_specs=[whole((rhs_count, own_width)), whole((1, own_width))],
        out_shape=[
            jax.ShapeDtypeStruct((rhs_count, own_width), jnp.float32),
            jax.ShapeDtypeStruct((1, own_width), jnp.float32),
        ],
        scratch_shapes=[pltpu.VMEM((rhs_count, own_width), jnp.float32)],
        compiler_params=params,
        name="last_sweep",
    )(kernel, every, adjoint_seed, area, reflectance, radiosity, emission)
    return adjoint, grad.reshape(own_width)


def on_device(adjoint_seed, *rest):
    on_grid_shape = lax.axis_size("row") == LINE * LINE and adjoint_seed.shape[1] == 2 * TILE
    return (on_grid if on_grid_shape else on_rows)(adjoint_seed, *rest)


def solution(mesh):
    placed = (
        P(None, ("scene", "row")),
        P(None, ("scene", "row")),
        P(None, ("scene", "row")),
        P(("scene", "row")),
        P(("scene", "row")),
        P(None, ("scene", "row")),
        P(("scene", "row"), None),
    )
    return jax.shard_map(
        on_device,
        mesh=mesh,
        in_specs=placed,
        out_specs=(P(None, ("scene", "row")), P(("scene", "row"))),
        check_vma=False,
    )
```

```python
import functools
import math

import jax
import jax.numpy as jnp
from jax import lax
from jax.experimental import pallas as pl
from jax.experimental.pallas import tpu as pltpu
from jax.sharding import PartitionSpec as P

TILE = 128
SWEEPS = 2
GROUP = 16
LINE = 4
EXTRA = 16
TERMS = 32
VMEM_BYTES = 48 * 1024 * 1024
GRID_BYTES = 8 * 1024 * 1024


def three_terms(value):
    high = value.astype(jnp.bfloat16).astype(jnp.float32)
    rest = value - high
    middle = rest.astype(jnp.bfloat16).astype(jnp.float32)
    return high, middle, rest - middle


def times_transpose(values, kernel):
    return lax.dot_general(
        values, kernel, (((1,), (1,)), ((), ())), preferred_element_type=jnp.float32
    )


def times(values, kernel):
    return jnp.dot(values, kernel, preferred_element_type=jnp.float32)


def finish(
    scale, total, seed_ref, area_ref, reflectance_ref, radiosity_ref, emission_ref, adjoint_ref, grad_ref
):
    adjoint = seed_ref[...] + (area_ref[...] * scale) * total
    adjoint_ref[...] = adjoint
    change = radiosity_ref[...].astype(jnp.float32) - emission_ref[...].astype(jnp.float32)
    grad_ref[...] = jnp.sum(adjoint * change, axis=0, keepdims=True) / reflectance_ref[...]


def prepare(scale, *refs):
    arguments, (packed_ref, boost_ref, rows, *held, sems) = refs[:5], refs[5:]
    copies = [
        pltpu.make_async_copy(argument, ref, sems.at[at])
        for at, (argument, ref) in enumerate(zip(arguments, held))
    ]
    for copy in copies:
        copy.start()
    rows[...] = jnp.zeros_like(rows)
    for copy in copies:
        copy.wait()
    pos_ref, words_ref, area_ref, reflectance_ref, seed_ref = held
    rhs_count = seed_ref.shape[0]
    for term, value in enumerate(three_terms(pos_ref[...])):
        rows[3 * term : 3 * term + 3, :] = value
    weight = area_ref[...] * scale
    for term, value in enumerate(three_terms(weight * reflectance_ref[...])):
        rows[9 + term : 10 + term, :] = value
    count = words_ref.shape[1]
    for place in range(4):
        part = (jnp.right_shift(words_ref[...], 8 * place) & 255).astype(jnp.float32)
        for local in range(words_ref.shape[0]):
            start = local * TILE
            rows[12 + place : 13 + place, start : start + count] = part[local : local + 1]
    packed_ref[:rhs_count] = (reflectance_ref[...] * seed_ref[...]).astype(jnp.bfloat16)
    packed_ref[rhs_count:] = rows[...].astype(jnp.bfloat16)
    boost_ref[...] = seed_ref[...] * (1.0 / weight)


def distance_terms(position, terms, as_rows):
    high, middle, low = three_terms(position)
    norm = jnp.sum(position * position, axis=0, keepdims=True)
    terms[...] = jnp.zeros_like(terms)
    if as_rows:
        for at, value in enumerate((high, high, high, middle, middle, low)):
            terms[3 * at : 3 * at + 3, :] = -2.0 * value
        ones, norms, norm = 21, 18, norm + 1.0
    else:
        for at, value in enumerate((high, middle, low, high, middle, high)):
            terms[3 * at : 3 * at + 3, :] = value
        ones, norms = 18, 21
    terms[ones : ones + 3, :] = jnp.ones_like(high)
    for at, value in enumerate(three_terms(norm)):
        terms[norms + at : norms + at + 1, :] = value


def shift_up(direct, group, lane):
    return 31 - jnp.where(direct, 8 * (group // 2) + lane // 16, 8 * (lane // 32) + group)


def kernel_values(distance, word, shift):
    value = pl.reciprocal(distance, approx=True)
    seen = jnp.left_shift(word, shift) < 0
    halves = [jnp.where(seen, value[:8], 0.0), jnp.where(seen, value[8:], 0.0)]
    return jnp.concatenate(halves).astype(jnp.bfloat16)


def form_block(t, s, line, column, distance, words, out_ref):
    lane = lax.broadcasted_iota(jnp.int32, (8, TILE), 1)
    row_chunk = line * LINE + jnp.bitwise_xor(column, t)
    direct = row_chunk < jnp.bitwise_xor(line, s) * LINE + column
    for group in range(TILE // GROUP):
        shift = shift_up(direct, group, lane)
        for row_block in range(2):
            first = row_block * TILE + group * GROUP
            for col_block in range(2):
                word = words[s, col_block * TILE + 2 * row_chunk + row_block]
                lanes = slice(col_block * TILE, (col_block + 1) * TILE)
                out_ref[first : first + GROUP, lanes] = kernel_values(
                    distance[first : first + GROUP, lanes], word, shift
                )


def form_own(me, distance, words, out_ref):
    lane = lax.broadcasted_iota(jnp.int32, (8, TILE), 1)
    row = lax.broadcasted_iota(jnp.int32, (8, TILE), 0)
    for row_block in range(2):
        for col_block in range(2):
            word = words[0, col_block * TILE + 2 * me + row_block]
            lanes = slice(col_block * TILE, (col_block + 1) * TILE)
            for group in range(TILE // GROUP):
                first = row_block * TILE + group * GROUP
                halves = []
                for half in range(first, first + GROUP, 8):
                    i, j = row + half, lane + col_block * TILE
                    low, high = jnp.minimum(i, j) % TILE, jnp.maximum(i, j) % TILE
                    seen = jnp.left_shift(word, 31 - (8 * (low // 32) + high // 16)) < 0
                    value = pl.reciprocal(distance[half : half + 8, lanes], approx=True)
                    halves.append(jnp.where(seen, value, 0.0))
                out_ref[first : first + GROUP, lanes] = jnp.concatenate(halves).astype(
                    jnp.bfloat16
                )


def read_extra(ref, rhs_count):
    extra = ref[rhs_count:, :].astype(jnp.float32)
    value = extra[12:16].astype(jnp.int32)
    word = value[0:1]
    for place in range(1, 4):
        word = jnp.bitwise_or(word, jnp.left_shift(value[place : place + 1], 8 * place))
    return extra[0:3] + extra[3:6] + extra[6:9], word


def grid_near(
    me_ref,
    own_ref,
    core_ref,
    pair_ref,
    boost_ref,
    kernel_ref,
    partial_ref,
    row_terms,
    words_vmem,
    words,
    terms,
    distance,
    sem,
):
    rhs_count = boost_ref.shape[0]
    me = me_ref[0]
    line, column = me // LINE, me % LINE
    position, words_vmem[0:1, :] = read_extra(own_ref, rhs_count)
    copy = pltpu.make_async_copy(words_vmem, words, sem)
    copy.start()
    distance_terms(position, terms, False)
    col_terms = terms[...].astype(jnp.bfloat16)
    for t, value in enumerate((position, core_ref[...], pair_ref[0], pair_ref[1])):
        distance_terms(value, terms, True)
        row_terms[t] = jnp.transpose(terms[...]).astype(jnp.bfloat16)
    copy.wait()
    own = own_ref[:rhs_count, :]
    for t in range(LINE):
        distance[...] = times(row_terms[t], col_terms)
        if t == 0:
            form_own(me, distance, words, kernel_ref.at[t])
        else:
            form_block(t, 0, line, column, distance, words, kernel_ref.at[t])
        held = times_transpose(own, kernel_ref[t])
        partial_ref[t] = held + boost_ref[...] if t == 0 else held


def grid_far(
    me_ref,
    z1_ref,
    z2_ref,
    z3_ref,
    own_ref,
    near_ref,
    row_terms,
    kernel_ref,
    partial_ref,
    sent_ref,
    words_vmem,
    words,
    terms,
    col_terms,
    distance,
    sem,
):
    rhs_count = near_ref.shape[1]
    me = me_ref[0]
    line, column = me // LINE, me % LINE
    lines = (z1_ref, z2_ref, z3_ref)
    positions = []
    for s, ref in enumerate(lines, 1):
        position, words_vmem[s : s + 1, :] = read_extra(ref, rhs_count)
        positions.append(position)
    copy = pltpu.make_async_copy(words_vmem, words, sem)
    copy.start()
    for s, position in enumerate(positions):
        distance_terms(position, terms, False)
        col_terms[s] = terms[...].astype(jnp.bfloat16)
    copy.wait()

    def form(t, carry):
        held = near_ref[t]
        for s in range(1, LINE):
            at = (LINE - 1) * t + s - 1
            slot = distance.at[s - 1]
            slot[...] = times(row_terms[t], col_terms[s - 1])
            form_block(t, s, line, column, slot, words, kernel_ref.at[at])
            held += times_transpose(lines[s - 1][:rhs_count, :], kernel_ref[at])
        partial_ref[t] = held
        start = pl.multiple_of(t * rhs_count, rhs_count)
        sent_ref[pl.ds(start, rhs_count), :] = held.astype(jnp.bfloat16)
        return carry

    lax.fori_loop(0, LINE, form, 0)
    sent_ref[LINE * rhs_count :] = own_ref[rhs_count:]


def grid_middle(partial_ref, core_ref, own_ref, both_ref, sent_ref, rows):
    rhs_count = partial_ref.shape[1]
    for t in range(LINE):
        start = (t ^ 1) * rhs_count
        both = partial_ref[t] + core_ref[start : start + rhs_count].astype(jnp.float32)
        both_ref[t] = both
        sent_ref[t * rhs_count : (t + 1) * rhs_count] = both.astype(jnp.bfloat16)
    rows[...] = jnp.zeros_like(rows)
    for at, ref in enumerate((own_ref, core_ref)):
        rows[3 * at : 3 * at + 3, :] = ref[-EXTRA:, :].astype(jnp.float32)[9:12]
    sent_ref[LINE * rhs_count :] = rows[...].astype(jnp.bfloat16)


def grid_second(
    near_ref, far_ref, both_ref, own_ref, x_ref, q0_ref, q1_ref, q2_ref, q3_ref
):
    rhs_count = q0_ref.shape[0]
    scaled = []
    for t in range(LINE):
        terms = (own_ref, x_ref)[t // 2][LINE * rhs_count :, :].astype(jnp.float32)
        at = 3 * (t % 2)
        factor = terms[at : at + 1] + terms[at + 1 : at + 2] + terms[at + 2 : at + 3]
        start = (t ^ 2) * rhs_count
        total = both_ref[t] + x_ref[start : start + rhs_count].astype(jnp.float32)
        scaled.append((factor * total).astype(jnp.bfloat16))
    for s, out_ref in enumerate((q0_ref, q1_ref, q2_ref, q3_ref)):
        held = None
        for t in range(LINE):
            kernel = near_ref[t] if s == 0 else far_ref[(LINE - 1) * t + s - 1]
            term = times(scaled[t], kernel)
            held = term if held is None else held + term
        out_ref[...] = held.astype(out_ref.dtype)


def grid_last(scale, q0_ref, q1_ref, q2_ref, q3_ref, *rest):
    total = q0_ref[...]
    for ref in (q1_ref, q2_ref, q3_ref):
        total = total + ref[...].astype(jnp.float32)
    finish(scale, total, *rest)


def on_grid(adjoint_seed, radiosity, emission, reflectance, area, position, visibility):
    rhs_count, own_width = adjoint_seed.shape
    devices = LINE * LINE
    my_index = lax.axis_index("row").astype(jnp.int32).reshape(1)
    scale = 1.0 / math.sqrt(own_width * devices)
    area = area.reshape(1, own_width)
    reflectance = reflectance.reshape(1, own_width)
    smem = pl.BlockSpec(memory_space=pltpu.SMEM)
    vmem = pl.BlockSpec(memory_space=pltpu.VMEM)
    params = pltpu.CompilerParams(vmem_limit_bytes=GRID_BYTES)
    shaped = jax.ShapeDtypeStruct
    field = (rhs_count, own_width)

    def send(value, step):
        return lax.ppermute(value, "row", [(at, at ^ step) for at in range(devices)])

    core = send(position, 1)
    arguments = (position, visibility, area, reflectance, adjoint_seed)
    packed, boost = pl.pallas_call(
        functools.partial(prepare, scale),
        in_specs=[pl.BlockSpec(memory_space=pltpu.HBM)] * 5,
        out_specs=[vmem] * 2,
        out_shape=[
            shaped((rhs_count + EXTRA, own_width), jnp.bfloat16),
            shaped(field, jnp.float32),
        ],
        scratch_shapes=[pltpu.VMEM((EXTRA, own_width), jnp.float32)]
        + [pltpu.VMEM(value.shape, value.dtype) for value in arguments]
        + [pltpu.SemaphoreType.DMA((5,))],
        compiler_params=params,
        name="prepare",
    )(*[pltpu.with_memory_space_constraint(value, pltpu.HBM) for value in arguments])
    pair = send(jnp.stack([position, core]), 2)
    lines = [send(packed, LINE * step) for step in range(1, LINE)]
    words_scratch = [
        pltpu.VMEM((LINE, own_width), jnp.int32),
        pltpu.SMEM((LINE, own_width), jnp.int32),
        pltpu.VMEM((TERMS, own_width), jnp.float32),
    ]
    near, partial, row_terms = pl.pallas_call(
        grid_near,
        in_specs=[smem] + [vmem] * 4,
        out_specs=[vmem] * 3,
        out_shape=[
            shaped((LINE, own_width, own_width), jnp.bfloat16),
            shaped((LINE,) + field, jnp.float32),
            shaped((LINE, own_width, TERMS), jnp.bfloat16),
        ],
        scratch_shapes=words_scratch
        + [pltpu.VMEM((own_width, own_width), jnp.float32), pltpu.SemaphoreType.DMA],
        compiler_params=params,
        name="grid_near",
    )(my_index, packed, core, pair, boost)
    sent = shaped((LINE * rhs_count + EXTRA, own_width), jnp.bfloat16)
    far, partial, terms = pl.pallas_call(
        grid_far,
        in_specs=[smem] + [vmem] * 6,
        out_specs=[vmem] * 3,
        out_shape=[
            shaped((devices - LINE, own_width, own_width), jnp.bfloat16),
            shaped((LINE,) + field, jnp.float32),
            sent,
        ],
        scratch_shapes=words_scratch
        + [
            pltpu.VMEM((LINE - 1, TERMS, own_width), jnp.bfloat16),
            pltpu.VMEM((LINE - 1, own_width, own_width), jnp.float32),
            pltpu.SemaphoreType.DMA,
        ],
        compiler_params=params,
        name="grid_far",
    )(my_index, *lines, packed, partial, row_terms)
    both, terms = pl.pallas_call(
        grid_middle,
        in_specs=[vmem] * 3,
        out_specs=[vmem] * 2,
        out_shape=[shaped((LINE,) + field, jnp.float32), sent],
        scratch_shapes=[pltpu.VMEM((EXTRA, own_width), jnp.float32)],
        compiler_params=params,
        name="grid_middle",
    )(partial, send(terms, 1), packed)
    sums = pl.pallas_call(
        grid_second,
        in_specs=[vmem] * 5,
        out_specs=[vmem] * LINE,
        out_shape=[shaped(field, jnp.float32)] + [shaped(field, jnp.bfloat16)] * (LINE - 1),
        compiler_params=params,
        name="grid_second",
    )(near, far, both, terms, send(terms, 2))
    sums = [sums[0]] + [send(sums[step], LINE * step) for step in range(1, LINE)]
    adjoint, grad = pl.pallas_call(
        functools.partial(grid_last, scale),
        in_specs=[vmem] * 9,
        out_specs=[vmem, vmem],
        out_shape=[shaped(field, jnp.float32), shaped((1, own_width), jnp.float32)],
        compiler_params=params,
        name="grid_last",
    )(*sums, adjoint_seed, area, reflectance, radiosity, emission)
    return adjoint, grad.reshape(own_width)


def spread_rows(pos_ref, spread):
    for coord in range(3):
        for block in range(spread.shape[1]):
            line = pos_ref[coord : coord + 1, block * TILE : (block + 1) * TILE]
            spread[coord, block] = jnp.transpose(jnp.broadcast_to(line, (TILE, TILE)))


def inverse_square(spread, pos_ref, at, own_block, rows, other_block):
    lanes = pl.ds(other_block * TILE, TILE)
    total = 1.0
    for coord in range(3):
        delta = spread[coord, own_block, rows, :] - pos_ref[at, coord : coord + 1, lanes]
        total = total + delta * delta
    return 1.0 / total


def form_part(me, at, part, words_ref, pos_ref, spread, kernel_ref):
    blocks = spread.shape[1]
    lane = lax.broadcasted_iota(jnp.int32, (GROUP, TILE), 1)
    for own_block in range(blocks):
        row_block = me * blocks + own_block
        for other_block in range(blocks):
            col_block = part * blocks + other_block
            word = words_ref[own_block, col_block]
            direct = row_block < col_block
            for group in range(TILE // GROUP):
                rows = slice(group * GROUP, (group + 1) * GROUP)
                bit = jnp.where(direct, 8 * (group // 2) + lane // 16, 8 * (lane // 32) + group)
                seen = (jnp.right_shift(word, bit) & 1) != 0
                value = inverse_square(spread, pos_ref, at, own_block, rows, other_block)
                value = jnp.where(seen, value, 0.0).astype(jnp.bfloat16)
                kernel_ref[
                    at,
                    own_block * TILE + group * GROUP : own_block * TILE + (group + 1) * GROUP,
                    other_block * TILE : (other_block + 1) * TILE,
                ] = value


def form_diagonal(me, at, words_ref, pos_ref, spread, kernel_ref):
    blocks = spread.shape[1]
    lane = lax.broadcasted_iota(jnp.int32, (TILE, TILE), 1)
    row = lax.broadcasted_iota(jnp.int32, (TILE, TILE), 0)
    low, high = jnp.minimum(row, lane), jnp.maximum(row, lane)
    bit = 8 * (low // 32) + high // 16
    for block in range(blocks):
        word = words_ref[block, me * blocks + block]
        seen = (jnp.right_shift(word, bit) & 1) != 0
        value = inverse_square(spread, pos_ref, at, block, slice(0, TILE), block)
        value = jnp.where(seen, value, 0.0).astype(jnp.bfloat16)
        kernel_ref[
            at, block * TILE : (block + 1) * TILE, block * TILE : (block + 1) * TILE
        ] = value


def gather_sum(every_ref, kernel_ref):
    total = times_transpose(every_ref[0], kernel_ref[0])
    for at in range(1, every_ref.shape[0]):
        total += times_transpose(every_ref[at], kernel_ref[at])
    return total


def first_sweep(
    scale,
    me_ref,
    words_ref,
    own_pos_ref,
    pos_ref,
    every_ref,
    seed_ref,
    area_ref,
    reflectance_ref,
    kernel_ref,
    scaled_ref,
    spread,
    total,
):
    step = pl.program_id(0)
    chunk = pos_ref.shape[0]
    me = me_ref[0]

    @pl.when(step == 0)
    def _():
        spread_rows(own_pos_ref, spread)
        total[...] = jnp.zeros_like(total)

    def form(at, carry):
        form_part(me, at, step * chunk + at, words_ref, pos_ref, spread, kernel_ref)
        return carry

    lax.fori_loop(0, chunk, form, 0)

    @pl.when((me >= step * chunk) & (me < (step + 1) * chunk))
    def _():
        form_diagonal(me, me - step * chunk, words_ref, pos_ref, spread, kernel_ref)

    total[...] += gather_sum(every_ref, kernel_ref)

    @pl.when(step == pl.num_programs(0) - 1)
    def _():
        adjoint = seed_ref[...] + (area_ref[...] * scale) * total[...]
        scaled_ref[...] = (reflectance_ref[...] * adjoint).astype(jnp.bfloat16)


def last_sweep(
    scale,
    kernel_ref,
    every_ref,
    seed_ref,
    area_ref,
    reflectance_ref,
    radiosity_ref,
    emission_ref,
    adjoint_ref,
    grad_ref,
    total,
):
    step = pl.program_id(0)

    @pl.when(step == 0)
    def _():
        total[...] = jnp.zeros_like(total)

    total[...] += gather_sum(every_ref, kernel_ref)

    @pl.when(step == pl.num_programs(0) - 1)
    def _():
        finish(
            scale,
            total[...],
            seed_ref,
            area_ref,
            reflectance_ref,
            radiosity_ref,
            emission_ref,
            adjoint_ref,
            grad_ref,
        )


def whole(shape):
    return pl.BlockSpec(shape, lambda step: (0,) * len(shape))


def parts(chunk, shape):
    return pl.BlockSpec((chunk,) + shape, lambda step: (step,) + (0,) * len(shape))


def on_rows(adjoint_seed, radiosity, emission, reflectance, area, position, visibility):
    rhs_count, own_width = adjoint_seed.shape
    devices = lax.axis_size("row")
    my_index = lax.axis_index("row").astype(jnp.int32).reshape(1)
    local_blocks = own_width // TILE
    scale = 1.0 / math.sqrt(own_width * devices)
    chunk = math.gcd(devices, 16)
    area = area.reshape(1, own_width)
    reflectance = reflectance.reshape(1, own_width)
    smem = pl.BlockSpec(memory_space=pltpu.SMEM)
    params = pltpu.CompilerParams(
        dimension_semantics=("arbitrary",), vmem_limit_bytes=VMEM_BYTES
    )

    all_pos = lax.all_gather(position, "row")
    every = lax.all_gather((reflectance * adjoint_seed).astype(jnp.bfloat16), "row")
    kernel, scaled = pl.pallas_call(
        functools.partial(first_sweep, scale),
        grid=(devices // chunk,),
        in_specs=[
            smem,
            smem,
            whole((3, own_width)),
            parts(chunk, (3, own_width)),
            parts(chunk, (rhs_count, own_width)),
            whole((rhs_count, own_width)),
            whole((1, own_width)),
            whole((1, own_width)),
        ],
        out_specs=[parts(chunk, (own_width, own_width)), whole((rhs_count, own_width))],
        out_shape=[
            jax.ShapeDtypeStruct((devices, own_width, own_width), jnp.bfloat16),
            jax.ShapeDtypeStruct((rhs_count, own_width), jnp.bfloat16),
        ],
        scratch_shapes=[
            pltpu.VMEM((3, local_blocks, TILE, TILE), jnp.float32),
            pltpu.VMEM((rhs_count, own_width), jnp.float32),
        ],
        compiler_params=params,
        name="first_sweep",
    )(my_index, visibility, position, all_pos, every, adjoint_seed, area, reflectance)

    every = lax.all_gather(scaled, "row")
    adjoint, grad = pl.pallas_call(
        functools.partial(last_sweep, scale),
        grid=(devices // chunk,),
        in_specs=[
            parts(chunk, (own_width, own_width)),
            parts(chunk, (rhs_count, own_width)),
            whole((rhs_count, own_width)),
            whole((1, own_width)),
            whole((1, own_width)),
            whole((rhs_count, own_width)),
            whole((rhs_count, own_width)),
        ],
        out_specs=[whole((rhs_count, own_width)), whole((1, own_width))],
        out_shape=[
            jax.ShapeDtypeStruct((rhs_count, own_width), jnp.float32),
            jax.ShapeDtypeStruct((1, own_width), jnp.float32),
        ],
        scratch_shapes=[pltpu.VMEM((rhs_count, own_width), jnp.float32)],
        compiler_params=params,
        name="last_sweep",
    )(kernel, every, adjoint_seed, area, reflectance, radiosity, emission)
    return adjoint, grad.reshape(own_width)


def on_device(adjoint_seed, *rest):
    on_grid_shape = lax.axis_size("row") == LINE * LINE and adjoint_seed.shape[1] == 2 * TILE
    return (on_grid if on_grid_shape else on_rows)(adjoint_seed, *rest)


def solution(mesh):
    placed = (
        P(None, ("scene", "row")),
        P(None, ("scene", "row")),
        P(None, ("scene", "row")),
        P(("scene", "row")),
        P(("scene", "row")),
        P(None, ("scene", "row")),
        P(("scene", "row"), None),
    )
    return jax.shard_map(
        on_device,
        mesh=mesh,
        in_specs=placed,
        out_specs=(P(None, ("scene", "row")), P(("scene", "row"))),
        check_vma=False,
    )
```

```python
import functools
import math

import jax
import jax.numpy as jnp
from jax import lax
from jax.experimental import pallas as pl
from jax.experimental.pallas import tpu as pltpu
from jax.sharding import PartitionSpec as P

TILE = 128
SWEEPS = 2
GROUP = 16
LINE = 4
EXTRA = 16
TERMS = 32
VMEM_BYTES = 48 * 1024 * 1024
GRID_BYTES = 8 * 1024 * 1024


def three_terms(value):
    high = value.astype(jnp.bfloat16).astype(jnp.float32)
    rest = value - high
    middle = rest.astype(jnp.bfloat16).astype(jnp.float32)
    return high, middle, rest - middle


def times_transpose(values, kernel):
    return lax.dot_general(
        values, kernel, (((1,), (1,)), ((), ())), preferred_element_type=jnp.float32
    )


def times(values, kernel):
    return jnp.dot(values, kernel, preferred_element_type=jnp.float32)


def finish(
    scale, total, seed_ref, area_ref, reflectance_ref, radiosity_ref, emission_ref, adjoint_ref, grad_ref
):
    adjoint = seed_ref[...] + (area_ref[...] * scale) * total
    adjoint_ref[...] = adjoint
    change = radiosity_ref[...].astype(jnp.float32) - emission_ref[...].astype(jnp.float32)
    grad_ref[...] = jnp.sum(adjoint * change, axis=0, keepdims=True) / reflectance_ref[...]


def prepare(scale, *refs):
    arguments, (packed_ref, boost_ref, spot_ref, rows, *held, sems) = refs[:5], refs[5:]
    copies = [
        pltpu.make_async_copy(argument, ref, sems.at[at])
        for at, (argument, ref) in enumerate(zip(arguments, held))
    ]
    for copy in copies:
        copy.start()
    rows[...] = jnp.zeros_like(rows)
    for copy in copies:
        copy.wait()
    pos_ref, words_ref, area_ref, reflectance_ref, seed_ref = held
    rhs_count = seed_ref.shape[0]
    for term, value in enumerate(three_terms(pos_ref[...])):
        rows[3 * term : 3 * term + 3, :] = value
    weight = area_ref[...] * scale
    for term, value in enumerate(three_terms(weight * reflectance_ref[...])):
        rows[9 + term : 10 + term, :] = value
    count = words_ref.shape[1]
    for place in range(4):
        part = (jnp.right_shift(words_ref[...], 8 * place) & 255).astype(jnp.float32)
        for local in range(words_ref.shape[0]):
            start = local * TILE
            rows[12 + place : 13 + place, start : start + count] = part[local : local + 1]
    packed_ref[:rhs_count] = (reflectance_ref[...] * seed_ref[...]).astype(jnp.bfloat16)
    packed_ref[rhs_count:] = rows[...].astype(jnp.bfloat16)
    boost_ref[...] = seed_ref[...] * (1.0 / weight)
    spot_ref[...] = pos_ref[...]


def distance_terms(position, terms, as_rows):
    high, middle, low = three_terms(position)
    norm = jnp.sum(position * position, axis=0, keepdims=True)
    terms[...] = jnp.zeros_like(terms)
    if as_rows:
        for at, value in enumerate((high, high, high, middle, middle, low)):
            terms[3 * at : 3 * at + 3, :] = -2.0 * value
        ones, norms, norm = 21, 18, norm + 1.0
    else:
        for at, value in enumerate((high, middle, low, high, middle, high)):
            terms[3 * at : 3 * at + 3, :] = value
        ones, norms = 18, 21
    terms[ones : ones + 3, :] = jnp.ones_like(high)
    for at, value in enumerate(three_terms(norm)):
        terms[norms + at : norms + at + 1, :] = value


def shift_up(direct, group, lane):
    return 31 - jnp.where(direct, 8 * (group // 2) + lane // 16, 8 * (lane // 32) + group)


def form_block(t, s, line, column, distance, words, out_ref):
    lane = lax.broadcasted_iota(jnp.int32, (8, TILE), 1)
    row_chunk = line * LINE + jnp.bitwise_xor(column, t)
    direct = row_chunk < jnp.bitwise_xor(line, s) * LINE + column
    shifts = [shift_up(direct, group, lane) for group in range(TILE // GROUP)]
    for row_block in range(2):
        for col_block in range(2):
            word = jnp.full(lane.shape, words[s, col_block * TILE + 2 * row_chunk + row_block])
            lanes = slice(col_block * TILE, (col_block + 1) * TILE)
            for group, shift in enumerate(shifts):
                first = row_block * TILE + group * GROUP
                seen = jnp.left_shift(word, shift) < 0
                halves = []
                for half in range(first, first + GROUP, 8):
                    value = pl.reciprocal(distance[half : half + 8, lanes], approx=True)
                    halves.append(jnp.where(seen, value, 0.0))
                out_ref[first : first + GROUP, lanes] = jnp.concatenate(halves).astype(
                    jnp.bfloat16
                )


def form_own(me, distance, words, out_ref):
    lane = lax.broadcasted_iota(jnp.int32, (8, TILE), 1)
    row = lax.broadcasted_iota(jnp.int32, (8, TILE), 0)
    for row_block in range(2):
        for col_block in range(2):
            word = words[0, col_block * TILE + 2 * me + row_block]
            lanes = slice(col_block * TILE, (col_block + 1) * TILE)
            for group in range(TILE // GROUP):
                first = row_block * TILE + group * GROUP
                halves = []
                for half in range(first, first + GROUP, 8):
                    i, j = row + half, lane + col_block * TILE
                    low, high = jnp.minimum(i, j) % TILE, jnp.maximum(i, j) % TILE
                    seen = jnp.left_shift(word, 31 - (8 * (low // 32) + high // 16)) < 0
                    value = pl.reciprocal(distance[half : half + 8, lanes], approx=True)
                    halves.append(jnp.where(seen, value, 0.0))
                out_ref[first : first + GROUP, lanes] = jnp.concatenate(halves).astype(
                    jnp.bfloat16
                )


def read_extra(ref, rhs_count):
    extra = ref[rhs_count:, :].astype(jnp.float32)
    value = extra[12:16].astype(jnp.int32)
    word = value[0:1]
    for place in range(1, 4):
        word = jnp.bitwise_or(word, jnp.left_shift(value[place : place + 1], 8 * place))
    return extra[0:3] + extra[3:6] + extra[6:9], word


def grid_near(
    me_ref,
    own_ref,
    core_ref,
    pair_ref,
    boost_ref,
    kernel_ref,
    partial_ref,
    row_terms,
    words_vmem,
    words,
    terms,
    distance,
    sem,
):
    rhs_count = boost_ref.shape[0]
    me = me_ref[0]
    line, column = me // LINE, me % LINE
    position, words_vmem[0:1, :] = read_extra(own_ref, rhs_count)
    copy = pltpu.make_async_copy(words_vmem, words, sem)
    copy.start()
    distance_terms(position, terms, False)
    col_terms = terms[...].astype(jnp.bfloat16)
    for t, value in enumerate((position, core_ref[...], pair_ref[0], pair_ref[1])):
        distance_terms(value, terms, True)
        row_terms[t] = jnp.transpose(terms[...]).astype(jnp.bfloat16)
    copy.wait()
    own = own_ref[:rhs_count, :]

    def measure(t):
        distance[t % 2] = times(row_terms[t], col_terms)

    def add(t):
        held = times_transpose(own, kernel_ref[t])
        partial_ref[t] = held + boost_ref[...] if t == 0 else held

    measure(0)
    for t in range(LINE):
        if t + 1 < LINE:
            measure(t + 1)
        if t == 0:
            form_own(me, distance.at[0], words, kernel_ref.at[0])
        else:
            form_block(t, 0, line, column, distance.at[t % 2], words, kernel_ref.at[t])
            add(t - 1)
    add(LINE - 1)


def grid_lines(steps, last, me_ref, *refs):
    count = len(steps)
    lines, (own_ref, before_ref, row_terms, kernel_ref, partial_ref, *refs) = (
        refs[:count],
        refs[count:],
    )
    sent_ref, refs = (refs[0], refs[1:]) if last else (None, refs)
    words_vmem, words, terms, col_terms, distance, sem = refs
    rhs_count = before_ref.shape[1]
    me = me_ref[0]
    line, column = me // LINE, me % LINE
    positions = []
    for s, ref in zip(steps, lines):
        position, words_vmem[s : s + 1, :] = read_extra(ref, rhs_count)
        positions.append(position)
    copy = pltpu.make_async_copy(words_vmem, words, sem)
    copy.start()
    for at, position in enumerate(positions):
        distance_terms(position, terms, False)
        col_terms[at] = terms[...].astype(jnp.bfloat16)
    copy.wait()
    blocks = [(t, at) for t in range(LINE) for at in range(count)]
    held = {}

    def measure(place):
        t, at = blocks[place]
        distance[place % 2] = times(row_terms[t], col_terms[at])

    def add(place):
        t, at = blocks[place]
        held[t] = held.get(t, before_ref[t]) + times_transpose(
            lines[at][:rhs_count, :], kernel_ref[place]
        )
        if at == count - 1:
            partial_ref[t] = held[t]
            if last:
                sent_ref[t * rhs_count : (t + 1) * rhs_count] = held[t].astype(jnp.bfloat16)

    measure(0)
    for place, (t, at) in enumerate(blocks):
        if place + 1 < len(blocks):
            measure(place + 1)
        form_block(t, steps[at], line, column, distance.at[place % 2], words, kernel_ref.at[place])
        if place:
            add(place - 1)
    add(len(blocks) - 1)
    if last:
        sent_ref[LINE * rhs_count :] = own_ref[rhs_count:]


def grid_middle(partial_ref, core_ref, own_ref, both_ref, sent_ref, rows):
    rhs_count = partial_ref.shape[1]
    for t in range(LINE):
        start = (t ^ 1) * rhs_count
        both = partial_ref[t] + core_ref[start : start + rhs_count].astype(jnp.float32)
        both_ref[t] = both
        sent_ref[t * rhs_count : (t + 1) * rhs_count] = both.astype(jnp.bfloat16)
    rows[...] = jnp.zeros_like(rows)
    for at, ref in enumerate((own_ref, core_ref)):
        rows[3 * at : 3 * at + 3, :] = ref[-EXTRA:, :].astype(jnp.float32)[9:12]
    sent_ref[LINE * rhs_count :] = rows[...].astype(jnp.bfloat16)


def grid_second(far_ref, both_ref, own_ref, x_ref, scaled_ref, q2_ref, q3_ref):
    rhs_count = q2_ref.shape[0]
    for t in range(LINE):
        terms = (own_ref, x_ref)[t // 2][LINE * rhs_count :, :].astype(jnp.float32)
        at = 3 * (t % 2)
        factor = terms[at : at + 1] + terms[at + 1 : at + 2] + terms[at + 2 : at + 3]
        start = (t ^ 2) * rhs_count
        total = both_ref[t] + x_ref[start : start + rhs_count].astype(jnp.float32)
        scaled_ref[t] = (factor * total).astype(jnp.bfloat16)
    for at, out_ref in enumerate((q2_ref, q3_ref)):
        held = times(scaled_ref[0], far_ref[at])
        for t in range(1, LINE):
            held = held + times(scaled_ref[t], far_ref[2 * t + at])
        out_ref[...] = held.astype(jnp.bfloat16)


def grid_third(near_ref, next_ref, scaled_ref, q0_ref, q1_ref):
    for kernel_ref, out_ref in ((next_ref, q1_ref), (near_ref, q0_ref)):
        held = times(scaled_ref[0], kernel_ref[0])
        for t in range(1, LINE):
            held = held + times(scaled_ref[t], kernel_ref[t])
        out_ref[...] = held.astype(out_ref.dtype)


def grid_last(scale, q3_ref, q2_ref, q1_ref, q0_ref, *rest):
    total = q0_ref[...]
    for ref in (q1_ref, q2_ref, q3_ref):
        total = total + ref[...].astype(jnp.float32)
    finish(scale, total, *rest)


def on_grid(adjoint_seed, radiosity, emission, reflectance, area, position, visibility):
    rhs_count, own_width = adjoint_seed.shape
    devices = LINE * LINE
    my_index = lax.axis_index("row").astype(jnp.int32).reshape(1)
    scale = 1.0 / math.sqrt(own_width * devices)
    area = area.reshape(1, own_width)
    reflectance = reflectance.reshape(1, own_width)
    smem = pl.BlockSpec(memory_space=pltpu.SMEM)
    vmem = pl.BlockSpec(memory_space=pltpu.VMEM)
    params = pltpu.CompilerParams(vmem_limit_bytes=GRID_BYTES)
    shaped = jax.ShapeDtypeStruct
    field = (rhs_count, own_width)

    def send(value, step):
        return lax.ppermute(value, "row", [(at, at ^ step) for at in range(devices)])

    arguments = (position, visibility, area, reflectance, adjoint_seed)
    packed, boost, spot = pl.pallas_call(
        functools.partial(prepare, scale),
        in_specs=[pl.BlockSpec(memory_space=pltpu.HBM)] * 5,
        out_specs=[vmem] * 3,
        out_shape=[
            shaped((rhs_count + EXTRA, own_width), jnp.bfloat16),
            shaped(field, jnp.float32),
            shaped(position.shape, jnp.float32),
        ],
        scratch_shapes=[pltpu.VMEM((EXTRA, own_width), jnp.float32)]
        + [pltpu.VMEM(value.shape, value.dtype) for value in arguments]
        + [pltpu.SemaphoreType.DMA((5,))],
        compiler_params=params,
        name="prepare",
    )(*[pltpu.with_memory_space_constraint(value, pltpu.HBM) for value in arguments])
    line3, line2 = send(packed, 3 * LINE), send(packed, 2 * LINE)
    core = send(position, 1)
    later, core = lax.optimization_barrier((packed, core))
    line1 = send(later, LINE)
    pair = send(jnp.stack([spot, core]), 2)
    words_scratch = [
        pltpu.VMEM((LINE, own_width), jnp.int32),
        pltpu.SMEM((LINE, own_width), jnp.int32),
        pltpu.VMEM((TERMS, own_width), jnp.float32),
    ]
    distance = pltpu.VMEM((2, own_width, own_width), jnp.float32)
    near, partial, row_terms = pl.pallas_call(
        grid_near,
        in_specs=[smem] + [vmem] * 4,
        out_specs=[vmem] * 3,
        out_shape=[
            shaped((LINE, own_width, own_width), jnp.bfloat16),
            shaped((LINE,) + field, jnp.float32),
            shaped((LINE, own_width, TERMS), jnp.bfloat16),
        ],
        scratch_shapes=words_scratch + [distance, pltpu.SemaphoreType.DMA],
        compiler_params=params,
        name="grid_near",
    )(my_index, packed, core, pair, boost)
    sent = shaped((LINE * rhs_count + EXTRA, own_width), jnp.bfloat16)

    def form_lines(steps, last, name, *operands):
        count = len(steps)
        return pl.pallas_call(
            functools.partial(grid_lines, steps, last),
            in_specs=[smem] + [vmem] * (count + 3),
            out_specs=[vmem] * (3 if last else 2),
            out_shape=[
                shaped((LINE * count, own_width, own_width), jnp.bfloat16),
                shaped((LINE,) + field, jnp.float32),
            ]
            + [sent] * last,
            scratch_shapes=words_scratch
            + [
                pltpu.VMEM((count, TERMS, own_width), jnp.bfloat16),
                distance,
                pltpu.SemaphoreType.DMA,
            ],
            compiler_params=params,
            name=name,
        )(my_index, *operands, row_terms)

    next_, partial = form_lines((1,), False, "grid_next", line1, packed, partial)
    far, partial, terms = form_lines((2, 3), True, "grid_far", line2, line3, packed, partial)
    both, terms = pl.pallas_call(
        grid_middle,
        in_specs=[vmem] * 3,
        out_specs=[vmem] * 2,
        out_shape=[shaped((LINE,) + field, jnp.float32), sent],
        scratch_shapes=[pltpu.VMEM((EXTRA, own_width), jnp.float32)],
        compiler_params=params,
        name="grid_middle",
    )(partial, send(terms, 1), packed)
    scaled, sum2, sum3 = pl.pallas_call(
        grid_second,
        in_specs=[vmem] * 4,
        out_specs=[vmem] * 3,
        out_shape=[shaped((LINE,) + field, jnp.bfloat16)] + [shaped(field, jnp.bfloat16)] * 2,
        compiler_params=params,
        name="grid_second",
    )(far, both, terms, send(terms, 2))
    sum3, sum2 = send(sum3, 3 * LINE), send(sum2, 2 * LINE)
    sum0, sum1 = pl.pallas_call(
        grid_third,
        in_specs=[vmem] * 3,
        out_specs=[vmem] * 2,
        out_shape=[shaped(field, jnp.float32), shaped(field, jnp.bfloat16)],
        compiler_params=params,
        cost_estimate=pl.CostEstimate(
            flops=4 * LINE * rhs_count * own_width**2,
            bytes_accessed=4 * LINE * own_width**2 + 12 * rhs_count * own_width,
            transcendentals=0,
        ),
        name="grid_third",
    )(near, next_, scaled)
    sum1 = send(sum1, LINE)
    adjoint, grad = pl.pallas_call(
        functools.partial(grid_last, scale),
        in_specs=[vmem] * 9,
        out_specs=[vmem, vmem],
        out_shape=[shaped(field, jnp.float32), shaped((1, own_width), jnp.float32)],
        compiler_params=params,
        name="grid_last",
    )(sum3, sum2, sum1, sum0, adjoint_seed, area, reflectance, radiosity, emission)
    return adjoint, grad.reshape(own_width)


def spread_rows(pos_ref, spread):
    for coord in range(3):
        for block in range(spread.shape[1]):
            line = pos_ref[coord : coord + 1, block * TILE : (block + 1) * TILE]
            spread[coord, block] = jnp.transpose(jnp.broadcast_to(line, (TILE, TILE)))


def inverse_square(spread, pos_ref, at, own_block, rows, other_block):
    lanes = pl.ds(other_block * TILE, TILE)
    total = 1.0
    for coord in range(3):
        delta = spread[coord, own_block, rows, :] - pos_ref[at, coord : coord + 1, lanes]
        total = total + delta * delta
    return 1.0 / total


def form_part(me, at, part, words_ref, pos_ref, spread, kernel_ref):
    blocks = spread.shape[1]
    lane = lax.broadcasted_iota(jnp.int32, (GROUP, TILE), 1)
    for own_block in range(blocks):
        row_block = me * blocks + own_block
        for other_block in range(blocks):
            col_block = part * blocks + other_block
            word = words_ref[own_block, col_block]
            direct = row_block < col_block
            for group in range(TILE // GROUP):
                rows = slice(group * GROUP, (group + 1) * GROUP)
                bit = jnp.where(direct, 8 * (group // 2) + lane // 16, 8 * (lane // 32) + group)
                seen = (jnp.right_shift(word, bit) & 1) != 0
                value = inverse_square(spread, pos_ref, at, own_block, rows, other_block)
                value = jnp.where(seen, value, 0.0).astype(jnp.bfloat16)
                kernel_ref[
                    at,
                    own_block * TILE + group * GROUP : own_block * TILE + (group + 1) * GROUP,
                    other_block * TILE : (other_block + 1) * TILE,
                ] = value


def form_diagonal(me, at, words_ref, pos_ref, spread, kernel_ref):
    blocks = spread.shape[1]
    lane = lax.broadcasted_iota(jnp.int32, (TILE, TILE), 1)
    row = lax.broadcasted_iota(jnp.int32, (TILE, TILE), 0)
    low, high = jnp.minimum(row, lane), jnp.maximum(row, lane)
    bit = 8 * (low // 32) + high // 16
    for block in range(blocks):
        word = words_ref[block, me * blocks + block]
        seen = (jnp.right_shift(word, bit) & 1) != 0
        value = inverse_square(spread, pos_ref, at, block, slice(0, TILE), block)
        value = jnp.where(seen, value, 0.0).astype(jnp.bfloat16)
        kernel_ref[
            at, block * TILE : (block + 1) * TILE, block * TILE : (block + 1) * TILE
        ] = value


def gather_sum(every_ref, kernel_ref):
    total = times_transpose(every_ref[0], kernel_ref[0])
    for at in range(1, every_ref.shape[0]):
        total += times_transpose(every_ref[at], kernel_ref[at])
    return total


def first_sweep(
    scale,
    me_ref,
    words_ref,
    own_pos_ref,
    pos_ref,
    every_ref,
    seed_ref,
    area_ref,
    reflectance_ref,
    kernel_ref,
    scaled_ref,
    spread,
    total,
):
    step = pl.program_id(0)
    chunk = pos_ref.shape[0]
    me = me_ref[0]

    @pl.when(step == 0)
    def _():
        spread_rows(own_pos_ref, spread)
        total[...] = jnp.zeros_like(total)

    def form(at, carry):
        form_part(me, at, step * chunk + at, words_ref, pos_ref, spread, kernel_ref)
        return carry

    lax.fori_loop(0, chunk, form, 0)

    @pl.when((me >= step * chunk) & (me < (step + 1) * chunk))
    def _():
        form_diagonal(me, me - step * chunk, words_ref, pos_ref, spread, kernel_ref)

    total[...] += gather_sum(every_ref, kernel_ref)

    @pl.when(step == pl.num_programs(0) - 1)
    def _():
        adjoint = seed_ref[...] + (area_ref[...] * scale) * total[...]
        scaled_ref[...] = (reflectance_ref[...] * adjoint).astype(jnp.bfloat16)


def last_sweep(
    scale,
    kernel_ref,
    every_ref,
    seed_ref,
    area_ref,
    reflectance_ref,
    radiosity_ref,
    emission_ref,
    adjoint_ref,
    grad_ref,
    total,
):
    step = pl.program_id(0)

    @pl.when(step == 0)
    def _():
        total[...] = jnp.zeros_like(total)

    total[...] += gather_sum(every_ref, kernel_ref)

    @pl.when(step == pl.num_programs(0) - 1)
    def _():
        finish(
            scale,
            total[...],
            seed_ref,
            area_ref,
            reflectance_ref,
            radiosity_ref,
            emission_ref,
            adjoint_ref,
            grad_ref,
        )


def whole(shape):
    return pl.BlockSpec(shape, lambda step: (0,) * len(shape))


def parts(chunk, shape):
    return pl.BlockSpec((chunk,) + shape, lambda step: (step,) + (0,) * len(shape))


def on_rows(adjoint_seed, radiosity, emission, reflectance, area, position, visibility):
    rhs_count, own_width = adjoint_seed.shape
    devices = lax.axis_size("row")
    my_index = lax.axis_index("row").astype(jnp.int32).reshape(1)
    local_blocks = own_width // TILE
    scale = 1.0 / math.sqrt(own_width * devices)
    chunk = math.gcd(devices, 16)
    area = area.reshape(1, own_width)
    reflectance = reflectance.reshape(1, own_width)
    smem = pl.BlockSpec(memory_space=pltpu.SMEM)
    params = pltpu.CompilerParams(
        dimension_semantics=("arbitrary",), vmem_limit_bytes=VMEM_BYTES
    )

    all_pos = lax.all_gather(position, "row")
    every = lax.all_gather((reflectance * adjoint_seed).astype(jnp.bfloat16), "row")
    kernel, scaled = pl.pallas_call(
        functools.partial(first_sweep, scale),
        grid=(devices // chunk,),
        in_specs=[
            smem,
            smem,
            whole((3, own_width)),
            parts(chunk, (3, own_width)),
            parts(chunk, (rhs_count, own_width)),
            whole((rhs_count, own_width)),
            whole((1, own_width)),
            whole((1, own_width)),
        ],
        out_specs=[parts(chunk, (own_width, own_width)), whole((rhs_count, own_width))],
        out_shape=[
            jax.ShapeDtypeStruct((devices, own_width, own_width), jnp.bfloat16),
            jax.ShapeDtypeStruct((rhs_count, own_width), jnp.bfloat16),
        ],
        scratch_shapes=[
            pltpu.VMEM((3, local_blocks, TILE, TILE), jnp.float32),
            pltpu.VMEM((rhs_count, own_width), jnp.float32),
        ],
        compiler_params=params,
        name="first_sweep",
    )(my_index, visibility, position, all_pos, every, adjoint_seed, area, reflectance)

    every = lax.all_gather(scaled, "row")
    adjoint, grad = pl.pallas_call(
        functools.partial(last_sweep, scale),
        grid=(devices // chunk,),
        in_specs=[
            parts(chunk, (own_width, own_width)),
            parts(chunk, (rhs_count, own_width)),
            whole((rhs_count, own_width)),
            whole((1, own_width)),
            whole((1, own_width)),
            whole((rhs_count, own_width)),
            whole((rhs_count, own_width)),
        ],
        out_specs=[whole((rhs_count, own_width)), whole((1, own_width))],
        out_shape=[
            jax.ShapeDtypeStruct((rhs_count, own_width), jnp.float32),
            jax.ShapeDtypeStruct((1, own_width), jnp.float32),
        ],
        scratch_shapes=[pltpu.VMEM((rhs_count, own_width), jnp.float32)],
        compiler_params=params,
        name="last_sweep",
    )(kernel, every, adjoint_seed, area, reflectance, radiosity, emission)
    return adjoint, grad.reshape(own_width)


def on_device(adjoint_seed, *rest):
    on_grid_shape = lax.axis_size("row") == LINE * LINE and adjoint_seed.shape[1] == 2 * TILE
    return (on_grid if on_grid_shape else on_rows)(adjoint_seed, *rest)


def solution(mesh):
    placed = (
        P(None, ("scene", "row")),
        P(None, ("scene", "row")),
        P(None, ("scene", "row")),
        P(("scene", "row")),
        P(("scene", "row")),
        P(None, ("scene", "row")),
        P(("scene", "row"), None),
    )
    return jax.shard_map(
        on_device,
        mesh=mesh,
        in_specs=placed,
        out_specs=(P(None, ("scene", "row")), P(("scene", "row"))),
        check_vma=False,
    )
```

```python
import functools
import math

import jax
import jax.numpy as jnp
from jax import lax
from jax.experimental import pallas as pl
from jax.experimental.pallas import tpu as pltpu
from jax.sharding import PartitionSpec as P

TILE = 128
SWEEPS = 2
GROUP = 16
LINE = 4
EXTRA = 16
TERMS = 32
VMEM_BYTES = 48 * 1024 * 1024
GRID_BYTES = 8 * 1024 * 1024


NEAR = [(0, 0), (1, 0)]
REST = [(t, s) for t in range(LINE) for s in range(LINE) if (t, s) not in NEAR]


def three_terms(value):
    high = value.astype(jnp.bfloat16).astype(jnp.float32)
    rest = value - high
    middle = rest.astype(jnp.bfloat16).astype(jnp.float32)
    return high, middle, rest - middle


def times_transpose(values, kernel):
    return lax.dot_general(
        values, kernel, (((1,), (1,)), ((), ())), preferred_element_type=jnp.float32
    )


def times(values, kernel):
    return jnp.dot(values, kernel, preferred_element_type=jnp.float32)


def finish(
    scale, total, seed_ref, area_ref, reflectance_ref, radiosity_ref, emission_ref, adjoint_ref, grad_ref
):
    adjoint = seed_ref[...] + (area_ref[...] * scale) * total
    adjoint_ref[...] = adjoint
    change = radiosity_ref[...].astype(jnp.float32) - emission_ref[...].astype(jnp.float32)
    grad_ref[...] = jnp.sum(adjoint * change, axis=0, keepdims=True) / reflectance_ref[...]


def prepare(scale, *refs):
    arguments, (packed_ref, boost_ref, spot_ref, rows, *held, sems) = refs[:5], refs[5:]
    copies = [
        pltpu.make_async_copy(argument, ref, sems.at[at])
        for at, (argument, ref) in enumerate(zip(arguments, held))
    ]
    for copy in copies:
        copy.start()
    rows[...] = jnp.zeros_like(rows)
    for copy in copies:
        copy.wait()
    pos_ref, words_ref, area_ref, reflectance_ref, seed_ref = held
    rhs_count = seed_ref.shape[0]
    for term, value in enumerate(three_terms(pos_ref[...])):
        rows[3 * term : 3 * term + 3, :] = value
    weight = area_ref[...] * scale
    for term, value in enumerate(three_terms(weight * reflectance_ref[...])):
        rows[9 + term : 10 + term, :] = value
    count = words_ref.shape[1]
    for place in range(4):
        part = (jnp.right_shift(words_ref[...], 8 * place) & 255).astype(jnp.float32)
        for local in range(words_ref.shape[0]):
            start = local * TILE
            rows[12 + place : 13 + place, start : start + count] = part[local : local + 1]
    packed_ref[:rhs_count] = (reflectance_ref[...] * seed_ref[...]).astype(jnp.bfloat16)
    packed_ref[rhs_count:] = rows[...].astype(jnp.bfloat16)
    boost_ref[...] = seed_ref[...] * (1.0 / weight)
    spot_ref[...] = pos_ref[...]


def distance_terms(position, terms, as_rows):
    high, middle, low = three_terms(position)
    norm = jnp.sum(position * position, axis=0, keepdims=True)
    terms[...] = jnp.zeros_like(terms)
    if as_rows:
        for at, value in enumerate((high, high, high, middle, middle, low)):
            terms[3 * at : 3 * at + 3, :] = -2.0 * value
        ones, norms, norm = 21, 18, norm + 1.0
    else:
        for at, value in enumerate((high, middle, low, high, middle, high)):
            terms[3 * at : 3 * at + 3, :] = value
        ones, norms = 18, 21
    terms[ones : ones + 3, :] = jnp.ones_like(high)
    for at, value in enumerate(three_terms(norm)):
        terms[norms + at : norms + at + 1, :] = value


def shift_up(direct, group, lane):
    return 31 - jnp.where(direct, 8 * (group // 2) + lane // 16, 8 * (lane // 32) + group)


def block_words(word, t, line, column):
    start = 2 * (line * LINE + jnp.bitwise_xor(column, t))
    splats = []
    for col_block in range(2):
        lanes = jnp.broadcast_to(word[:, col_block * TILE : (col_block + 1) * TILE], (8, TILE))
        lanes = pltpu.roll(lanes, TILE - start, 1)
        splats.append(
            [jnp.broadcast_to(lanes[:, at : at + 1], (8, TILE)) for at in range(2)]
        )
    return splats


def form_block(t, s, line, column, distance, word, out_ref):
    lane = lax.broadcasted_iota(jnp.int32, (8, TILE), 1)
    row_chunk = line * LINE + jnp.bitwise_xor(column, t)
    direct = row_chunk < jnp.bitwise_xor(line, s) * LINE + column
    shifts = [shift_up(direct, group, lane) for group in range(TILE // GROUP)]
    splats = block_words(word, t, line, column)
    for row_block in range(2):
        for col_block in range(2):
            lanes = slice(col_block * TILE, (col_block + 1) * TILE)
            for group, shift in enumerate(shifts):
                first = row_block * TILE + group * GROUP
                seen = jnp.left_shift(splats[col_block][row_block], shift) < 0
                halves = []
                for half in range(first, first + GROUP, 8):
                    value = pl.reciprocal(distance[half : half + 8, lanes], approx=True)
                    halves.append(jnp.where(seen, value, 0.0))
                out_ref[first : first + GROUP, lanes] = jnp.concatenate(halves).astype(
                    jnp.bfloat16
                )


def form_own(line, column, distance, word, out_ref):
    lane = lax.broadcasted_iota(jnp.int32, (8, TILE), 1)
    row = lax.broadcasted_iota(jnp.int32, (8, TILE), 0)
    splats = block_words(word, 0, line, column)
    for row_block in range(2):
        for col_block in range(2):
            lanes = slice(col_block * TILE, (col_block + 1) * TILE)
            for group in range(TILE // GROUP):
                first = row_block * TILE + group * GROUP
                halves = []
                for half in range(first, first + GROUP, 8):
                    i, j = row + half, lane + col_block * TILE
                    low, high = jnp.minimum(i, j) % TILE, jnp.maximum(i, j) % TILE
                    shift = 31 - (8 * (low // 32) + high // 16)
                    seen = jnp.left_shift(splats[col_block][row_block], shift) < 0
                    value = pl.reciprocal(distance[half : half + 8, lanes], approx=True)
                    halves.append(jnp.where(seen, value, 0.0))
                out_ref[first : first + GROUP, lanes] = jnp.concatenate(halves).astype(
                    jnp.bfloat16
                )


def read_extra(ref, rhs_count):
    extra = ref[rhs_count:, :].astype(jnp.float32)
    value = extra[12:16].astype(jnp.int32)
    word = value[0:1]
    for place in range(1, 4):
        word = jnp.bitwise_or(word, jnp.left_shift(value[place : place + 1], 8 * place))
    return extra[0:3] + extra[3:6] + extra[6:9], word


def form_all(blocks, line, column, row_terms, col_terms, words, fields, start, refs, finish_row):
    kernel_ref, distance = refs
    held = {}

    def measure(place):
        t, s = blocks[place]
        distance[place % 2] = times(row_terms(t), col_terms(s))

    def add(place):
        t, s = blocks[place]
        term = times_transpose(fields[s], kernel_ref[place])
        held[t] = (held[t] if t in held else start(t)) + term
        if place + 1 == len(blocks) or blocks[place + 1][0] != t:
            finish_row(t, held[t])

    measure(0)
    for place, (t, s) in enumerate(blocks):
        if place + 1 < len(blocks):
            measure(place + 1)
        slot, out_ref = distance.at[place % 2], kernel_ref.at[place]
        if t == 0 and s == 0:
            form_own(line, column, slot, words[s], out_ref)
        else:
            form_block(t, s, line, column, slot, words[s], out_ref)
        if place:
            add(place - 1)
    add(len(blocks) - 1)


def grid_near(
    me_ref,
    own_ref,
    core_ref,
    boost_ref,
    kernel_ref,
    partial_ref,
    row_terms,
    col_terms,
    terms,
    distance,
):
    rhs_count = boost_ref.shape[0]
    line, column = me_ref[0] // LINE, me_ref[0] % LINE
    position, word = read_extra(own_ref, rhs_count)
    distance_terms(position, terms.at[0], False)
    col_terms[...] = terms[0].astype(jnp.bfloat16)
    for t, value in enumerate((position, core_ref[...])):
        distance_terms(value, terms.at[1 + t], True)
        row_terms[t] = jnp.transpose(terms[1 + t]).astype(jnp.bfloat16)

    def finish_row(t, value):
        partial_ref[t] = value

    form_all(
        NEAR,
        line,
        column,
        lambda t: row_terms[t],
        lambda s: col_terms[...],
        [word],
        [own_ref[:rhs_count, :]],
        lambda t: boost_ref[...] if t == 0 else 0.0,
        (kernel_ref, distance),
        finish_row,
    )


def grid_rest(
    me_ref,
    own_ref,
    z1_ref,
    z2_ref,
    z3_ref,
    pair_ref,
    before_ref,
    row_ref,
    col_ref,
    kernel_ref,
    partial_ref,
    sent_ref,
    terms,
    row_terms,
    col_terms,
    distance,
):
    rhs_count = before_ref.shape[1]
    line, column = me_ref[0] // LINE, me_ref[0] % LINE
    lines = (own_ref, z1_ref, z2_ref, z3_ref)
    words = []
    for s, ref in enumerate(lines):
        position, word = read_extra(ref, rhs_count)
        words.append(word)
        if s:
            distance_terms(position, terms.at[s], False)
            col_terms[s] = terms[s].astype(jnp.bfloat16)
    for t in range(2):
        slot = terms.at[LINE * t]
        distance_terms(pair_ref[t], slot, True)
        row_terms[t] = jnp.transpose(slot[...]).astype(jnp.bfloat16)

    def finish_row(t, value):
        partial_ref[t] = value
        sent_ref[t * rhs_count : (t + 1) * rhs_count] = value.astype(jnp.bfloat16)

    form_all(
        REST,
        line,
        column,
        lambda t: row_ref[t] if t < 2 else row_terms[t - 2],
        lambda s: col_terms[s] if s else col_ref[...],
        words,
        [ref[:rhs_count, :] for ref in lines],
        lambda t: before_ref[t] if t < 2 else 0.0,
        (kernel_ref, distance),
        finish_row,
    )
    sent_ref[LINE * rhs_count :] = own_ref[rhs_count:]


def grid_middle(partial_ref, core_ref, own_ref, both_ref, sent_ref, rows):
    rhs_count = partial_ref.shape[1]
    for t in range(LINE):
        start = (t ^ 1) * rhs_count
        both = partial_ref[t] + core_ref[start : start + rhs_count].astype(jnp.float32)
        both_ref[t] = both
        sent_ref[t * rhs_count : (t + 1) * rhs_count] = both.astype(jnp.bfloat16)
    rows[...] = jnp.zeros_like(rows)
    for at, ref in enumerate((own_ref, core_ref)):
        rows[3 * at : 3 * at + 3, :] = ref[-EXTRA:, :].astype(jnp.float32)[9:12]
    sent_ref[LINE * rhs_count :] = rows[...].astype(jnp.bfloat16)


def product(scaled_ref, near_ref, rest_ref, s):
    held = None
    for t in range(LINE):
        near = (t, s) in NEAR
        kernel = near_ref[NEAR.index((t, s))] if near else rest_ref[REST.index((t, s))]
        term = times(scaled_ref[t], kernel)
        held = term if held is None else held + term
    return held


def grid_second(rest_ref, both_ref, own_ref, x_ref, scaled_ref, q2_ref, q3_ref):
    rhs_count = q2_ref.shape[0]
    for t in range(LINE):
        terms = (own_ref, x_ref)[t // 2][LINE * rhs_count :, :].astype(jnp.float32)
        at = 3 * (t % 2)
        factor = terms[at : at + 1] + terms[at + 1 : at + 2] + terms[at + 2 : at + 3]
        start = (t ^ 2) * rhs_count
        total = both_ref[t] + x_ref[start : start + rhs_count].astype(jnp.float32)
        scaled_ref[t] = (factor * total).astype(jnp.bfloat16)
    q3_ref[...] = product(scaled_ref, None, rest_ref, 3).astype(jnp.bfloat16)
    q2_ref[...] = product(scaled_ref, None, rest_ref, 2).astype(jnp.bfloat16)


def grid_third(near_ref, rest_ref, scaled_ref, q0_ref, q1_ref):
    q1_ref[...] = product(scaled_ref, None, rest_ref, 1).astype(jnp.bfloat16)
    q0_ref[...] = product(scaled_ref, near_ref, rest_ref, 0)


def grid_last(scale, q3_ref, q2_ref, q1_ref, q0_ref, *rest):
    total = q0_ref[...]
    for ref in (q1_ref, q2_ref, q3_ref):
        total = total + ref[...].astype(jnp.float32)
    finish(scale, total, *rest)


def on_grid(adjoint_seed, radiosity, emission, reflectance, area, position, visibility):
    rhs_count, own_width = adjoint_seed.shape
    devices = LINE * LINE
    my_index = lax.axis_index("row").astype(jnp.int32).reshape(1)
    scale = 1.0 / math.sqrt(own_width * devices)
    area = area.reshape(1, own_width)
    reflectance = reflectance.reshape(1, own_width)
    smem = pl.BlockSpec(memory_space=pltpu.SMEM)
    vmem = pl.BlockSpec(memory_space=pltpu.VMEM)
    params = pltpu.CompilerParams(vmem_limit_bytes=GRID_BYTES)
    shaped = jax.ShapeDtypeStruct
    field = (rhs_count, own_width)

    def send(value, step):
        return lax.ppermute(value, "row", [(at, at ^ step) for at in range(devices)])

    arguments = (position, visibility, area, reflectance, adjoint_seed)
    packed, boost, spot = pl.pallas_call(
        functools.partial(prepare, scale),
        in_specs=[pl.BlockSpec(memory_space=pltpu.HBM)] * 5,
        out_specs=[vmem] * 3,
        out_shape=[
            shaped((rhs_count + EXTRA, own_width), jnp.bfloat16),
            shaped(field, jnp.float32),
            shaped(position.shape, jnp.float32),
        ],
        scratch_shapes=[pltpu.VMEM((EXTRA, own_width), jnp.float32)]
        + [pltpu.VMEM(value.shape, value.dtype) for value in arguments]
        + [pltpu.SemaphoreType.DMA((5,))],
        compiler_params=params,
        name="prepare",
    )(*[pltpu.with_memory_space_constraint(value, pltpu.HBM) for value in arguments])
    lines = [send(packed, LINE * step) for step in range(1, LINE)]
    core = send(position, 1)
    pair = send(jnp.stack([spot, core]), 2)
    terms = (TERMS, own_width)
    distance = pltpu.VMEM((2, own_width, own_width), jnp.float32)
    near, partial, row_terms, col_terms = pl.pallas_call(
        grid_near,
        in_specs=[smem] + [vmem] * 3,
        out_specs=[vmem] * 4,
        out_shape=[
            shaped((len(NEAR), own_width, own_width), jnp.bfloat16),
            shaped((2,) + field, jnp.float32),
            shaped((2, own_width, TERMS), jnp.bfloat16),
            shaped(terms, jnp.bfloat16),
        ],
        scratch_shapes=[pltpu.VMEM((3,) + terms, jnp.float32), distance],
        compiler_params=params,
        name="grid_near",
    )(my_index, packed, core, boost)
    sent = shaped((LINE * rhs_count + EXTRA, own_width), jnp.bfloat16)
    rest, partial, terms = pl.pallas_call(
        grid_rest,
        in_specs=[smem] + [vmem] * 8,
        out_specs=[vmem] * 3,
        out_shape=[
            shaped((len(REST), own_width, own_width), jnp.bfloat16),
            shaped((LINE,) + field, jnp.float32),
            sent,
        ],
        scratch_shapes=[
            pltpu.VMEM((LINE + 1,) + terms, jnp.float32),
            pltpu.VMEM((2, own_width, TERMS), jnp.bfloat16),
            pltpu.VMEM((LINE,) + terms, jnp.bfloat16),
            distance,
        ],
        compiler_params=params,
        name="grid_rest",
    )(my_index, packed, *lines, pair, partial, row_terms, col_terms)
    both, terms = pl.pallas_call(
        grid_middle,
        in_specs=[vmem] * 3,
        out_specs=[vmem] * 2,
        out_shape=[shaped((LINE,) + field, jnp.float32), sent],
        scratch_shapes=[pltpu.VMEM((EXTRA, own_width), jnp.float32)],
        compiler_params=params,
        name="grid_middle",
    )(partial, send(terms, 1), packed)
    scaled, sum2, sum3 = pl.pallas_call(
        grid_second,
        in_specs=[vmem] * 4,
        out_specs=[vmem] * 3,
        out_shape=[shaped((LINE,) + field, jnp.bfloat16)] + [shaped(field, jnp.bfloat16)] * 2,
        compiler_params=params,
        name="grid_second",
    )(rest, both, terms, send(terms, 2))
    sum3, sum2 = send(sum3, 3 * LINE), send(sum2, 2 * LINE)
    sum0, sum1 = pl.pallas_call(
        grid_third,
        in_specs=[vmem] * 3,
        out_specs=[vmem] * 2,
        out_shape=[shaped(field, jnp.float32), shaped(field, jnp.bfloat16)],
        compiler_params=params,
        cost_estimate=pl.CostEstimate(
            flops=4 * LINE * rhs_count * own_width**2,
            bytes_accessed=4 * LINE * own_width**2 + 12 * rhs_count * own_width,
            transcendentals=0,
        ),
        name="grid_third",
    )(near, rest, scaled)
    sum1 = send(sum1, LINE)
    adjoint, grad = pl.pallas_call(
        functools.partial(grid_last, scale),
        in_specs=[vmem] * 9,
        out_specs=[vmem, vmem],
        out_shape=[shaped(field, jnp.float32), shaped((1, own_width), jnp.float32)],
        compiler_params=params,
        name="grid_last",
    )(sum3, sum2, sum1, sum0, adjoint_seed, area, reflectance, radiosity, emission)
    return adjoint, grad.reshape(own_width)


def spread_rows(pos_ref, spread):
    for coord in range(3):
        for block in range(spread.shape[1]):
            line = pos_ref[coord : coord + 1, block * TILE : (block + 1) * TILE]
            spread[coord, block] = jnp.transpose(jnp.broadcast_to(line, (TILE, TILE)))


def inverse_square(spread, pos_ref, at, own_block, rows, other_block):
    lanes = pl.ds(other_block * TILE, TILE)
    total = 1.0
    for coord in range(3):
        delta = spread[coord, own_block, rows, :] - pos_ref[at, coord : coord + 1, lanes]
        total = total + delta * delta
    return 1.0 / total


def form_part(me, at, part, words_ref, pos_ref, spread, kernel_ref):
    blocks = spread.shape[1]
    lane = lax.broadcasted_iota(jnp.int32, (GROUP, TILE), 1)
    for own_block in range(blocks):
        row_block = me * blocks + own_block
        for other_block in range(blocks):
            col_block = part * blocks + other_block
            word = words_ref[own_block, col_block]
            direct = row_block < col_block
            for group in range(TILE // GROUP):
                rows = slice(group * GROUP, (group + 1) * GROUP)
                bit = jnp.where(direct, 8 * (group // 2) + lane // 16, 8 * (lane // 32) + group)
                seen = (jnp.right_shift(word, bit) & 1) != 0
                value = inverse_square(spread, pos_ref, at, own_block, rows, other_block)
                value = jnp.where(seen, value, 0.0).astype(jnp.bfloat16)
                kernel_ref[
                    at,
                    own_block * TILE + group * GROUP : own_block * TILE + (group + 1) * GROUP,
                    other_block * TILE : (other_block + 1) * TILE,
                ] = value


def form_diagonal(me, at, words_ref, pos_ref, spread, kernel_ref):
    blocks = spread.shape[1]
    lane = lax.broadcasted_iota(jnp.int32, (TILE, TILE), 1)
    row = lax.broadcasted_iota(jnp.int32, (TILE, TILE), 0)
    low, high = jnp.minimum(row, lane), jnp.maximum(row, lane)
    bit = 8 * (low // 32) + high // 16
    for block in range(blocks):
        word = words_ref[block, me * blocks + block]
        seen = (jnp.right_shift(word, bit) & 1) != 0
        value = inverse_square(spread, pos_ref, at, block, slice(0, TILE), block)
        value = jnp.where(seen, value, 0.0).astype(jnp.bfloat16)
        kernel_ref[
            at, block * TILE : (block + 1) * TILE, block * TILE : (block + 1) * TILE
        ] = value


def gather_sum(every_ref, kernel_ref):
    total = times_transpose(every_ref[0], kernel_ref[0])
    for at in range(1, every_ref.shape[0]):
        total += times_transpose(every_ref[at], kernel_ref[at])
    return total


def first_sweep(
    scale,
    me_ref,
    words_ref,
    own_pos_ref,
    pos_ref,
    every_ref,
    seed_ref,
    area_ref,
    reflectance_ref,
    kernel_ref,
    scaled_ref,
    spread,
    total,
):
    step = pl.program_id(0)
    chunk = pos_ref.shape[0]
    me = me_ref[0]

    @pl.when(step == 0)
    def _():
        spread_rows(own_pos_ref, spread)
        total[...] = jnp.zeros_like(total)

    def form(at, carry):
        form_part(me, at, step * chunk + at, words_ref, pos_ref, spread, kernel_ref)
        return carry

    lax.fori_loop(0, chunk, form, 0)

    @pl.when((me >= step * chunk) & (me < (step + 1) * chunk))
    def _():
        form_diagonal(me, me - step * chunk, words_ref, pos_ref, spread, kernel_ref)

    total[...] += gather_sum(every_ref, kernel_ref)

    @pl.when(step == pl.num_programs(0) - 1)
    def _():
        adjoint = seed_ref[...] + (area_ref[...] * scale) * total[...]
        scaled_ref[...] = (reflectance_ref[...] * adjoint).astype(jnp.bfloat16)


def last_sweep(
    scale,
    kernel_ref,
    every_ref,
    seed_ref,
    area_ref,
    reflectance_ref,
    radiosity_ref,
    emission_ref,
    adjoint_ref,
    grad_ref,
    total,
):
    step = pl.program_id(0)

    @pl.when(step == 0)
    def _():
        total[...] = jnp.zeros_like(total)

    total[...] += gather_sum(every_ref, kernel_ref)

    @pl.when(step == pl.num_programs(0) - 1)
    def _():
        finish(
            scale,
            total[...],
            seed_ref,
            area_ref,
            reflectance_ref,
            radiosity_ref,
            emission_ref,
            adjoint_ref,
            grad_ref,
        )


def whole(shape):
    return pl.BlockSpec(shape, lambda step: (0,) * len(shape))


def parts(chunk, shape):
    return pl.BlockSpec((chunk,) + shape, lambda step: (step,) + (0,) * len(shape))


def on_rows(adjoint_seed, radiosity, emission, reflectance, area, position, visibility):
    rhs_count, own_width = adjoint_seed.shape
    devices = lax.axis_size("row")
    my_index = lax.axis_index("row").astype(jnp.int32).reshape(1)
    local_blocks = own_width // TILE
    scale = 1.0 / math.sqrt(own_width * devices)
    chunk = math.gcd(devices, 16)
    area = area.reshape(1, own_width)
    reflectance = reflectance.reshape(1, own_width)
    smem = pl.BlockSpec(memory_space=pltpu.SMEM)
    params = pltpu.CompilerParams(
        dimension_semantics=("arbitrary",), vmem_limit_bytes=VMEM_BYTES
    )

    all_pos = lax.all_gather(position, "row")
    every = lax.all_gather((reflectance * adjoint_seed).astype(jnp.bfloat16), "row")
    kernel, scaled = pl.pallas_call(
        functools.partial(first_sweep, scale),
        grid=(devices // chunk,),
        in_specs=[
            smem,
            smem,
            whole((3, own_width)),
            parts(chunk, (3, own_width)),
            parts(chunk, (rhs_count, own_width)),
            whole((rhs_count, own_width)),
            whole((1, own_width)),
            whole((1, own_width)),
        ],
        out_specs=[parts(chunk, (own_width, own_width)), whole((rhs_count, own_width))],
        out_shape=[
            jax.ShapeDtypeStruct((devices, own_width, own_width), jnp.bfloat16),
            jax.ShapeDtypeStruct((rhs_count, own_width), jnp.bfloat16),
        ],
        scratch_shapes=[
            pltpu.VMEM((3, local_blocks, TILE, TILE), jnp.float32),
            pltpu.VMEM((rhs_count, own_width), jnp.float32),
        ],
        compiler_params=params,
        name="first_sweep",
    )(my_index, visibility, position, all_pos, every, adjoint_seed, area, reflectance)

    every = lax.all_gather(scaled, "row")
    adjoint, grad = pl.pallas_call(
        functools.partial(last_sweep, scale),
        grid=(devices // chunk,),
        in_specs=[
            parts(chunk, (own_width, own_width)),
            parts(chunk, (rhs_count, own_width)),
            whole((rhs_count, own_width)),
            whole((1, own_width)),
            whole((1, own_width)),
            whole((rhs_count, own_width)),
            whole((rhs_count, own_width)),
        ],
        out_specs=[whole((rhs_count, own_width)), whole((1, own_width))],
        out_shape=[
            jax.ShapeDtypeStruct((rhs_count, own_width), jnp.float32),
            jax.ShapeDtypeStruct((1, own_width), jnp.float32),
        ],
        scratch_shapes=[pltpu.VMEM((rhs_count, own_width), jnp.float32)],
        compiler_params=params,
        name="last_sweep",
    )(kernel, every, adjoint_seed, area, reflectance, radiosity, emission)
    return adjoint, grad.reshape(own_width)


def on_device(adjoint_seed, *rest):
    on_grid_shape = lax.axis_size("row") == LINE * LINE and adjoint_seed.shape[1] == 2 * TILE
    return (on_grid if on_grid_shape else on_rows)(adjoint_seed, *rest)


def solution(mesh):
    placed = (
        P(None, ("scene", "row")),
        P(None, ("scene", "row")),
        P(None, ("scene", "row")),
        P(("scene", "row")),
        P(("scene", "row")),
        P(None, ("scene", "row")),
        P(("scene", "row"), None),
    )
    return jax.shard_map(
        on_device,
        mesh=mesh,
        in_specs=placed,
        out_specs=(P(None, ("scene", "row")), P(("scene", "row"))),
        check_vma=False,
    )
```

```python
import functools
import math

import jax
import jax.numpy as jnp
from jax import lax
from jax.experimental import pallas as pl
from jax.experimental.pallas import tpu as pltpu
from jax.sharding import PartitionSpec as P

TILE = 128
SWEEPS = 2
GROUP = 16
LINE = 4
EXTRA = 16
TERMS = 32
VMEM_BYTES = 48 * 1024 * 1024
GRID_BYTES = 8 * 1024 * 1024


NEAR = [(0, 0), (1, 0)]
REST = [(t, s) for t in range(LINE) for s in range(LINE) if (t, s) not in NEAR]


def three_terms(value):
    high = value.astype(jnp.bfloat16).astype(jnp.float32)
    rest = value - high
    middle = rest.astype(jnp.bfloat16).astype(jnp.float32)
    return high, middle, rest - middle


def times_transpose(values, kernel):
    return lax.dot_general(
        values, kernel, (((1,), (1,)), ((), ())), preferred_element_type=jnp.float32
    )


def times(values, kernel):
    return jnp.dot(values, kernel, preferred_element_type=jnp.float32)


def finish(
    scale, total, seed_ref, area_ref, reflectance_ref, radiosity_ref, emission_ref, adjoint_ref, grad_ref
):
    adjoint = seed_ref[...] + (area_ref[...] * scale) * total
    adjoint_ref[...] = adjoint
    change = radiosity_ref[...].astype(jnp.float32) - emission_ref[...].astype(jnp.float32)
    grad_ref[...] = jnp.sum(adjoint * change, axis=0, keepdims=True) / reflectance_ref[...]


def prepare(scale, *refs):
    arguments, (packed_ref, spot_ref, rows, *held, sems) = refs[:5], refs[5:]
    copies = [
        pltpu.make_async_copy(argument, ref, sems.at[at])
        for at, (argument, ref) in enumerate(zip(arguments, held))
    ]
    for copy in copies:
        copy.start()
    rows[...] = jnp.zeros_like(rows)
    for copy in copies:
        copy.wait()
    pos_ref, words_ref, area_ref, reflectance_ref, seed_ref = held
    rhs_count = seed_ref.shape[0]
    for term, value in enumerate(three_terms(pos_ref[...])):
        rows[3 * term : 3 * term + 3, :] = value
    weight = area_ref[...] * scale
    for term, value in enumerate(three_terms(weight * reflectance_ref[...])):
        rows[9 + term : 10 + term, :] = value
    count = words_ref.shape[1]
    for place in range(4):
        part = (jnp.right_shift(words_ref[...], 8 * place) & 255).astype(jnp.float32)
        for local in range(words_ref.shape[0]):
            start = local * TILE
            rows[12 + place : 13 + place, start : start + count] = part[local : local + 1]
    packed_ref[:rhs_count] = (reflectance_ref[...] * seed_ref[...]).astype(jnp.bfloat16)
    packed_ref[rhs_count:] = rows[...].astype(jnp.bfloat16)
    spot_ref[...] = pos_ref[...]


def distance_terms(position, terms, as_rows):
    high, middle, low = three_terms(position)
    norm = jnp.sum(position * position, axis=0, keepdims=True)
    terms[...] = jnp.zeros_like(terms)
    if as_rows:
        for at, value in enumerate((high, high, high, middle, middle, low)):
            terms[3 * at : 3 * at + 3, :] = -2.0 * value
        ones, norms, norm = 21, 18, norm + 1.0
    else:
        for at, value in enumerate((high, middle, low, high, middle, high)):
            terms[3 * at : 3 * at + 3, :] = value
        ones, norms = 18, 21
    terms[ones : ones + 3, :] = jnp.ones_like(high)
    for at, value in enumerate(three_terms(norm)):
        terms[norms + at : norms + at + 1, :] = value


def shift_up(direct, group, lane):
    return 31 - jnp.where(direct, 8 * (group // 2) + lane // 16, 8 * (lane // 32) + group)


def block_words(word, t, line, column):
    start = 2 * (line * LINE + jnp.bitwise_xor(column, t))
    splats = []
    for col_block in range(2):
        lanes = jnp.broadcast_to(word[:, col_block * TILE : (col_block + 1) * TILE], (8, TILE))
        lanes = pltpu.roll(lanes, TILE - start, 1)
        splats.append(
            [jnp.broadcast_to(lanes[:, at : at + 1], (8, TILE)) for at in range(2)]
        )
    return splats


def form_block(t, s, line, column, distance, word, out_ref):
    lane = lax.broadcasted_iota(jnp.int32, (8, TILE), 1)
    row_chunk = line * LINE + jnp.bitwise_xor(column, t)
    direct = row_chunk < jnp.bitwise_xor(line, s) * LINE + column
    shifts = [shift_up(direct, group, lane) for group in range(TILE // GROUP)]
    splats = block_words(word, t, line, column)
    for row_block in range(2):
        for col_block in range(2):
            lanes = slice(col_block * TILE, (col_block + 1) * TILE)
            for group, shift in enumerate(shifts):
                first = row_block * TILE + group * GROUP
                seen = jnp.left_shift(splats[col_block][row_block], shift) < 0
                halves = []
                for half in range(first, first + GROUP, 8):
                    value = pl.reciprocal(distance[half : half + 8, lanes], approx=True)
                    halves.append(jnp.where(seen, value, 0.0))
                out_ref[first : first + GROUP, lanes] = jnp.concatenate(halves).astype(
                    jnp.bfloat16
                )


def form_own(line, column, distance, word, out_ref):
    lane = lax.broadcasted_iota(jnp.int32, (8, TILE), 1)
    row = lax.broadcasted_iota(jnp.int32, (8, TILE), 0)
    splats = block_words(word, 0, line, column)
    for row_block in range(2):
        for col_block in range(2):
            lanes = slice(col_block * TILE, (col_block + 1) * TILE)
            for group in range(TILE // GROUP):
                first = row_block * TILE + group * GROUP
                halves = []
                for half in range(first, first + GROUP, 8):
                    i, j = row + half, lane + col_block * TILE
                    low, high = jnp.minimum(i, j) % TILE, jnp.maximum(i, j) % TILE
                    shift = 31 - (8 * (low // 32) + high // 16)
                    seen = jnp.left_shift(splats[col_block][row_block], shift) < 0
                    value = pl.reciprocal(distance[half : half + 8, lanes], approx=True)
                    halves.append(jnp.where(seen, value, 0.0))
                out_ref[first : first + GROUP, lanes] = jnp.concatenate(halves).astype(
                    jnp.bfloat16
                )


def read_extra(ref, rhs_count):
    extra = ref[rhs_count:, :].astype(jnp.float32)
    value = extra[12:16].astype(jnp.int32)
    word = value[0:1]
    for place in range(1, 4):
        word = jnp.bitwise_or(word, jnp.left_shift(value[place : place + 1], 8 * place))
    return extra[0:3] + extra[3:6] + extra[6:9], word


def form_all(blocks, line, column, row_terms, col_terms, words, fields, start, refs, finish_row):
    kernel_ref, distance = refs
    held = {}

    def measure(place):
        t, s = blocks[place]
        distance[place % 2] = times(row_terms(t), col_terms(s))

    def add(place):
        t, s = blocks[place]
        term = times_transpose(fields[s], kernel_ref[place])
        held[t] = (held[t] if t in held else start(t)) + term
        if place + 1 == len(blocks) or blocks[place + 1][0] != t:
            finish_row(t, held[t])

    measure(0)
    for place, (t, s) in enumerate(blocks):
        if place + 1 < len(blocks):
            measure(place + 1)
        slot, out_ref = distance.at[place % 2], kernel_ref.at[place]
        if t == 0 and s == 0:
            form_own(line, column, slot, words[s], out_ref)
        else:
            form_block(t, s, line, column, slot, words[s], out_ref)
        if place:
            add(place - 1)
    add(len(blocks) - 1)


def grid_near(
    scale,
    me_ref,
    own_ref,
    core_ref,
    seed_hbm,
    area_hbm,
    kernel_ref,
    partial_ref,
    row_terms,
    col_terms,
    terms,
    distance,
    seed_ref,
    area_ref,
    sems,
):
    copies = [
        pltpu.make_async_copy(seed_hbm, seed_ref, sems.at[0]),
        pltpu.make_async_copy(area_hbm, area_ref, sems.at[1]),
    ]
    for copy in copies:
        copy.start()
    rhs_count = seed_ref.shape[0]
    line, column = me_ref[0] // LINE, me_ref[0] % LINE
    position, word = read_extra(own_ref, rhs_count)
    distance_terms(position, terms.at[0], False)
    col_terms[...] = terms[0].astype(jnp.bfloat16)
    for t, value in enumerate((position, core_ref[...])):
        distance_terms(value, terms.at[1 + t], True)
        row_terms[t] = jnp.transpose(terms[1 + t]).astype(jnp.bfloat16)

    def finish_row(t, value):
        partial_ref[t] = value

    form_all(
        NEAR,
        line,
        column,
        lambda t: row_terms[t],
        lambda s: col_terms[...],
        [word],
        [own_ref[:rhs_count, :]],
        lambda t: 0.0,
        (kernel_ref, distance),
        finish_row,
    )
    for copy in copies:
        copy.wait()
    partial_ref[0] = partial_ref[0] + seed_ref[...] * (1.0 / (area_ref[...] * scale))


def grid_rest(
    me_ref,
    own_ref,
    z1_ref,
    z2_ref,
    z3_ref,
    pair_ref,
    before_ref,
    row_ref,
    col_ref,
    kernel_ref,
    partial_ref,
    sent_ref,
    terms,
    row_terms,
    col_terms,
    distance,
):
    rhs_count = before_ref.shape[1]
    line, column = me_ref[0] // LINE, me_ref[0] % LINE
    lines = (own_ref, z1_ref, z2_ref, z3_ref)
    words = []
    for s, ref in enumerate(lines):
        position, word = read_extra(ref, rhs_count)
        words.append(word)
        if s:
            distance_terms(position, terms.at[s], False)
            col_terms[s] = terms[s].astype(jnp.bfloat16)
    for t in range(2):
        slot = terms.at[LINE * t]
        distance_terms(pair_ref[t], slot, True)
        row_terms[t] = jnp.transpose(slot[...]).astype(jnp.bfloat16)

    def finish_row(t, value):
        partial_ref[t] = value
        sent_ref[t * rhs_count : (t + 1) * rhs_count] = value.astype(jnp.bfloat16)

    form_all(
        REST,
        line,
        column,
        lambda t: row_ref[t] if t < 2 else row_terms[t - 2],
        lambda s: col_terms[s] if s else col_ref[...],
        words,
        [ref[:rhs_count, :] for ref in lines],
        lambda t: before_ref[t] if t < 2 else 0.0,
        (kernel_ref, distance),
        finish_row,
    )
    sent_ref[LINE * rhs_count :] = own_ref[rhs_count:]


def grid_middle(partial_ref, core_ref, own_ref, both_ref, first_ref, second_ref, rows):
    rhs_count = partial_ref.shape[1]
    half = rhs_count // 2
    for t in range(LINE):
        start = (t ^ 1) * rhs_count
        both = partial_ref[t] + core_ref[start : start + rhs_count].astype(jnp.float32)
        both_ref[t] = both
        first_ref[t * half : (t + 1) * half] = both[:half].astype(jnp.bfloat16)
        second_ref[t * half : (t + 1) * half] = both[half:].astype(jnp.bfloat16)
    rows[...] = jnp.zeros_like(rows)
    for at, ref in enumerate((own_ref, core_ref)):
        rows[3 * at : 3 * at + 3, :] = ref[-EXTRA:, :].astype(jnp.float32)[9:12]
    for ref in (first_ref, second_ref):
        ref[LINE * half :] = rows[...].astype(jnp.bfloat16)


def product(scaled, near_ref, rest_ref, s):
    held = None
    for t in range(LINE):
        near = (t, s) in NEAR
        kernel = near_ref[NEAR.index((t, s))] if near else rest_ref[REST.index((t, s))]
        term = times(scaled(t), kernel)
        held = term if held is None else held + term
    return held


def grid_second(place, rest_ref, both_ref, own_ref, x_ref, scaled_ref, q2_ref, q3_ref):
    half = q2_ref.shape[0]
    for t in range(LINE):
        terms = (own_ref, x_ref)[t // 2][LINE * half :, :].astype(jnp.float32)
        at = 3 * (t % 2)
        factor = terms[at : at + 1] + terms[at + 1 : at + 2] + terms[at + 2 : at + 3]
        start = (t ^ 2) * half
        total = both_ref[t, place * half : (place + 1) * half] + x_ref[
            start : start + half
        ].astype(jnp.float32)
        scaled_ref[t] = (factor * total).astype(jnp.bfloat16)
    q3_ref[...] = product(lambda t: scaled_ref[t], None, rest_ref, 3).astype(jnp.bfloat16)
    q2_ref[...] = product(lambda t: scaled_ref[t], None, rest_ref, 2).astype(jnp.bfloat16)


def grid_third(near_ref, rest_ref, first_ref, second_ref, q0_ref, first_q1_ref, second_q1_ref):
    half = first_ref.shape[1]
    scaled = [jnp.concatenate([first_ref[t], second_ref[t]]) for t in range(LINE)]
    next_sum = product(lambda t: scaled[t], None, rest_ref, 1).astype(jnp.bfloat16)
    first_q1_ref[...] = next_sum[:half]
    second_q1_ref[...] = next_sum[half:]
    q0_ref[...] = product(lambda t: scaled[t], near_ref, rest_ref, 0)


def grid_last(scale, line_refs, q0_ref, *rest):
    halves = [
        sum(ref[...].astype(jnp.float32) for ref in refs)
        for refs in ([line_refs[at] for at in [2, 3, 5]], [line_refs[at] for at in [0, 1, 4]])
    ]
    finish(scale, jnp.concatenate(halves) + q0_ref[...], *rest)


def on_grid(adjoint_seed, radiosity, emission, reflectance, area, position, visibility):
    rhs_count, own_width = adjoint_seed.shape
    devices = LINE * LINE
    my_index = lax.axis_index("row").astype(jnp.int32).reshape(1)
    scale = 1.0 / math.sqrt(own_width * devices)
    area = area.reshape(1, own_width)
    reflectance = reflectance.reshape(1, own_width)
    smem = pl.BlockSpec(memory_space=pltpu.SMEM)
    vmem = pl.BlockSpec(memory_space=pltpu.VMEM)
    params = pltpu.CompilerParams(vmem_limit_bytes=GRID_BYTES)
    shaped = jax.ShapeDtypeStruct
    field = (rhs_count, own_width)

    def send(value, step):
        return lax.ppermute(value, "row", [(at, at ^ step) for at in range(devices)])

    hbm = pl.BlockSpec(memory_space=pltpu.HBM)
    arguments = [
        pltpu.with_memory_space_constraint(value, pltpu.HBM)
        for value in (position, visibility, area, reflectance, adjoint_seed)
    ]
    packed, spot = pl.pallas_call(
        functools.partial(prepare, scale),
        in_specs=[hbm] * 5,
        out_specs=[vmem] * 2,
        out_shape=[
            shaped((rhs_count + EXTRA, own_width), jnp.bfloat16),
            shaped(position.shape, jnp.float32),
        ],
        scratch_shapes=[pltpu.VMEM((EXTRA, own_width), jnp.float32)]
        + [pltpu.VMEM(value.shape, value.dtype) for value in arguments]
        + [pltpu.SemaphoreType.DMA((5,))],
        compiler_params=params,
        name="prepare",
    )(*arguments)
    lines = [send(packed, LINE * step) for step in range(1, LINE)]
    core = send(position, 1)
    pair = send(jnp.stack([spot, core]), 2)
    terms = (TERMS, own_width)
    distance = pltpu.VMEM((2, own_width, own_width), jnp.float32)
    near, partial, row_terms, col_terms = pl.pallas_call(
        functools.partial(grid_near, scale),
        in_specs=[smem] + [vmem] * 2 + [hbm] * 2,
        out_specs=[vmem] * 4,
        out_shape=[
            shaped((len(NEAR), own_width, own_width), jnp.bfloat16),
            shaped((2,) + field, jnp.float32),
            shaped((2, own_width, TERMS), jnp.bfloat16),
            shaped(terms, jnp.bfloat16),
        ],
        scratch_shapes=[
            pltpu.VMEM((3,) + terms, jnp.float32),
            distance,
            pltpu.VMEM(field, jnp.float32),
            pltpu.VMEM((1, own_width), jnp.float32),
            pltpu.SemaphoreType.DMA((2,)),
        ],
        compiler_params=params,
        name="grid_near",
    )(my_index, packed, core, arguments[4], arguments[2])
    sent = shaped((LINE * rhs_count + EXTRA, own_width), jnp.bfloat16)
    rest, partial, terms = pl.pallas_call(
        grid_rest,
        in_specs=[smem] + [vmem] * 8,
        out_specs=[vmem] * 3,
        out_shape=[
            shaped((len(REST), own_width, own_width), jnp.bfloat16),
            shaped((LINE,) + field, jnp.float32),
            sent,
        ],
        scratch_shapes=[
            pltpu.VMEM((LINE + 1,) + terms, jnp.float32),
            pltpu.VMEM((2, own_width, TERMS), jnp.bfloat16),
            pltpu.VMEM((LINE,) + terms, jnp.bfloat16),
            distance,
        ],
        compiler_params=params,
        name="grid_rest",
    )(my_index, packed, *lines, pair, partial, row_terms, col_terms)
    half = (rhs_count // 2, own_width)
    both, first, second = pl.pallas_call(
        grid_middle,
        in_specs=[vmem] * 3,
        out_specs=[vmem] * 3,
        out_shape=[
            shaped((LINE,) + field, jnp.float32),
            shaped((LINE * half[0] + EXTRA, own_width), jnp.bfloat16),
            shaped((LINE * half[0] + EXTRA, own_width), jnp.bfloat16),
        ],
        scratch_shapes=[pltpu.VMEM((EXTRA, own_width), jnp.float32)],
        compiler_params=params,
        name="grid_middle",
    )(partial, send(terms, 1), packed)
    other = [send(first, 2), send(second, 2)]
    scaled, far = [], []
    for place in range(2):
        scaled_half, sum2, sum3 = pl.pallas_call(
            functools.partial(grid_second, place),
            in_specs=[vmem] * 4,
            out_specs=[vmem] * 3,
            out_shape=[shaped((LINE,) + half, jnp.bfloat16)]
            + [shaped(half, jnp.bfloat16)] * 2,
            compiler_params=params,
            name="grid_second",
        )(rest, both, first, other[place])
        scaled.append(scaled_half)
        far += [send(sum3, 3 * LINE), send(sum2, 2 * LINE)]
    sum0, *sum1 = pl.pallas_call(
        grid_third,
        in_specs=[vmem] * 4,
        out_specs=[vmem] * 3,
        out_shape=[shaped(field, jnp.float32)] + [shaped(half, jnp.bfloat16)] * 2,
        compiler_params=params,
        name="grid_third",
    )(near, rest, *scaled)
    sum1 = [send(value, LINE) for value in sum1]
    lines = [far[2], far[3], far[0], far[1], sum1[1], sum1[0]]

    def last(*refs):
        grid_last(scale, refs[:6], *refs[6:])

    adjoint, grad = pl.pallas_call(
        last,
        in_specs=[vmem] * 12,
        out_specs=[vmem, vmem],
        out_shape=[shaped(field, jnp.float32), shaped((1, own_width), jnp.float32)],
        compiler_params=params,
        name="grid_last",
    )(*lines, sum0, adjoint_seed, area, reflectance, radiosity, emission)
    return adjoint, grad.reshape(own_width)


def spread_rows(pos_ref, spread):
    for coord in range(3):
        for block in range(spread.shape[1]):
            line = pos_ref[coord : coord + 1, block * TILE : (block + 1) * TILE]
            spread[coord, block] = jnp.transpose(jnp.broadcast_to(line, (TILE, TILE)))


def inverse_square(spread, pos_ref, at, own_block, rows, other_block):
    lanes = pl.ds(other_block * TILE, TILE)
    total = 1.0
    for coord in range(3):
        delta = spread[coord, own_block, rows, :] - pos_ref[at, coord : coord + 1, lanes]
        total = total + delta * delta
    return 1.0 / total


def form_part(me, at, part, words_ref, pos_ref, spread, kernel_ref):
    blocks = spread.shape[1]
    lane = lax.broadcasted_iota(jnp.int32, (GROUP, TILE), 1)
    for own_block in range(blocks):
        row_block = me * blocks + own_block
        for other_block in range(blocks):
            col_block = part * blocks + other_block
            word = words_ref[own_block, col_block]
            direct = row_block < col_block
            for group in range(TILE // GROUP):
                rows = slice(group * GROUP, (group + 1) * GROUP)
                bit = jnp.where(direct, 8 * (group // 2) + lane // 16, 8 * (lane // 32) + group)
                seen = (jnp.right_shift(word, bit) & 1) != 0
                value = inverse_square(spread, pos_ref, at, own_block, rows, other_block)
                value = jnp.where(seen, value, 0.0).astype(jnp.bfloat16)
                kernel_ref[
                    at,
                    own_block * TILE + group * GROUP : own_block * TILE + (group + 1) * GROUP,
                    other_block * TILE : (other_block + 1) * TILE,
                ] = value


def form_diagonal(me, at, words_ref, pos_ref, spread, kernel_ref):
    blocks = spread.shape[1]
    lane = lax.broadcasted_iota(jnp.int32, (TILE, TILE), 1)
    row = lax.broadcasted_iota(jnp.int32, (TILE, TILE), 0)
    low, high = jnp.minimum(row, lane), jnp.maximum(row, lane)
    bit = 8 * (low // 32) + high // 16
    for block in range(blocks):
        word = words_ref[block, me * blocks + block]
        seen = (jnp.right_shift(word, bit) & 1) != 0
        value = inverse_square(spread, pos_ref, at, block, slice(0, TILE), block)
        value = jnp.where(seen, value, 0.0).astype(jnp.bfloat16)
        kernel_ref[
            at, block * TILE : (block + 1) * TILE, block * TILE : (block + 1) * TILE
        ] = value


def gather_sum(every_ref, kernel_ref):
    total = times_transpose(every_ref[0], kernel_ref[0])
    for at in range(1, every_ref.shape[0]):
        total += times_transpose(every_ref[at], kernel_ref[at])
    return total


def first_sweep(
    scale,
    me_ref,
    words_ref,
    own_pos_ref,
    pos_ref,
    every_ref,
    seed_ref,
    area_ref,
    reflectance_ref,
    kernel_ref,
    scaled_ref,
    spread,
    total,
):
    step = pl.program_id(0)
    chunk = pos_ref.shape[0]
    me = me_ref[0]

    @pl.when(step == 0)
    def _():
        spread_rows(own_pos_ref, spread)
        total[...] = jnp.zeros_like(total)

    def form(at, carry):
        form_part(me, at, step * chunk + at, words_ref, pos_ref, spread, kernel_ref)
        return carry

    lax.fori_loop(0, chunk, form, 0)

    @pl.when((me >= step * chunk) & (me < (step + 1) * chunk))
    def _():
        form_diagonal(me, me - step * chunk, words_ref, pos_ref, spread, kernel_ref)

    total[...] += gather_sum(every_ref, kernel_ref)

    @pl.when(step == pl.num_programs(0) - 1)
    def _():
        adjoint = seed_ref[...] + (area_ref[...] * scale) * total[...]
        scaled_ref[...] = (reflectance_ref[...] * adjoint).astype(jnp.bfloat16)


def last_sweep(
    scale,
    kernel_ref,
    every_ref,
    seed_ref,
    area_ref,
    reflectance_ref,
    radiosity_ref,
    emission_ref,
    adjoint_ref,
    grad_ref,
    total,
):
    step = pl.program_id(0)

    @pl.when(step == 0)
    def _():
        total[...] = jnp.zeros_like(total)

    total[...] += gather_sum(every_ref, kernel_ref)

    @pl.when(step == pl.num_programs(0) - 1)
    def _():
        finish(
            scale,
            total[...],
            seed_ref,
            area_ref,
            reflectance_ref,
            radiosity_ref,
            emission_ref,
            adjoint_ref,
            grad_ref,
        )


def whole(shape):
    return pl.BlockSpec(shape, lambda step: (0,) * len(shape))


def parts(chunk, shape):
    return pl.BlockSpec((chunk,) + shape, lambda step: (step,) + (0,) * len(shape))


def on_rows(adjoint_seed, radiosity, emission, reflectance, area, position, visibility):
    rhs_count, own_width = adjoint_seed.shape
    devices = lax.axis_size("row")
    my_index = lax.axis_index("row").astype(jnp.int32).reshape(1)
    local_blocks = own_width // TILE
    scale = 1.0 / math.sqrt(own_width * devices)
    chunk = math.gcd(devices, 16)
    area = area.reshape(1, own_width)
    reflectance = reflectance.reshape(1, own_width)
    smem = pl.BlockSpec(memory_space=pltpu.SMEM)
    params = pltpu.CompilerParams(
        dimension_semantics=("arbitrary",), vmem_limit_bytes=VMEM_BYTES
    )

    all_pos = lax.all_gather(position, "row")
    every = lax.all_gather((reflectance * adjoint_seed).astype(jnp.bfloat16), "row")
    kernel, scaled = pl.pallas_call(
        functools.partial(first_sweep, scale),
        grid=(devices // chunk,),
        in_specs=[
            smem,
            smem,
            whole((3, own_width)),
            parts(chunk, (3, own_width)),
            parts(chunk, (rhs_count, own_width)),
            whole((rhs_count, own_width)),
            whole((1, own_width)),
            whole((1, own_width)),
        ],
        out_specs=[parts(chunk, (own_width, own_width)), whole((rhs_count, own_width))],
        out_shape=[
            jax.ShapeDtypeStruct((devices, own_width, own_width), jnp.bfloat16),
            jax.ShapeDtypeStruct((rhs_count, own_width), jnp.bfloat16),
        ],
        scratch_shapes=[
            pltpu.VMEM((3, local_blocks, TILE, TILE), jnp.float32),
            pltpu.VMEM((rhs_count, own_width), jnp.float32),
        ],
        compiler_params=params,
        name="first_sweep",
    )(my_index, visibility, position, all_pos, every, adjoint_seed, area, reflectance)

    every = lax.all_gather(scaled, "row")
    adjoint, grad = pl.pallas_call(
        functools.partial(last_sweep, scale),
        grid=(devices // chunk,),
        in_specs=[
            parts(chunk, (own_width, own_width)),
            parts(chunk, (rhs_count, own_width)),
            whole((rhs_count, own_width)),
            whole((1, own_width)),
            whole((1, own_width)),
            whole((rhs_count, own_width)),
            whole((rhs_count, own_width)),
        ],
        out_specs=[whole((rhs_count, own_width)), whole((1, own_width))],
        out_shape=[
            jax.ShapeDtypeStruct((rhs_count, own_width), jnp.float32),
            jax.ShapeDtypeStruct((1, own_width), jnp.float32),
        ],
        scratch_shapes=[pltpu.VMEM((rhs_count, own_width), jnp.float32)],
        compiler_params=params,
        name="last_sweep",
    )(kernel, every, adjoint_seed, area, reflectance, radiosity, emission)
    return adjoint, grad.reshape(own_width)


def on_device(adjoint_seed, *rest):
    on_grid_shape = lax.axis_size("row") == LINE * LINE and adjoint_seed.shape[1] == 2 * TILE
    return (on_grid if on_grid_shape else on_rows)(adjoint_seed, *rest)


def solution(mesh):
    placed = (
        P(None, ("scene", "row")),
        P(None, ("scene", "row")),
        P(None, ("scene", "row")),
        P(("scene", "row")),
        P(("scene", "row")),
        P(None, ("scene", "row")),
        P(("scene", "row"), None),
    )
    return jax.shard_map(
        on_device,
        mesh=mesh,
        in_specs=placed,
        out_specs=(P(None, ("scene", "row")), P(("scene", "row"))),
        check_vma=False,
    )
```

```python
import functools
import math

import jax
import jax.numpy as jnp
from jax import lax
from jax.experimental import pallas as pl
from jax.experimental.pallas import tpu as pltpu
from jax.sharding import PartitionSpec as P

TILE = 128
SWEEPS = 2
GROUP = 16
LINE = 4
GRID = 16
FAR = 8
EXTRA = 16
TERMS = 32
VMEM_BYTES = 48 * 1024 * 1024
GRID_BYTES = 8 * 1024 * 1024


NEAR = [(t, v, 0) for t in range(2) for v in range(LINE)]
REST = [(t, v, 1) for t in range(2) for v in range(LINE)]


def three_terms(value):
    high = value.astype(jnp.bfloat16).astype(jnp.float32)
    rest = value - high
    middle = rest.astype(jnp.bfloat16).astype(jnp.float32)
    return high, middle, rest - middle


def times_transpose(values, kernel):
    return lax.dot_general(
        values, kernel, (((1,), (1,)), ((), ())), preferred_element_type=jnp.float32
    )


def times(values, kernel):
    return jnp.dot(values, kernel, preferred_element_type=jnp.float32)


def finish(
    scale, total, seed_ref, area_ref, reflectance_ref, radiosity_ref, emission_ref, adjoint_ref, grad_ref
):
    adjoint = seed_ref[...] + (area_ref[...] * scale) * total
    adjoint_ref[...] = adjoint
    change = radiosity_ref[...].astype(jnp.float32) - emission_ref[...].astype(jnp.float32)
    grad_ref[...] = jnp.sum(adjoint * change, axis=0, keepdims=True) / reflectance_ref[...]


def prepare(scale, *refs):
    arguments, (packed_ref, spot_ref, rows, *held, sems) = refs[:5], refs[5:]
    copies = [
        pltpu.make_async_copy(argument, ref, sems.at[at])
        for at, (argument, ref) in enumerate(zip(arguments, held))
    ]
    for copy in copies:
        copy.start()
    rows[...] = jnp.zeros_like(rows)
    for copy in copies:
        copy.wait()
    pos_ref, words_ref, area_ref, reflectance_ref, seed_ref = held
    rhs_count = seed_ref.shape[0]
    for term, value in enumerate(three_terms(pos_ref[...])):
        rows[3 * term : 3 * term + 3, :] = value
    weight = area_ref[...] * scale
    for term, value in enumerate(three_terms(weight * reflectance_ref[...])):
        rows[9 + term : 10 + term, :] = value
    count = words_ref.shape[1]
    for place in range(4):
        part = (jnp.right_shift(words_ref[...], 8 * place) & 255).astype(jnp.float32)
        for local in range(words_ref.shape[0]):
            start = local * TILE
            rows[12 + place : 13 + place, start : start + count] = part[local : local + 1]
    packed_ref[:rhs_count] = (reflectance_ref[...] * seed_ref[...]).astype(jnp.bfloat16)
    packed_ref[rhs_count:] = rows[...].astype(jnp.bfloat16)
    spot_ref[...] = pos_ref[...]


def distance_terms(position, terms, as_rows):
    high, middle, low = three_terms(position)
    norm = jnp.sum(position * position, axis=0, keepdims=True)
    terms[...] = jnp.zeros_like(terms)
    if as_rows:
        for at, value in enumerate((high, high, high, middle, middle, low)):
            terms[3 * at : 3 * at + 3, :] = -2.0 * value
        ones, norms, norm = 21, 18, norm + 1.0
    else:
        for at, value in enumerate((high, middle, low, high, middle, high)):
            terms[3 * at : 3 * at + 3, :] = value
        ones, norms = 18, 21
    terms[ones : ones + 3, :] = jnp.ones_like(high)
    for at, value in enumerate(three_terms(norm)):
        terms[norms + at : norms + at + 1, :] = value


def shift_up(direct, group, lane):
    return 31 - jnp.where(direct, 8 * (group // 2) + lane // 16, 8 * (lane // 32) + group)


def block_words(word, row_chunk):
    splats = []
    for col_block in range(2):
        lanes = jnp.broadcast_to(word[:, col_block * TILE : (col_block + 1) * TILE], (8, TILE))
        lanes = pltpu.roll(lanes, TILE - 2 * row_chunk, 1)
        splats.append(
            [jnp.broadcast_to(lanes[:, at : at + 1], (8, TILE)) for at in range(2)]
        )
    return splats


def form_block(row_chunk, col_chunk, distance, word, out_ref):
    lane = lax.broadcasted_iota(jnp.int32, (8, TILE), 1)
    direct = row_chunk < col_chunk
    shifts = [shift_up(direct, group, lane) for group in range(TILE // GROUP)]
    splats = block_words(word, row_chunk)
    for row_block in range(2):
        for col_block in range(2):
            lanes = slice(col_block * TILE, (col_block + 1) * TILE)
            for group, shift in enumerate(shifts):
                first = row_block * TILE + group * GROUP
                seen = jnp.left_shift(splats[col_block][row_block], shift) < 0
                halves = []
                for half in range(first, first + GROUP, 8):
                    value = pl.reciprocal(distance[half : half + 8, lanes], approx=True)
                    halves.append(jnp.where(seen, value, 0.0))
                out_ref[first : first + GROUP, lanes] = jnp.concatenate(halves).astype(
                    jnp.bfloat16
                )


def form_own(row_chunk, distance, word, out_ref):
    lane = lax.broadcasted_iota(jnp.int32, (8, TILE), 1)
    row = lax.broadcasted_iota(jnp.int32, (8, TILE), 0)
    splats = block_words(word, row_chunk)
    for row_block in range(2):
        for col_block in range(2):
            lanes = slice(col_block * TILE, (col_block + 1) * TILE)
            for group in range(TILE // GROUP):
                first = row_block * TILE + group * GROUP
                halves = []
                for half in range(first, first + GROUP, 8):
                    i, j = row + half, lane + col_block * TILE
                    low, high = jnp.minimum(i, j) % TILE, jnp.maximum(i, j) % TILE
                    shift = 31 - (8 * (low // 32) + high // 16)
                    seen = jnp.left_shift(splats[col_block][row_block], shift) < 0
                    value = pl.reciprocal(distance[half : half + 8, lanes], approx=True)
                    halves.append(jnp.where(seen, value, 0.0))
                out_ref[first : first + GROUP, lanes] = jnp.concatenate(halves).astype(
                    jnp.bfloat16
                )


def read_extra(rows):
    extra = rows.astype(jnp.float32)
    value = extra[12:16].astype(jnp.int32)
    word = value[0:1]
    for place in range(1, 4):
        word = jnp.bitwise_or(word, jnp.left_shift(value[place : place + 1], 8 * place))
    return extra[0:3] + extra[3:6] + extra[6:9], word


def form_all(blocks, me, row_terms, col_terms, words, fields, start, refs, finish_row):
    kernel_ref, distance = refs
    held = {}

    def measure(place):
        t, v, w = blocks[place]
        distance[place % 2] = times(row_terms[t], col_terms[v])

    def add(place):
        t, v, w = blocks[place]
        term = times_transpose(fields(v), kernel_ref[place])
        held[t] = (held[t] if t in held else start(t)) + term
        if place + 1 == len(blocks) or blocks[place + 1][0] != t:
            finish_row(t, held[t])

    measure(0)
    for place, (t, v, w) in enumerate(blocks):
        if place + 1 < len(blocks):
            measure(place + 1)
        slot, out_ref = distance.at[place % 2], kernel_ref.at[place]
        row_chunk = jnp.bitwise_xor(me, FAR * t)
        if t == 0 and v == 0 and w == 0:
            form_own(row_chunk, slot, words[v], out_ref)
        else:
            form_block(row_chunk, jnp.bitwise_xor(me, 2 * v + w), slot, words[v], out_ref)
        if place:
            add(place - 1)
    add(len(blocks) - 1)


def column_terms(rows, terms, col_terms):
    words = []
    for v in range(LINE):
        position, word = read_extra(rows(v))
        words.append(word)
        distance_terms(position, terms.at[v], False)
        col_terms[v] = terms[v].astype(jnp.bfloat16)
    return words


def grid_pack(v0_ref, v1_ref, v2_ref, v3_ref, out_ref):
    for v, ref in enumerate((v0_ref, v1_ref, v2_ref, v3_ref)):
        out_ref[v] = ref[...]


def grid_near(
    scale,
    me_ref,
    packed_ref,
    far_ref,
    seed_hbm,
    area_hbm,
    kernel_ref,
    partial_ref,
    row_terms,
    terms,
    col_terms,
    distance,
    seed_ref,
    area_ref,
    sems,
):
    copies = [
        pltpu.make_async_copy(seed_hbm, seed_ref, sems.at[0]),
        pltpu.make_async_copy(area_hbm, area_ref, sems.at[1]),
    ]
    for copy in copies:
        copy.start()
    rhs_count = seed_ref.shape[0]
    me = me_ref[0]
    words = column_terms(lambda v: packed_ref[v, rhs_count:], terms, col_terms)
    own, _ = read_extra(packed_ref[0, rhs_count:])
    for t, value in enumerate((own, far_ref[...])):
        slot = terms.at[LINE + t]
        distance_terms(value, slot, True)
        row_terms[t] = jnp.transpose(slot[...]).astype(jnp.bfloat16)

    def finish_row(t, value):
        partial_ref[t] = value

    form_all(
        NEAR,
        me,
        row_terms,
        col_terms,
        words,
        lambda v: packed_ref[v, :rhs_count],
        lambda t: 0.0,
        (kernel_ref, distance),
        finish_row,
    )
    for copy in copies:
        copy.wait()
    partial_ref[0] = partial_ref[0] + seed_ref[...] * (1.0 / (area_ref[...] * scale))


def grid_rest(
    me_ref,
    packed_ref,
    core_ref,
    before_ref,
    row_terms,
    kernel_ref,
    partial_ref,
    sent_ref,
    terms,
    col_terms,
    distance,
):
    rhs_count = before_ref.shape[1]
    words = column_terms(lambda v: core_ref[v, rhs_count:], terms, col_terms)

    def finish_row(t, value):
        partial_ref[t] = value
        sent_ref[t * rhs_count : (t + 1) * rhs_count] = value.astype(jnp.bfloat16)

    form_all(
        REST,
        me_ref[0],
        row_terms,
        col_terms,
        words,
        lambda v: core_ref[v, :rhs_count],
        lambda t: before_ref[t],
        (kernel_ref, distance),
        finish_row,
    )
    sent_ref[2 * rhs_count :] = packed_ref[0, rhs_count:]


def product(scaled_ref, kernel_ref, v):
    return times(scaled_ref[0], kernel_ref[v]) + times(scaled_ref[1], kernel_ref[LINE + v])


def grid_second(rest_ref, partial_ref, packed_ref, far_ref, scaled_ref, sent_ref):
    rhs_count = partial_ref.shape[1]
    extras = (packed_ref[0, rhs_count:], far_ref[2 * rhs_count :, :])
    for t in range(2):
        terms = extras[t].astype(jnp.float32)
        factor = terms[9:10] + terms[10:11] + terms[11:12]
        start = (1 - t) * rhs_count
        total = partial_ref[t] + far_ref[start : start + rhs_count].astype(jnp.float32)
        scaled_ref[t] = (factor * total).astype(jnp.bfloat16)
    for v in range(LINE):
        sent_ref[v] = product(scaled_ref, rest_ref, v).astype(jnp.bfloat16)


def grid_third(near_ref, scaled_ref, sum_ref):
    for v in range(LINE):
        sum_ref[v] = product(scaled_ref, near_ref, v)


def grid_fourth(sum_ref, core_ref, q0_ref, q1_ref, q2_ref, q3_ref):
    for v, ref in enumerate((q0_ref, q1_ref, q2_ref, q3_ref)):
        ref[...] = (sum_ref[v] + core_ref[v].astype(jnp.float32)).astype(ref.dtype)


def grid_last(scale, q3_ref, q2_ref, q1_ref, q0_ref, *rest):
    total = q0_ref[...]
    for ref in (q1_ref, q2_ref, q3_ref):
        total = total + ref[...].astype(jnp.float32)
    finish(scale, total, *rest)


def on_grid(adjoint_seed, radiosity, emission, reflectance, area, position, visibility):
    rhs_count, own_width = adjoint_seed.shape
    devices = GRID
    my_index = lax.axis_index("row").astype(jnp.int32).reshape(1)
    scale = 1.0 / math.sqrt(own_width * devices)
    area = area.reshape(1, own_width)
    reflectance = reflectance.reshape(1, own_width)
    smem = pl.BlockSpec(memory_space=pltpu.SMEM)
    vmem = pl.BlockSpec(memory_space=pltpu.VMEM)
    params = pltpu.CompilerParams(vmem_limit_bytes=GRID_BYTES)
    shaped = jax.ShapeDtypeStruct
    field = (rhs_count, own_width)

    def send(value, step):
        return lax.ppermute(value, "row", [(at, at ^ step) for at in range(devices)])

    hbm = pl.BlockSpec(memory_space=pltpu.HBM)
    arguments = [
        pltpu.with_memory_space_constraint(value, pltpu.HBM)
        for value in (position, visibility, area, reflectance, adjoint_seed)
    ]

    def call(body, name, operands, in_specs, out_shape, scratch_shapes=()):
        return pl.pallas_call(
            body,
            in_specs=in_specs,
            out_specs=[vmem] * len(out_shape),
            out_shape=out_shape,
            scratch_shapes=scratch_shapes,
            compiler_params=params,
            name=name,
        )(*operands)

    packed_rows = rhs_count + EXTRA
    own, spot = call(
        functools.partial(prepare, scale),
        "prepare",
        arguments,
        [hbm] * 5,
        [
            shaped((packed_rows, own_width), jnp.bfloat16),
            shaped(position.shape, jnp.float32),
        ],
        [pltpu.VMEM((EXTRA, own_width), jnp.float32)]
        + [pltpu.VMEM(value.shape, value.dtype) for value in arguments]
        + [pltpu.SemaphoreType.DMA((5,))],
    )
    lines = [send(own, 2 * v) for v in range(1, LINE)]
    far_spot = send(spot, FAR)
    first, far_spot = lax.optimization_barrier((own, far_spot))
    packed_shape = shaped((LINE, packed_rows, own_width), jnp.bfloat16)
    (packed,) = call(grid_pack, "grid_pack", (first, *lines), [vmem] * LINE, [packed_shape])
    core = send(packed, 1)
    terms = (TERMS, own_width)
    blocks = shaped((2 * LINE, own_width, own_width), jnp.bfloat16)
    pair = shaped((2,) + field, jnp.float32)
    scratch = [
        pltpu.VMEM((LINE + 2,) + terms, jnp.float32),
        pltpu.VMEM((LINE,) + terms, jnp.bfloat16),
        pltpu.VMEM((2, own_width, own_width), jnp.float32),
    ]
    near, partial, row_terms = call(
        functools.partial(grid_near, scale),
        "grid_near",
        (my_index, packed, far_spot, arguments[4], arguments[2]),
        [smem] + [vmem] * 2 + [hbm] * 2,
        [blocks, pair, shaped((2, own_width, TERMS), jnp.bfloat16)],
        scratch
        + [
            pltpu.VMEM(field, jnp.float32),
            pltpu.VMEM((1, own_width), jnp.float32),
            pltpu.SemaphoreType.DMA((2,)),
        ],
    )
    rest, partial, sent = call(
        grid_rest,
        "grid_rest",
        (my_index, packed, core, partial, row_terms),
        [smem] + [vmem] * 4,
        [blocks, pair, shaped((2 * rhs_count + EXTRA, own_width), jnp.bfloat16)],
        scratch,
    )
    four = (LINE,) + field
    scaled, sent = call(
        grid_second,
        "grid_second",
        (rest, partial, packed, send(sent, FAR)),
        [vmem] * 4,
        [shaped((2,) + field, jnp.bfloat16), shaped(four, jnp.bfloat16)],
    )
    other = send(sent, 1)
    (sums,) = call(
        grid_third, "grid_third", (near, scaled), [vmem] * 2, [shaped(four, jnp.float32)]
    )
    sums = call(
        grid_fourth,
        "grid_fourth",
        (sums, other),
        [vmem] * 2,
        [shaped(field, jnp.float32)] + [shaped(field, jnp.bfloat16)] * 3,
    )
    lines = [send(sums[v], 2 * v) for v in range(1, LINE)]
    adjoint, grad = call(
        functools.partial(grid_last, scale),
        "grid_last",
        (*lines[::-1], sums[0], adjoint_seed, area, reflectance, radiosity, emission),
        [vmem] * 9,
        [shaped(field, jnp.float32), shaped((1, own_width), jnp.float32)],
    )
    return adjoint, grad.reshape(own_width)


def spread_rows(pos_ref, spread):
    for coord in range(3):
        for block in range(spread.shape[1]):
            line = pos_ref[coord : coord + 1, block * TILE : (block + 1) * TILE]
            spread[coord, block] = jnp.transpose(jnp.broadcast_to(line, (TILE, TILE)))


def inverse_square(spread, pos_ref, at, own_block, rows, other_block):
    lanes = pl.ds(other_block * TILE, TILE)
    total = 1.0
    for coord in range(3):
        delta = spread[coord, own_block, rows, :] - pos_ref[at, coord : coord + 1, lanes]
        total = total + delta * delta
    return 1.0 / total


def form_part(me, at, part, words_ref, pos_ref, spread, kernel_ref):
    blocks = spread.shape[1]
    lane = lax.broadcasted_iota(jnp.int32, (GROUP, TILE), 1)
    for own_block in range(blocks):
        row_block = me * blocks + own_block
        for other_block in range(blocks):
            col_block = part * blocks + other_block
            word = words_ref[own_block, col_block]
            direct = row_block < col_block
            for group in range(TILE // GROUP):
                rows = slice(group * GROUP, (group + 1) * GROUP)
                bit = jnp.where(direct, 8 * (group // 2) + lane // 16, 8 * (lane // 32) + group)
                seen = (jnp.right_shift(word, bit) & 1) != 0
                value = inverse_square(spread, pos_ref, at, own_block, rows, other_block)
                value = jnp.where(seen, value, 0.0).astype(jnp.bfloat16)
                kernel_ref[
                    at,
                    own_block * TILE + group * GROUP : own_block * TILE + (group + 1) * GROUP,
                    other_block * TILE : (other_block + 1) * TILE,
                ] = value


def form_diagonal(me, at, words_ref, pos_ref, spread, kernel_ref):
    blocks = spread.shape[1]
    lane = lax.broadcasted_iota(jnp.int32, (TILE, TILE), 1)
    row = lax.broadcasted_iota(jnp.int32, (TILE, TILE), 0)
    low, high = jnp.minimum(row, lane), jnp.maximum(row, lane)
    bit = 8 * (low // 32) + high // 16
    for block in range(blocks):
        word = words_ref[block, me * blocks + block]
        seen = (jnp.right_shift(word, bit) & 1) != 0
        value = inverse_square(spread, pos_ref, at, block, slice(0, TILE), block)
        value = jnp.where(seen, value, 0.0).astype(jnp.bfloat16)
        kernel_ref[
            at, block * TILE : (block + 1) * TILE, block * TILE : (block + 1) * TILE
        ] = value


def gather_sum(every_ref, kernel_ref):
    total = times_transpose(every_ref[0], kernel_ref[0])
    for at in range(1, every_ref.shape[0]):
        total += times_transpose(every_ref[at], kernel_ref[at])
    return total


def first_sweep(
    scale,
    me_ref,
    words_ref,
    own_pos_ref,
    pos_ref,
    every_ref,
    seed_ref,
    area_ref,
    reflectance_ref,
    kernel_ref,
    scaled_ref,
    spread,
    total,
):
    step = pl.program_id(0)
    chunk = pos_ref.shape[0]
    me = me_ref[0]

    @pl.when(step == 0)
    def _():
        spread_rows(own_pos_ref, spread)
        total[...] = jnp.zeros_like(total)

    def form(at, carry):
        form_part(me, at, step * chunk + at, words_ref, pos_ref, spread, kernel_ref)
        return carry

    lax.fori_loop(0, chunk, form, 0)

    @pl.when((me >= step * chunk) & (me < (step + 1) * chunk))
    def _():
        form_diagonal(me, me - step * chunk, words_ref, pos_ref, spread, kernel_ref)

    total[...] += gather_sum(every_ref, kernel_ref)

    @pl.when(step == pl.num_programs(0) - 1)
    def _():
        adjoint = seed_ref[...] + (area_ref[...] * scale) * total[...]
        scaled_ref[...] = (reflectance_ref[...] * adjoint).astype(jnp.bfloat16)


def last_sweep(
    scale,
    kernel_ref,
    every_ref,
    seed_ref,
    area_ref,
    reflectance_ref,
    radiosity_ref,
    emission_ref,
    adjoint_ref,
    grad_ref,
    total,
):
    step = pl.program_id(0)

    @pl.when(step == 0)
    def _():
        total[...] = jnp.zeros_like(total)

    total[...] += gather_sum(every_ref, kernel_ref)

    @pl.when(step == pl.num_programs(0) - 1)
    def _():
        finish(
            scale,
            total[...],
            seed_ref,
            area_ref,
            reflectance_ref,
            radiosity_ref,
            emission_ref,
            adjoint_ref,
            grad_ref,
        )


def whole(shape):
    return pl.BlockSpec(shape, lambda step: (0,) * len(shape))


def parts(chunk, shape):
    return pl.BlockSpec((chunk,) + shape, lambda step: (step,) + (0,) * len(shape))


def on_rows(adjoint_seed, radiosity, emission, reflectance, area, position, visibility):
    rhs_count, own_width = adjoint_seed.shape
    devices = lax.axis_size("row")
    my_index = lax.axis_index("row").astype(jnp.int32).reshape(1)
    local_blocks = own_width // TILE
    scale = 1.0 / math.sqrt(own_width * devices)
    chunk = math.gcd(devices, 16)
    area = area.reshape(1, own_width)
    reflectance = reflectance.reshape(1, own_width)
    smem = pl.BlockSpec(memory_space=pltpu.SMEM)
    params = pltpu.CompilerParams(
        dimension_semantics=("arbitrary",), vmem_limit_bytes=VMEM_BYTES
    )

    all_pos = lax.all_gather(position, "row")
    every = lax.all_gather((reflectance * adjoint_seed).astype(jnp.bfloat16), "row")
    kernel, scaled = pl.pallas_call(
        functools.partial(first_sweep, scale),
        grid=(devices // chunk,),
        in_specs=[
            smem,
            smem,
            whole((3, own_width)),
            parts(chunk, (3, own_width)),
            parts(chunk, (rhs_count, own_width)),
            whole((rhs_count, own_width)),
            whole((1, own_width)),
            whole((1, own_width)),
        ],
        out_specs=[parts(chunk, (own_width, own_width)), whole((rhs_count, own_width))],
        out_shape=[
            jax.ShapeDtypeStruct((devices, own_width, own_width), jnp.bfloat16),
            jax.ShapeDtypeStruct((rhs_count, own_width), jnp.bfloat16),
        ],
        scratch_shapes=[
            pltpu.VMEM((3, local_blocks, TILE, TILE), jnp.float32),
            pltpu.VMEM((rhs_count, own_width), jnp.float32),
        ],
        compiler_params=params,
        name="first_sweep",
    )(my_index, visibility, position, all_pos, every, adjoint_seed, area, reflectance)

    every = lax.all_gather(scaled, "row")
    adjoint, grad = pl.pallas_call(
        functools.partial(last_sweep, scale),
        grid=(devices // chunk,),
        in_specs=[
            parts(chunk, (own_width, own_width)),
            parts(chunk, (rhs_count, own_width)),
            whole((rhs_count, own_width)),
            whole((1, own_width)),
            whole((1, own_width)),
            whole((rhs_count, own_width)),
            whole((rhs_count, own_width)),
        ],
        out_specs=[whole((rhs_count, own_width)), whole((1, own_width))],
        out_shape=[
            jax.ShapeDtypeStruct((rhs_count, own_width), jnp.float32),
            jax.ShapeDtypeStruct((1, own_width), jnp.float32),
        ],
        scratch_shapes=[pltpu.VMEM((rhs_count, own_width), jnp.float32)],
        compiler_params=params,
        name="last_sweep",
    )(kernel, every, adjoint_seed, area, reflectance, radiosity, emission)
    return adjoint, grad.reshape(own_width)


def on_device(adjoint_seed, *rest):
    on_grid_shape = lax.axis_size("row") == GRID and adjoint_seed.shape[1] == 2 * TILE
    return (on_grid if on_grid_shape else on_rows)(adjoint_seed, *rest)


def solution(mesh):
    placed = (
        P(None, ("scene", "row")),
        P(None, ("scene", "row")),
        P(None, ("scene", "row")),
        P(("scene", "row")),
        P(("scene", "row")),
        P(None, ("scene", "row")),
        P(("scene", "row"), None),
    )
    return jax.shard_map(
        on_device,
        mesh=mesh,
        in_specs=placed,
        out_specs=(P(None, ("scene", "row")), P(("scene", "row"))),
        check_vma=False,
    )
```

```python
import functools
import math

import jax
import jax.numpy as jnp
from jax import lax
from jax.experimental import pallas as pl
from jax.experimental.pallas import tpu as pltpu
from jax.sharding import PartitionSpec as P

TILE = 128
SWEEPS = 2
GROUP = 16
LINE = 4
GRID = 16
FAR = 8
EXTRA = 16
TERMS = 32
LONG = pl.CostEstimate(flops=10**11, bytes_accessed=10**8, transcendentals=0)
VMEM_BYTES = 48 * 1024 * 1024
GRID_BYTES = 8 * 1024 * 1024


NEAR = [(t, v, 0) for t in range(2) for v in range(LINE)]
REST = [(t, v, 1) for t in range(2) for v in range(LINE)]


def three_terms(value):
    high = value.astype(jnp.bfloat16).astype(jnp.float32)
    rest = value - high
    middle = rest.astype(jnp.bfloat16).astype(jnp.float32)
    return high, middle, rest - middle


def times_transpose(values, kernel):
    return lax.dot_general(
        values, kernel, (((1,), (1,)), ((), ())), preferred_element_type=jnp.float32
    )


def times(values, kernel):
    return jnp.dot(values, kernel, preferred_element_type=jnp.float32)


def finish(
    scale, total, seed_ref, area_ref, reflectance_ref, radiosity_ref, emission_ref, adjoint_ref, grad_ref
):
    adjoint = seed_ref[...] + (area_ref[...] * scale) * total
    adjoint_ref[...] = adjoint
    change = radiosity_ref[...].astype(jnp.float32) - emission_ref[...].astype(jnp.float32)
    grad_ref[...] = jnp.sum(adjoint * change, axis=0, keepdims=True) / reflectance_ref[...]


def prepare(scale, *refs):
    arguments, (packed_ref, rows, *held, sems) = refs[:5], refs[5:]
    copies = [
        pltpu.make_async_copy(argument, ref, sems.at[at])
        for at, (argument, ref) in enumerate(zip(arguments, held))
    ]
    for copy in copies:
        copy.start()
    rows[...] = jnp.zeros_like(rows)
    for copy in copies:
        copy.wait()
    pos_ref, words_ref, area_ref, reflectance_ref, seed_ref = held
    rhs_count = seed_ref.shape[0]
    for term, value in enumerate(three_terms(pos_ref[...])):
        rows[3 * term : 3 * term + 3, :] = value
    weight = area_ref[...] * scale
    for term, value in enumerate(three_terms(weight * reflectance_ref[...])):
        rows[9 + term : 10 + term, :] = value
    count = words_ref.shape[1]
    for place in range(4):
        part = (jnp.right_shift(words_ref[...], 8 * place) & 255).astype(jnp.float32)
        for local in range(words_ref.shape[0]):
            start = local * TILE
            rows[12 + place : 13 + place, start : start + count] = part[local : local + 1]
    packed_ref[:rhs_count] = (reflectance_ref[...] * seed_ref[...]).astype(jnp.bfloat16)
    packed_ref[rhs_count:] = rows[...].astype(jnp.bfloat16)


def distance_terms(position, terms, as_rows):
    high, middle, low = three_terms(position)
    norm = jnp.sum(position * position, axis=0, keepdims=True)
    terms[...] = jnp.zeros_like(terms)
    if as_rows:
        for at, value in enumerate((high, high, high, middle, middle, low)):
            terms[3 * at : 3 * at + 3, :] = -2.0 * value
        ones, norms, norm = 21, 18, norm + 1.0
    else:
        for at, value in enumerate((high, middle, low, high, middle, high)):
            terms[3 * at : 3 * at + 3, :] = value
        ones, norms = 18, 21
    terms[ones : ones + 3, :] = jnp.ones_like(high)
    for at, value in enumerate(three_terms(norm)):
        terms[norms + at : norms + at + 1, :] = value


def shift_up(direct, group, lane):
    return 31 - jnp.where(direct, 8 * (group // 2) + lane // 16, 8 * (lane // 32) + group)


def block_words(word, row_chunk):
    splats = []
    for col_block in range(2):
        lanes = jnp.broadcast_to(word[:, col_block * TILE : (col_block + 1) * TILE], (8, TILE))
        lanes = pltpu.roll(lanes, TILE - 2 * row_chunk, 1)
        splats.append(
            [jnp.broadcast_to(lanes[:, at : at + 1], (8, TILE)) for at in range(2)]
        )
    return splats


def form_block(row_chunk, col_chunk, distance, word, out_ref):
    lane = lax.broadcasted_iota(jnp.int32, (8, TILE), 1)
    direct = row_chunk < col_chunk
    shifts = [shift_up(direct, group, lane) for group in range(TILE // GROUP)]
    splats = block_words(word, row_chunk)
    for row_block in range(2):
        for col_block in range(2):
            lanes = slice(col_block * TILE, (col_block + 1) * TILE)
            for group, shift in enumerate(shifts):
                first = row_block * TILE + group * GROUP
                seen = jnp.left_shift(splats[col_block][row_block], shift) < 0
                halves = []
                for half in range(first, first + GROUP, 8):
                    value = pl.reciprocal(distance[half : half + 8, lanes], approx=True)
                    halves.append(jnp.where(seen, value, 0.0))
                out_ref[first : first + GROUP, lanes] = jnp.concatenate(halves).astype(
                    jnp.bfloat16
                )


def form_own(row_chunk, distance, word, out_ref):
    lane = lax.broadcasted_iota(jnp.int32, (8, TILE), 1)
    row = lax.broadcasted_iota(jnp.int32, (8, TILE), 0)
    splats = block_words(word, row_chunk)
    for row_block in range(2):
        for col_block in range(2):
            lanes = slice(col_block * TILE, (col_block + 1) * TILE)
            for group in range(TILE // GROUP):
                first = row_block * TILE + group * GROUP
                halves = []
                for half in range(first, first + GROUP, 8):
                    i, j = row + half, lane + col_block * TILE
                    low, high = jnp.minimum(i, j) % TILE, jnp.maximum(i, j) % TILE
                    shift = 31 - (8 * (low // 32) + high // 16)
                    seen = jnp.left_shift(splats[col_block][row_block], shift) < 0
                    value = pl.reciprocal(distance[half : half + 8, lanes], approx=True)
                    halves.append(jnp.where(seen, value, 0.0))
                out_ref[first : first + GROUP, lanes] = jnp.concatenate(halves).astype(
                    jnp.bfloat16
                )


def read_extra(rows):
    extra = rows.astype(jnp.float32)
    value = extra[12:16].astype(jnp.int32)
    word = value[0:1]
    for place in range(1, 4):
        word = jnp.bitwise_or(word, jnp.left_shift(value[place : place + 1], 8 * place))
    return extra[0:3] + extra[3:6] + extra[6:9], word


def form_all(blocks, me, row_terms, col_terms, words, fields, start, refs, finish_row):
    kernel_ref, distance = refs
    held = {}

    def measure(place):
        t, v, w = blocks[place]
        distance[place % 2] = times(row_terms[t], col_terms[v])

    def add(place):
        t, v, w = blocks[place]
        term = times_transpose(fields(v), kernel_ref[place])
        held[t] = (held[t] if t in held else start(t)) + term
        if place + 1 == len(blocks) or blocks[place + 1][0] != t:
            finish_row(t, held[t])

    measure(0)
    for place, (t, v, w) in enumerate(blocks):
        if place + 1 < len(blocks):
            measure(place + 1)
        slot, out_ref = distance.at[place % 2], kernel_ref.at[place]
        row_chunk = jnp.bitwise_xor(me, FAR * t)
        if t == 0 and v == 0 and w == 0:
            form_own(row_chunk, slot, words[v], out_ref)
        else:
            form_block(row_chunk, jnp.bitwise_xor(me, 2 * v + w), slot, words[v], out_ref)
        if place:
            add(place - 1)
    add(len(blocks) - 1)


def column_terms(rows, terms, col_terms):
    words = []
    for v in range(LINE):
        position, word = read_extra(rows(v))
        words.append(word)
        distance_terms(position, terms.at[v], False)
        col_terms[v] = terms[v].astype(jnp.bfloat16)
    return words


def grid_rows(own_ref, far_ref, row_terms, terms):
    own, _ = read_extra(own_ref[-EXTRA:, :])
    for t, value in enumerate((own, far_ref[...])):
        distance_terms(value, terms.at[t], True)
        row_terms[t] = jnp.transpose(terms[t]).astype(jnp.bfloat16)


def grid_pack(v0_ref, v1_ref, v2_ref, v3_ref, out_ref):
    for v, ref in enumerate((v0_ref, v1_ref, v2_ref, v3_ref)):
        out_ref[v] = ref[...]


def grid_near(
    scale,
    me_ref,
    packed_ref,
    row_terms,
    seed_hbm,
    area_hbm,
    kernel_ref,
    partial_ref,
    terms,
    col_terms,
    distance,
    seed_ref,
    area_ref,
    sems,
):
    copies = [
        pltpu.make_async_copy(seed_hbm, seed_ref, sems.at[0]),
        pltpu.make_async_copy(area_hbm, area_ref, sems.at[1]),
    ]
    for copy in copies:
        copy.start()
    rhs_count = seed_ref.shape[0]
    me = me_ref[0]
    words = column_terms(lambda v: packed_ref[v, rhs_count:], terms, col_terms)

    def finish_row(t, value):
        partial_ref[t] = value

    form_all(
        NEAR,
        me,
        row_terms,
        col_terms,
        words,
        lambda v: packed_ref[v, :rhs_count],
        lambda t: 0.0,
        (kernel_ref, distance),
        finish_row,
    )
    for copy in copies:
        copy.wait()
    partial_ref[0] = partial_ref[0] + seed_ref[...] * (1.0 / (area_ref[...] * scale))


def grid_rest(
    me_ref,
    packed_ref,
    core_ref,
    before_ref,
    row_terms,
    kernel_ref,
    partial_ref,
    sent_ref,
    terms,
    col_terms,
    distance,
):
    rhs_count = before_ref.shape[1]
    words = column_terms(lambda v: core_ref[v, rhs_count:], terms, col_terms)

    def finish_row(t, value):
        partial_ref[t] = value
        sent_ref[t * rhs_count : (t + 1) * rhs_count] = value.astype(jnp.bfloat16)

    form_all(
        REST,
        me_ref[0],
        row_terms,
        col_terms,
        words,
        lambda v: core_ref[v, :rhs_count],
        lambda t: before_ref[t],
        (kernel_ref, distance),
        finish_row,
    )
    sent_ref[2 * rhs_count :] = packed_ref[0, rhs_count:]


def product(scaled_ref, kernel_ref, v):
    return times(scaled_ref[0], kernel_ref[v]) + times(scaled_ref[1], kernel_ref[LINE + v])


def grid_second(rest_ref, partial_ref, packed_ref, far_ref, scaled_ref, sent_ref):
    rhs_count = partial_ref.shape[1]
    extras = (packed_ref[0, rhs_count:], far_ref[2 * rhs_count :, :])
    for t in range(2):
        terms = extras[t].astype(jnp.float32)
        factor = terms[9:10] + terms[10:11] + terms[11:12]
        start = (1 - t) * rhs_count
        total = partial_ref[t] + far_ref[start : start + rhs_count].astype(jnp.float32)
        scaled_ref[t] = (factor * total).astype(jnp.bfloat16)
    for v in range(LINE):
        sent_ref[v] = product(scaled_ref, rest_ref, v).astype(jnp.bfloat16)


def grid_third(near_ref, scaled_ref, sum_ref):
    for v in range(LINE):
        sum_ref[v] = product(scaled_ref, near_ref, v)


def grid_fourth(sum_ref, core_ref, q0_ref, q1_ref, q2_ref, q3_ref):
    for v, ref in enumerate((q0_ref, q1_ref, q2_ref, q3_ref)):
        ref[...] = (sum_ref[v] + core_ref[v].astype(jnp.float32)).astype(ref.dtype)


def grid_last(scale, q3_ref, q2_ref, q1_ref, q0_ref, *rest):
    total = q0_ref[...]
    for ref in (q1_ref, q2_ref, q3_ref):
        total = total + ref[...].astype(jnp.float32)
    finish(scale, total, *rest)


def on_grid(adjoint_seed, radiosity, emission, reflectance, area, position, visibility):
    rhs_count, own_width = adjoint_seed.shape
    devices = GRID
    my_index = lax.axis_index("row").astype(jnp.int32).reshape(1)
    scale = 1.0 / math.sqrt(own_width * devices)
    area = area.reshape(1, own_width)
    reflectance = reflectance.reshape(1, own_width)
    smem = pl.BlockSpec(memory_space=pltpu.SMEM)
    vmem = pl.BlockSpec(memory_space=pltpu.VMEM)
    params = pltpu.CompilerParams(vmem_limit_bytes=GRID_BYTES)
    shaped = jax.ShapeDtypeStruct
    field = (rhs_count, own_width)

    def send(value, step):
        return lax.ppermute(value, "row", [(at, at ^ step) for at in range(devices)])

    hbm = pl.BlockSpec(memory_space=pltpu.HBM)
    arguments = [
        pltpu.with_memory_space_constraint(value, pltpu.HBM)
        for value in (position, visibility, area, reflectance, adjoint_seed)
    ]

    def call(body, name, operands, in_specs, out_shape, scratch_shapes=(), cost=None):
        return pl.pallas_call(
            body,
            in_specs=in_specs,
            out_specs=[vmem] * len(out_shape),
            out_shape=out_shape,
            scratch_shapes=scratch_shapes,
            compiler_params=params,
            cost_estimate=cost,
            name=name,
        )(*operands)

    packed_rows = rhs_count + EXTRA
    (own,) = call(
        functools.partial(prepare, scale),
        "prepare",
        arguments,
        [hbm] * 5,
        [shaped((packed_rows, own_width), jnp.bfloat16)],
        [pltpu.VMEM((EXTRA, own_width), jnp.float32)]
        + [pltpu.VMEM(value.shape, value.dtype) for value in arguments]
        + [pltpu.SemaphoreType.DMA((5,))],
    )
    lines = [send(own, 2 * v) for v in range(1, LINE)]
    terms = (TERMS, own_width)
    (row_terms,) = call(
        grid_rows,
        "grid_rows",
        (own, send(position, FAR)),
        [vmem] * 2,
        [shaped((2, own_width, TERMS), jnp.bfloat16)],
        [pltpu.VMEM((2,) + terms, jnp.float32)],
        LONG,
    )
    first, row_terms = lax.optimization_barrier((own, row_terms))
    packed_shape = shaped((LINE, packed_rows, own_width), jnp.bfloat16)
    (packed,) = call(grid_pack, "grid_pack", (first, *lines), [vmem] * LINE, [packed_shape])
    core = send(packed, 1)
    blocks = shaped((2 * LINE, own_width, own_width), jnp.bfloat16)
    pair = shaped((2,) + field, jnp.float32)
    scratch = [
        pltpu.VMEM((LINE,) + terms, jnp.float32),
        pltpu.VMEM((LINE,) + terms, jnp.bfloat16),
        pltpu.VMEM((2, own_width, own_width), jnp.float32),
    ]
    near, partial = call(
        functools.partial(grid_near, scale),
        "grid_near",
        (my_index, packed, row_terms, arguments[4], arguments[2]),
        [smem] + [vmem] * 2 + [hbm] * 2,
        [blocks, pair],
        scratch
        + [
            pltpu.VMEM(field, jnp.float32),
            pltpu.VMEM((1, own_width), jnp.float32),
            pltpu.SemaphoreType.DMA((2,)),
        ],
    )
    rest, partial, sent = call(
        grid_rest,
        "grid_rest",
        (my_index, packed, core, partial, row_terms),
        [smem] + [vmem] * 4,
        [blocks, pair, shaped((2 * rhs_count + EXTRA, own_width), jnp.bfloat16)],
        scratch,
    )
    four = (LINE,) + field
    scaled, sent = call(
        grid_second,
        "grid_second",
        (rest, partial, packed, send(sent, FAR)),
        [vmem] * 4,
        [shaped((2,) + field, jnp.bfloat16), shaped(four, jnp.bfloat16)],
    )
    other = send(sent, 1)
    (sums,) = call(
        grid_third, "grid_third", (near, scaled), [vmem] * 2, [shaped(four, jnp.float32)]
    )
    sums = call(
        grid_fourth,
        "grid_fourth",
        (sums, other),
        [vmem] * 2,
        [shaped(field, jnp.float32)] + [shaped(field, jnp.bfloat16)] * 3,
    )
    lines = [send(sums[v], 2 * v) for v in range(1, LINE)]
    adjoint, grad = call(
        functools.partial(grid_last, scale),
        "grid_last",
        (*lines[::-1], sums[0], adjoint_seed, area, reflectance, radiosity, emission),
        [vmem] * 9,
        [shaped(field, jnp.float32), shaped((1, own_width), jnp.float32)],
    )
    return adjoint, grad.reshape(own_width)


def spread_rows(pos_ref, spread):
    for coord in range(3):
        for block in range(spread.shape[1]):
            line = pos_ref[coord : coord + 1, block * TILE : (block + 1) * TILE]
            spread[coord, block] = jnp.transpose(jnp.broadcast_to(line, (TILE, TILE)))


def inverse_square(spread, pos_ref, at, own_block, rows, other_block):
    lanes = pl.ds(other_block * TILE, TILE)
    total = 1.0
    for coord in range(3):
        delta = spread[coord, own_block, rows, :] - pos_ref[at, coord : coord + 1, lanes]
        total = total + delta * delta
    return 1.0 / total


def form_part(me, at, part, words_ref, pos_ref, spread, kernel_ref):
    blocks = spread.shape[1]
    lane = lax.broadcasted_iota(jnp.int32, (GROUP, TILE), 1)
    for own_block in range(blocks):
        row_block = me * blocks + own_block
        for other_block in range(blocks):
            col_block = part * blocks + other_block
            word = words_ref[own_block, col_block]
            direct = row_block < col_block
            for group in range(TILE // GROUP):
                rows = slice(group * GROUP, (group + 1) * GROUP)
                bit = jnp.where(direct, 8 * (group // 2) + lane // 16, 8 * (lane // 32) + group)
                seen = (jnp.right_shift(word, bit) & 1) != 0
                value = inverse_square(spread, pos_ref, at, own_block, rows, other_block)
                value = jnp.where(seen, value, 0.0).astype(jnp.bfloat16)
                kernel_ref[
                    at,
                    own_block * TILE + group * GROUP : own_block * TILE + (group + 1) * GROUP,
                    other_block * TILE : (other_block + 1) * TILE,
                ] = value


def form_diagonal(me, at, words_ref, pos_ref, spread, kernel_ref):
    blocks = spread.shape[1]
    lane = lax.broadcasted_iota(jnp.int32, (TILE, TILE), 1)
    row = lax.broadcasted_iota(jnp.int32, (TILE, TILE), 0)
    low, high = jnp.minimum(row, lane), jnp.maximum(row, lane)
    bit = 8 * (low // 32) + high // 16
    for block in range(blocks):
        word = words_ref[block, me * blocks + block]
        seen = (jnp.right_shift(word, bit) & 1) != 0
        value = inverse_square(spread, pos_ref, at, block, slice(0, TILE), block)
        value = jnp.where(seen, value, 0.0).astype(jnp.bfloat16)
        kernel_ref[
            at, block * TILE : (block + 1) * TILE, block * TILE : (block + 1) * TILE
        ] = value


def gather_sum(every_ref, kernel_ref):
    total = times_transpose(every_ref[0], kernel_ref[0])
    for at in range(1, every_ref.shape[0]):
        total += times_transpose(every_ref[at], kernel_ref[at])
    return total


def first_sweep(
    scale,
    me_ref,
    words_ref,
    own_pos_ref,
    pos_ref,
    every_ref,
    seed_ref,
    area_ref,
    reflectance_ref,
    kernel_ref,
    scaled_ref,
    spread,
    total,
):
    step = pl.program_id(0)
    chunk = pos_ref.shape[0]
    me = me_ref[0]

    @pl.when(step == 0)
    def _():
        spread_rows(own_pos_ref, spread)
        total[...] = jnp.zeros_like(total)

    def form(at, carry):
        form_part(me, at, step * chunk + at, words_ref, pos_ref, spread, kernel_ref)
        return carry

    lax.fori_loop(0, chunk, form, 0)

    @pl.when((me >= step * chunk) & (me < (step + 1) * chunk))
    def _():
        form_diagonal(me, me - step * chunk, words_ref, pos_ref, spread, kernel_ref)

    total[...] += gather_sum(every_ref, kernel_ref)

    @pl.when(step == pl.num_programs(0) - 1)
    def _():
        adjoint = seed_ref[...] + (area_ref[...] * scale) * total[...]
        scaled_ref[...] = (reflectance_ref[...] * adjoint).astype(jnp.bfloat16)


def last_sweep(
    scale,
    kernel_ref,
    every_ref,
    seed_ref,
    area_ref,
    reflectance_ref,
    radiosity_ref,
    emission_ref,
    adjoint_ref,
    grad_ref,
    total,
):
    step = pl.program_id(0)

    @pl.when(step == 0)
    def _():
        total[...] = jnp.zeros_like(total)

    total[...] += gather_sum(every_ref, kernel_ref)

    @pl.when(step == pl.num_programs(0) - 1)
    def _():
        finish(
            scale,
            total[...],
            seed_ref,
            area_ref,
            reflectance_ref,
            radiosity_ref,
            emission_ref,
            adjoint_ref,
            grad_ref,
        )


def whole(shape):
    return pl.BlockSpec(shape, lambda step: (0,) * len(shape))


def parts(chunk, shape):
    return pl.BlockSpec((chunk,) + shape, lambda step: (step,) + (0,) * len(shape))


def on_rows(adjoint_seed, radiosity, emission, reflectance, area, position, visibility):
    rhs_count, own_width = adjoint_seed.shape
    devices = lax.axis_size("row")
    my_index = lax.axis_index("row").astype(jnp.int32).reshape(1)
    local_blocks = own_width // TILE
    scale = 1.0 / math.sqrt(own_width * devices)
    chunk = math.gcd(devices, 16)
    area = area.reshape(1, own_width)
    reflectance = reflectance.reshape(1, own_width)
    smem = pl.BlockSpec(memory_space=pltpu.SMEM)
    params = pltpu.CompilerParams(
        dimension_semantics=("arbitrary",), vmem_limit_bytes=VMEM_BYTES
    )

    all_pos = lax.all_gather(position, "row")
    every = lax.all_gather((reflectance * adjoint_seed).astype(jnp.bfloat16), "row")
    kernel, scaled = pl.pallas_call(
        functools.partial(first_sweep, scale),
        grid=(devices // chunk,),
        in_specs=[
            smem,
            smem,
            whole((3, own_width)),
            parts(chunk, (3, own_width)),
            parts(chunk, (rhs_count, own_width)),
            whole((rhs_count, own_width)),
            whole((1, own_width)),
            whole((1, own_width)),
        ],
        out_specs=[parts(chunk, (own_width, own_width)), whole((rhs_count, own_width))],
        out_shape=[
            jax.ShapeDtypeStruct((devices, own_width, own_width), jnp.bfloat16),
            jax.ShapeDtypeStruct((rhs_count, own_width), jnp.bfloat16),
        ],
        scratch_shapes=[
            pltpu.VMEM((3, local_blocks, TILE, TILE), jnp.float32),
            pltpu.VMEM((rhs_count, own_width), jnp.float32),
        ],
        compiler_params=params,
        name="first_sweep",
    )(my_index, visibility, position, all_pos, every, adjoint_seed, area, reflectance)

    every = lax.all_gather(scaled, "row")
    adjoint, grad = pl.pallas_call(
        functools.partial(last_sweep, scale),
        grid=(devices // chunk,),
        in_specs=[
            parts(chunk, (own_width, own_width)),
            parts(chunk, (rhs_count, own_width)),
            whole((rhs_count, own_width)),
            whole((1, own_width)),
            whole((1, own_width)),
            whole((rhs_count, own_width)),
            whole((rhs_count, own_width)),
        ],
        out_specs=[whole((rhs_count, own_width)), whole((1, own_width))],
        out_shape=[
            jax.ShapeDtypeStruct((rhs_count, own_width), jnp.float32),
            jax.ShapeDtypeStruct((1, own_width), jnp.float32),
        ],
        scratch_shapes=[pltpu.VMEM((rhs_count, own_width), jnp.float32)],
        compiler_params=params,
        name="last_sweep",
    )(kernel, every, adjoint_seed, area, reflectance, radiosity, emission)
    return adjoint, grad.reshape(own_width)


def on_device(adjoint_seed, *rest):
    on_grid_shape = lax.axis_size("row") == GRID and adjoint_seed.shape[1] == 2 * TILE
    return (on_grid if on_grid_shape else on_rows)(adjoint_seed, *rest)


def solution(mesh):
    placed = (
        P(None, ("scene", "row")),
        P(None, ("scene", "row")),
        P(None, ("scene", "row")),
        P(("scene", "row")),
        P(("scene", "row")),
        P(None, ("scene", "row")),
        P(("scene", "row"), None),
    )
    return jax.shard_map(
        on_device,
        mesh=mesh,
        in_specs=placed,
        out_specs=(P(None, ("scene", "row")), P(("scene", "row"))),
        check_vma=False,
    )
```

```python
import functools
import math

import jax
import jax.numpy as jnp
from jax import lax
from jax.experimental import pallas as pl
from jax.experimental.pallas import tpu as pltpu
from jax.sharding import PartitionSpec as P

TILE = 128
SWEEPS = 2
GROUP = 16
LINE = 4
GRID = 16
STEP = 4
FAR = 2
EXTRA = 16
TERMS = 32
VMEM_BYTES = 48 * 1024 * 1024
GRID_BYTES = 8 * 1024 * 1024


NEAR = [(t, v, 0) for t in range(2) for v in range(LINE)]
REST = [(t, v, 1) for t in range(2) for v in range(LINE)]


def three_terms(value):
    high = value.astype(jnp.bfloat16).astype(jnp.float32)
    rest = value - high
    middle = rest.astype(jnp.bfloat16).astype(jnp.float32)
    return high, middle, rest - middle


def times_transpose(values, kernel):
    return lax.dot_general(
        values, kernel, (((1,), (1,)), ((), ())), preferred_element_type=jnp.float32
    )


def times(values, kernel):
    return jnp.dot(values, kernel, preferred_element_type=jnp.float32)


def finish(
    scale, total, seed_ref, area_ref, reflectance_ref, radiosity_ref, emission_ref, adjoint_ref, grad_ref
):
    adjoint = seed_ref[...] + (area_ref[...] * scale) * total
    adjoint_ref[...] = adjoint
    change = radiosity_ref[...].astype(jnp.float32) - emission_ref[...].astype(jnp.float32)
    grad_ref[...] = jnp.sum(adjoint * change, axis=0, keepdims=True) / reflectance_ref[...]


def prepare(scale, *refs):
    arguments, (packed_ref, spot_ref, rows, *held, sems) = refs[:5], refs[5:]
    copies = [
        pltpu.make_async_copy(argument, ref, sems.at[at])
        for at, (argument, ref) in enumerate(zip(arguments, held))
    ]
    for copy in copies:
        copy.start()
    rows[...] = jnp.zeros_like(rows)
    for copy in copies:
        copy.wait()
    pos_ref, words_ref, area_ref, reflectance_ref, seed_ref = held
    rhs_count = seed_ref.shape[0]
    for term, value in enumerate(three_terms(pos_ref[...])):
        rows[3 * term : 3 * term + 3, :] = value
    weight = area_ref[...] * scale
    for term, value in enumerate(three_terms(weight * reflectance_ref[...])):
        rows[9 + term : 10 + term, :] = value
    count = words_ref.shape[1]
    for place in range(4):
        part = (jnp.right_shift(words_ref[...], 8 * place) & 255).astype(jnp.float32)
        for local in range(words_ref.shape[0]):
            start = local * TILE
            rows[12 + place : 13 + place, start : start + count] = part[local : local + 1]
    packed_ref[:rhs_count] = (reflectance_ref[...] * seed_ref[...]).astype(jnp.bfloat16)
    packed_ref[rhs_count:] = rows[...].astype(jnp.bfloat16)
    spot_ref[...] = pos_ref[...]


def distance_terms(position, terms, as_rows):
    high, middle, low = three_terms(position)
    norm = jnp.sum(position * position, axis=0, keepdims=True)
    terms[...] = jnp.zeros_like(terms)
    if as_rows:
        for at, value in enumerate((high, high, high, middle, middle, low)):
            terms[3 * at : 3 * at + 3, :] = -2.0 * value
        ones, norms, norm = 21, 18, norm + 1.0
    else:
        for at, value in enumerate((high, middle, low, high, middle, high)):
            terms[3 * at : 3 * at + 3, :] = value
        ones, norms = 18, 21
    terms[ones : ones + 3, :] = jnp.ones_like(high)
    for at, value in enumerate(three_terms(norm)):
        terms[norms + at : norms + at + 1, :] = value


def shift_up(direct, group, lane):
    return 31 - jnp.where(direct, 8 * (group // 2) + lane // 16, 8 * (lane // 32) + group)


def block_words(word, row_chunk):
    splats = []
    for col_block in range(2):
        lanes = jnp.broadcast_to(word[:, col_block * TILE : (col_block + 1) * TILE], (8, TILE))
        lanes = pltpu.roll(lanes, TILE - 2 * row_chunk, 1)
        splats.append(
            [jnp.broadcast_to(lanes[:, at : at + 1], (8, TILE)) for at in range(2)]
        )
    return splats


def form_block(row_chunk, col_chunk, distance, word, out_ref):
    lane = lax.broadcasted_iota(jnp.int32, (8, TILE), 1)
    direct = row_chunk < col_chunk
    shifts = [shift_up(direct, group, lane) for group in range(TILE // GROUP)]
    splats = block_words(word, row_chunk)
    for row_block in range(2):
        for col_block in range(2):
            lanes = slice(col_block * TILE, (col_block + 1) * TILE)
            for group, shift in enumerate(shifts):
                first = row_block * TILE + group * GROUP
                seen = jnp.left_shift(splats[col_block][row_block], shift) < 0
                halves = []
                for half in range(first, first + GROUP, 8):
                    value = pl.reciprocal(distance[half : half + 8, lanes], approx=True)
                    halves.append(jnp.where(seen, value, 0.0))
                out_ref[first : first + GROUP, lanes] = jnp.concatenate(halves).astype(
                    jnp.bfloat16
                )


def form_own(row_chunk, distance, word, out_ref):
    lane = lax.broadcasted_iota(jnp.int32, (8, TILE), 1)
    row = lax.broadcasted_iota(jnp.int32, (8, TILE), 0)
    splats = block_words(word, row_chunk)
    for row_block in range(2):
        for col_block in range(2):
            lanes = slice(col_block * TILE, (col_block + 1) * TILE)
            for group in range(TILE // GROUP):
                first = row_block * TILE + group * GROUP
                halves = []
                for half in range(first, first + GROUP, 8):
                    i, j = row + half, lane + col_block * TILE
                    low, high = jnp.minimum(i, j) % TILE, jnp.maximum(i, j) % TILE
                    shift = 31 - (8 * (low // 32) + high // 16)
                    seen = jnp.left_shift(splats[col_block][row_block], shift) < 0
                    value = pl.reciprocal(distance[half : half + 8, lanes], approx=True)
                    halves.append(jnp.where(seen, value, 0.0))
                out_ref[first : first + GROUP, lanes] = jnp.concatenate(halves).astype(
                    jnp.bfloat16
                )


def read_extra(rows):
    extra = rows.astype(jnp.float32)
    value = extra[12:16].astype(jnp.int32)
    word = value[0:1]
    for place in range(1, 4):
        word = jnp.bitwise_or(word, jnp.left_shift(value[place : place + 1], 8 * place))
    return extra[0:3] + extra[3:6] + extra[6:9], word


def form_all(blocks, me, row_terms, col_terms, words, fields, start, refs, finish_row):
    kernel_ref, distance = refs
    held = {}

    def measure(place):
        t, v, w = blocks[place]
        distance[place % 2] = times(row_terms[t], col_terms[v])

    def add(place):
        t, v, w = blocks[place]
        term = times_transpose(fields(v), kernel_ref[place])
        held[t] = (held[t] if t in held else start(t)) + term
        if place + 1 == len(blocks) or blocks[place + 1][0] != t:
            finish_row(t, held[t])

    measure(0)
    for place, (t, v, w) in enumerate(blocks):
        if place + 1 < len(blocks):
            measure(place + 1)
        slot, out_ref = distance.at[place % 2], kernel_ref.at[place]
        row_chunk = jnp.bitwise_xor(me, FAR * t)
        if t == 0 and v == 0 and w == 0:
            form_own(row_chunk, slot, words[v], out_ref)
        else:
            form_block(row_chunk, jnp.bitwise_xor(me, STEP * v + w), slot, words[v], out_ref)
        if place:
            add(place - 1)
    add(len(blocks) - 1)


def column_terms(rows, terms, col_terms):
    words = []
    for v in range(LINE):
        position, word = read_extra(rows(v))
        words.append(word)
        distance_terms(position, terms.at[v], False)
        col_terms[v] = terms[v].astype(jnp.bfloat16)
    return words


def grid_pack(v0_ref, v1_ref, v2_ref, v3_ref, out_ref):
    for v, ref in enumerate((v0_ref, v1_ref, v2_ref, v3_ref)):
        out_ref[v] = ref[...]


def grid_near(
    scale,
    me_ref,
    packed_ref,
    far_ref,
    seed_hbm,
    area_hbm,
    kernel_ref,
    partial_ref,
    row_terms,
    terms,
    col_terms,
    distance,
    seed_ref,
    area_ref,
    sems,
):
    copies = [
        pltpu.make_async_copy(seed_hbm, seed_ref, sems.at[0]),
        pltpu.make_async_copy(area_hbm, area_ref, sems.at[1]),
    ]
    for copy in copies:
        copy.start()
    rhs_count = seed_ref.shape[0]
    me = me_ref[0]
    words = column_terms(lambda v: packed_ref[v, rhs_count:], terms, col_terms)
    own, _ = read_extra(packed_ref[0, rhs_count:])
    for t, value in enumerate((own, far_ref[...])):
        slot = terms.at[LINE + t]
        distance_terms(value, slot, True)
        row_terms[t] = jnp.transpose(slot[...]).astype(jnp.bfloat16)

    def finish_row(t, value):
        partial_ref[t] = value

    form_all(
        NEAR,
        me,
        row_terms,
        col_terms,
        words,
        lambda v: packed_ref[v, :rhs_count],
        lambda t: 0.0,
        (kernel_ref, distance),
        finish_row,
    )
    for copy in copies:
        copy.wait()
    partial_ref[0] = partial_ref[0] + seed_ref[...] * (1.0 / (area_ref[...] * scale))


def grid_rest(
    me_ref,
    packed_ref,
    core_ref,
    before_ref,
    row_terms,
    kernel_ref,
    partial_ref,
    sent_ref,
    terms,
    col_terms,
    distance,
):
    rhs_count = before_ref.shape[1]
    words = column_terms(lambda v: core_ref[v, rhs_count:], terms, col_terms)

    def finish_row(t, value):
        partial_ref[t] = value
        sent_ref[t * rhs_count : (t + 1) * rhs_count] = value.astype(jnp.bfloat16)

    form_all(
        REST,
        me_ref[0],
        row_terms,
        col_terms,
        words,
        lambda v: core_ref[v, :rhs_count],
        lambda t: before_ref[t],
        (kernel_ref, distance),
        finish_row,
    )
    sent_ref[2 * rhs_count :] = packed_ref[0, rhs_count:]


def product(scaled_ref, kernel_ref, v):
    return times(scaled_ref[0], kernel_ref[v]) + times(scaled_ref[1], kernel_ref[LINE + v])


def grid_second(rest_ref, partial_ref, packed_ref, far_ref, scaled_ref, sent_ref):
    rhs_count = partial_ref.shape[1]
    extras = (packed_ref[0, rhs_count:], far_ref[2 * rhs_count :, :])
    for t in range(2):
        terms = extras[t].astype(jnp.float32)
        factor = terms[9:10] + terms[10:11] + terms[11:12]
        start = (1 - t) * rhs_count
        total = partial_ref[t] + far_ref[start : start + rhs_count].astype(jnp.float32)
        scaled_ref[t] = (factor * total).astype(jnp.bfloat16)
    for v in range(LINE):
        sent_ref[v] = product(scaled_ref, rest_ref, v).astype(jnp.bfloat16)


def grid_third(near_ref, scaled_ref, sum_ref):
    for v in range(LINE):
        sum_ref[v] = product(scaled_ref, near_ref, v)


def grid_fourth(sum_ref, core_ref, q0_ref, q1_ref, q2_ref, q3_ref):
    for v, ref in enumerate((q0_ref, q1_ref, q2_ref, q3_ref)):
        ref[...] = (sum_ref[v] + core_ref[v].astype(jnp.float32)).astype(ref.dtype)


def grid_last(scale, q3_ref, q2_ref, q1_ref, q0_ref, *rest):
    total = q0_ref[...]
    for ref in (q1_ref, q2_ref, q3_ref):
        total = total + ref[...].astype(jnp.float32)
    finish(scale, total, *rest)


def on_grid(adjoint_seed, radiosity, emission, reflectance, area, position, visibility):
    rhs_count, own_width = adjoint_seed.shape
    devices = GRID
    my_index = lax.axis_index("row").astype(jnp.int32).reshape(1)
    scale = 1.0 / math.sqrt(own_width * devices)
    area = area.reshape(1, own_width)
    reflectance = reflectance.reshape(1, own_width)
    smem = pl.BlockSpec(memory_space=pltpu.SMEM)
    vmem = pl.BlockSpec(memory_space=pltpu.VMEM)
    params = pltpu.CompilerParams(vmem_limit_bytes=GRID_BYTES)
    shaped = jax.ShapeDtypeStruct
    field = (rhs_count, own_width)

    def send(value, step):
        return lax.ppermute(value, "row", [(at, at ^ step) for at in range(devices)])

    hbm = pl.BlockSpec(memory_space=pltpu.HBM)
    arguments = [
        pltpu.with_memory_space_constraint(value, pltpu.HBM)
        for value in (position, visibility, area, reflectance, adjoint_seed)
    ]

    def call(body, name, operands, in_specs, out_shape, scratch_shapes=()):
        return pl.pallas_call(
            body,
            in_specs=in_specs,
            out_specs=[vmem] * len(out_shape),
            out_shape=out_shape,
            scratch_shapes=scratch_shapes,
            compiler_params=params,
            name=name,
        )(*operands)

    packed_rows = rhs_count + EXTRA
    own, spot = call(
        functools.partial(prepare, scale),
        "prepare",
        arguments,
        [hbm] * 5,
        [
            shaped((packed_rows, own_width), jnp.bfloat16),
            shaped(position.shape, jnp.float32),
        ],
        [pltpu.VMEM((EXTRA, own_width), jnp.float32)]
        + [pltpu.VMEM(value.shape, value.dtype) for value in arguments]
        + [pltpu.SemaphoreType.DMA((5,))],
    )
    lines = [send(own, STEP * v) for v in range(1, LINE)]
    far_spot = send(spot, FAR)
    first, far_spot = lax.optimization_barrier((own, far_spot))
    packed_shape = shaped((LINE, packed_rows, own_width), jnp.bfloat16)
    (packed,) = call(grid_pack, "grid_pack", (first, *lines), [vmem] * LINE, [packed_shape])
    core = send(packed, 1)
    terms = (TERMS, own_width)
    blocks = shaped((2 * LINE, own_width, own_width), jnp.bfloat16)
    pair = shaped((2,) + field, jnp.float32)
    scratch = [
        pltpu.VMEM((LINE + 2,) + terms, jnp.float32),
        pltpu.VMEM((LINE,) + terms, jnp.bfloat16),
        pltpu.VMEM((2, own_width, own_width), jnp.float32),
    ]
    near, partial, row_terms = call(
        functools.partial(grid_near, scale),
        "grid_near",
        (my_index, packed, far_spot, arguments[4], arguments[2]),
        [smem] + [vmem] * 2 + [hbm] * 2,
        [blocks, pair, shaped((2, own_width, TERMS), jnp.bfloat16)],
        scratch
        + [
            pltpu.VMEM(field, jnp.float32),
            pltpu.VMEM((1, own_width), jnp.float32),
            pltpu.SemaphoreType.DMA((2,)),
        ],
    )
    rest, partial, sent = call(
        grid_rest,
        "grid_rest",
        (my_index, packed, core, partial, row_terms),
        [smem] + [vmem] * 4,
        [blocks, pair, shaped((2 * rhs_count + EXTRA, own_width), jnp.bfloat16)],
        scratch,
    )
    four = (LINE,) + field
    scaled, sent = call(
        grid_second,
        "grid_second",
        (rest, partial, packed, send(sent, FAR)),
        [vmem] * 4,
        [shaped((2,) + field, jnp.bfloat16), shaped(four, jnp.bfloat16)],
    )
    other = send(sent, 1)
    (sums,) = call(
        grid_third, "grid_third", (near, scaled), [vmem] * 2, [shaped(four, jnp.float32)]
    )
    sums = call(
        grid_fourth,
        "grid_fourth",
        (sums, other),
        [vmem] * 2,
        [shaped(field, jnp.float32)] + [shaped(field, jnp.bfloat16)] * 3,
    )
    lines = [send(sums[v], STEP * v) for v in range(1, LINE)]
    adjoint, grad = call(
        functools.partial(grid_last, scale),
        "grid_last",
        (*lines[::-1], sums[0], adjoint_seed, area, reflectance, radiosity, emission),
        [vmem] * 9,
        [shaped(field, jnp.float32), shaped((1, own_width), jnp.float32)],
    )
    return adjoint, grad.reshape(own_width)


def spread_rows(pos_ref, spread):
    for coord in range(3):
        for block in range(spread.shape[1]):
            line = pos_ref[coord : coord + 1, block * TILE : (block + 1) * TILE]
            spread[coord, block] = jnp.transpose(jnp.broadcast_to(line, (TILE, TILE)))


def inverse_square(spread, pos_ref, at, own_block, rows, other_block):
    lanes = pl.ds(other_block * TILE, TILE)
    total = 1.0
    for coord in range(3):
        delta = spread[coord, own_block, rows, :] - pos_ref[at, coord : coord + 1, lanes]
        total = total + delta * delta
    return 1.0 / total


def form_part(me, at, part, words_ref, pos_ref, spread, kernel_ref):
    blocks = spread.shape[1]
    lane = lax.broadcasted_iota(jnp.int32, (GROUP, TILE), 1)
    for own_block in range(blocks):
        row_block = me * blocks + own_block
        for other_block in range(blocks):
            col_block = part * blocks + other_block
            word = words_ref[own_block, col_block]
            direct = row_block < col_block
            for group in range(TILE // GROUP):
                rows = slice(group * GROUP, (group + 1) * GROUP)
                bit = jnp.where(direct, 8 * (group // 2) + lane // 16, 8 * (lane // 32) + group)
                seen = (jnp.right_shift(word, bit) & 1) != 0
                value = inverse_square(spread, pos_ref, at, own_block, rows, other_block)
                value = jnp.where(seen, value, 0.0).astype(jnp.bfloat16)
                kernel_ref[
                    at,
                    own_block * TILE + group * GROUP : own_block * TILE + (group + 1) * GROUP,
                    other_block * TILE : (other_block + 1) * TILE,
                ] = value


def form_diagonal(me, at, words_ref, pos_ref, spread, kernel_ref):
    blocks = spread.shape[1]
    lane = lax.broadcasted_iota(jnp.int32, (TILE, TILE), 1)
    row = lax.broadcasted_iota(jnp.int32, (TILE, TILE), 0)
    low, high = jnp.minimum(row, lane), jnp.maximum(row, lane)
    bit = 8 * (low // 32) + high // 16
    for block in range(blocks):
        word = words_ref[block, me * blocks + block]
        seen = (jnp.right_shift(word, bit) & 1) != 0
        value = inverse_square(spread, pos_ref, at, block, slice(0, TILE), block)
        value = jnp.where(seen, value, 0.0).astype(jnp.bfloat16)
        kernel_ref[
            at, block * TILE : (block + 1) * TILE, block * TILE : (block + 1) * TILE
        ] = value


def gather_sum(every_ref, kernel_ref):
    total = times_transpose(every_ref[0], kernel_ref[0])
    for at in range(1, every_ref.shape[0]):
        total += times_transpose(every_ref[at], kernel_ref[at])
    return total


def first_sweep(
    scale,
    me_ref,
    words_ref,
    own_pos_ref,
    pos_ref,
    every_ref,
    seed_ref,
    area_ref,
    reflectance_ref,
    kernel_ref,
    scaled_ref,
    spread,
    total,
):
    step = pl.program_id(0)
    chunk = pos_ref.shape[0]
    me = me_ref[0]

    @pl.when(step == 0)
    def _():
        spread_rows(own_pos_ref, spread)
        total[...] = jnp.zeros_like(total)

    def form(at, carry):
        form_part(me, at, step * chunk + at, words_ref, pos_ref, spread, kernel_ref)
        return carry

    lax.fori_loop(0, chunk, form, 0)

    @pl.when((me >= step * chunk) & (me < (step + 1) * chunk))
    def _():
        form_diagonal(me, me - step * chunk, words_ref, pos_ref, spread, kernel_ref)

    total[...] += gather_sum(every_ref, kernel_ref)

    @pl.when(step == pl.num_programs(0) - 1)
    def _():
        adjoint = seed_ref[...] + (area_ref[...] * scale) * total[...]
        scaled_ref[...] = (reflectance_ref[...] * adjoint).astype(jnp.bfloat16)


def last_sweep(
    scale,
    kernel_ref,
    every_ref,
    seed_ref,
    area_ref,
    reflectance_ref,
    radiosity_ref,
    emission_ref,
    adjoint_ref,
    grad_ref,
    total,
):
    step = pl.program_id(0)

    @pl.when(step == 0)
    def _():
        total[...] = jnp.zeros_like(total)

    total[...] += gather_sum(every_ref, kernel_ref)

    @pl.when(step == pl.num_programs(0) - 1)
    def _():
        finish(
            scale,
            total[...],
            seed_ref,
            area_ref,
            reflectance_ref,
            radiosity_ref,
            emission_ref,
            adjoint_ref,
            grad_ref,
        )


def whole(shape):
    return pl.BlockSpec(shape, lambda step: (0,) * len(shape))


def parts(chunk, shape):
    return pl.BlockSpec((chunk,) + shape, lambda step: (step,) + (0,) * len(shape))


def on_rows(adjoint_seed, radiosity, emission, reflectance, area, position, visibility):
    rhs_count, own_width = adjoint_seed.shape
    devices = lax.axis_size("row")
    my_index = lax.axis_index("row").astype(jnp.int32).reshape(1)
    local_blocks = own_width // TILE
    scale = 1.0 / math.sqrt(own_width * devices)
    chunk = math.gcd(devices, 16)
    area = area.reshape(1, own_width)
    reflectance = reflectance.reshape(1, own_width)
    smem = pl.BlockSpec(memory_space=pltpu.SMEM)
    params = pltpu.CompilerParams(
        dimension_semantics=("arbitrary",), vmem_limit_bytes=VMEM_BYTES
    )

    all_pos = lax.all_gather(position, "row")
    every = lax.all_gather((reflectance * adjoint_seed).astype(jnp.bfloat16), "row")
    kernel, scaled = pl.pallas_call(
        functools.partial(first_sweep, scale),
        grid=(devices // chunk,),
        in_specs=[
            smem,
            smem,
            whole((3, own_width)),
            parts(chunk, (3, own_width)),
            parts(chunk, (rhs_count, own_width)),
            whole((rhs_count, own_width)),
            whole((1, own_width)),
            whole((1, own_width)),
        ],
        out_specs=[parts(chunk, (own_width, own_width)), whole((rhs_count, own_width))],
        out_shape=[
            jax.ShapeDtypeStruct((devices, own_width, own_width), jnp.bfloat16),
            jax.ShapeDtypeStruct((rhs_count, own_width), jnp.bfloat16),
        ],
        scratch_shapes=[
            pltpu.VMEM((3, local_blocks, TILE, TILE), jnp.float32),
            pltpu.VMEM((rhs_count, own_width), jnp.float32),
        ],
        compiler_params=params,
        name="first_sweep",
    )(my_index, visibility, position, all_pos, every, adjoint_seed, area, reflectance)

    every = lax.all_gather(scaled, "row")
    adjoint, grad = pl.pallas_call(
        functools.partial(last_sweep, scale),
        grid=(devices // chunk,),
        in_specs=[
            parts(chunk, (own_width, own_width)),
            parts(chunk, (rhs_count, own_width)),
            whole((rhs_count, own_width)),
            whole((1, own_width)),
            whole((1, own_width)),
            whole((rhs_count, own_width)),
            whole((rhs_count, own_width)),
        ],
        out_specs=[whole((rhs_count, own_width)), whole((1, own_width))],
        out_shape=[
            jax.ShapeDtypeStruct((rhs_count, own_width), jnp.float32),
            jax.ShapeDtypeStruct((1, own_width), jnp.float32),
        ],
        scratch_shapes=[pltpu.VMEM((rhs_count, own_width), jnp.float32)],
        compiler_params=params,
        name="last_sweep",
    )(kernel, every, adjoint_seed, area, reflectance, radiosity, emission)
    return adjoint, grad.reshape(own_width)


def on_device(adjoint_seed, *rest):
    on_grid_shape = lax.axis_size("row") == GRID and adjoint_seed.shape[1] == 2 * TILE
    return (on_grid if on_grid_shape else on_rows)(adjoint_seed, *rest)


def solution(mesh):
    placed = (
        P(None, ("scene", "row")),
        P(None, ("scene", "row")),
        P(None, ("scene", "row")),
        P(("scene", "row")),
        P(("scene", "row")),
        P(None, ("scene", "row")),
        P(("scene", "row"), None),
    )
    return jax.shard_map(
        on_device,
        mesh=mesh,
        in_specs=placed,
        out_specs=(P(None, ("scene", "row")), P(("scene", "row"))),
        check_vma=False,
    )
```

```python
import functools
import math

import jax
import jax.numpy as jnp
from jax import lax
from jax.experimental import pallas as pl
from jax.experimental.pallas import tpu as pltpu
from jax.sharding import PartitionSpec as P

TILE = 128
SWEEPS = 2
GROUP = 16
LINE = 8
GRID = 16
STEP = 2
FAR = 1
EXTRA = 16
TERMS = 32
VMEM_BYTES = 48 * 1024 * 1024
GRID_BYTES = 8 * 1024 * 1024


FIRST = (0, 7, 6, 5, 4)
THEN = (3, 2, 1)
NEAR = [(t, v) for t in range(2) for v in FIRST]
REST = [(t, v) for t in range(2) for v in THEN]


def three_terms(value):
    high = value.astype(jnp.bfloat16).astype(jnp.float32)
    rest = value - high
    middle = rest.astype(jnp.bfloat16).astype(jnp.float32)
    return high, middle, rest - middle


def times_transpose(values, kernel):
    return lax.dot_general(
        values, kernel, (((1,), (1,)), ((), ())), preferred_element_type=jnp.float32
    )


def times(values, kernel):
    return jnp.dot(values, kernel, preferred_element_type=jnp.float32)


def finish(
    scale, total, seed_ref, area_ref, reflectance_ref, radiosity_ref, emission_ref, adjoint_ref, grad_ref
):
    adjoint = seed_ref[...] + (area_ref[...] * scale) * total
    adjoint_ref[...] = adjoint
    change = radiosity_ref[...].astype(jnp.float32) - emission_ref[...].astype(jnp.float32)
    grad_ref[...] = jnp.sum(adjoint * change, axis=0, keepdims=True) / reflectance_ref[...]


def prepare(scale, *refs):
    arguments, (packed_ref, spot_ref, rows, *held, sems) = refs[:5], refs[5:]
    copies = [
        pltpu.make_async_copy(argument, ref, sems.at[at])
        for at, (argument, ref) in enumerate(zip(arguments, held))
    ]
    for copy in copies:
        copy.start()
    rows[...] = jnp.zeros_like(rows)
    for copy in copies:
        copy.wait()
    pos_ref, words_ref, area_ref, reflectance_ref, seed_ref = held
    rhs_count = seed_ref.shape[0]
    for term, value in enumerate(three_terms(pos_ref[...])):
        rows[3 * term : 3 * term + 3, :] = value
    weight = area_ref[...] * scale
    for term, value in enumerate(three_terms(weight * reflectance_ref[...])):
        rows[9 + term : 10 + term, :] = value
    count = words_ref.shape[1]
    for place in range(4):
        part = (jnp.right_shift(words_ref[...], 8 * place) & 255).astype(jnp.float32)
        for local in range(words_ref.shape[0]):
            start = local * TILE
            rows[12 + place : 13 + place, start : start + count] = part[local : local + 1]
    packed_ref[:rhs_count] = (reflectance_ref[...] * seed_ref[...]).astype(jnp.bfloat16)
    packed_ref[rhs_count:] = rows[...].astype(jnp.bfloat16)
    spot_ref[...] = pos_ref[...]


def distance_terms(position, terms, as_rows):
    high, middle, low = three_terms(position)
    norm = jnp.sum(position * position, axis=0, keepdims=True)
    terms[...] = jnp.zeros_like(terms)
    if as_rows:
        for at, value in enumerate((high, high, high, middle, middle, low)):
            terms[3 * at : 3 * at + 3, :] = -2.0 * value
        ones, norms, norm = 21, 18, norm + 1.0
    else:
        for at, value in enumerate((high, middle, low, high, middle, high)):
            terms[3 * at : 3 * at + 3, :] = value
        ones, norms = 18, 21
    terms[ones : ones + 3, :] = jnp.ones_like(high)
    for at, value in enumerate(three_terms(norm)):
        terms[norms + at : norms + at + 1, :] = value


def shift_up(direct, group, lane):
    return 31 - jnp.where(direct, 8 * (group // 2) + lane // 16, 8 * (lane // 32) + group)


def block_words(word, row_chunk):
    splats = []
    for col_block in range(2):
        lanes = jnp.broadcast_to(word[:, col_block * TILE : (col_block + 1) * TILE], (8, TILE))
        lanes = pltpu.roll(lanes, TILE - 2 * row_chunk, 1)
        splats.append(
            [jnp.broadcast_to(lanes[:, at : at + 1], (8, TILE)) for at in range(2)]
        )
    return splats


def form_block(row_chunk, col_chunk, distance, word, out_ref):
    lane = lax.broadcasted_iota(jnp.int32, (8, TILE), 1)
    direct = row_chunk < col_chunk
    shifts = [shift_up(direct, group, lane) for group in range(TILE // GROUP)]
    splats = block_words(word, row_chunk)
    for row_block in range(2):
        for col_block in range(2):
            lanes = slice(col_block * TILE, (col_block + 1) * TILE)
            for group, shift in enumerate(shifts):
                first = row_block * TILE + group * GROUP
                seen = jnp.left_shift(splats[col_block][row_block], shift) < 0
                halves = []
                for half in range(first, first + GROUP, 8):
                    value = pl.reciprocal(distance[half : half + 8, lanes], approx=True)
                    halves.append(jnp.where(seen, value, 0.0))
                out_ref[first : first + GROUP, lanes] = jnp.concatenate(halves).astype(
                    jnp.bfloat16
                )


def form_own(row_chunk, distance, word, out_ref):
    lane = lax.broadcasted_iota(jnp.int32, (8, TILE), 1)
    row = lax.broadcasted_iota(jnp.int32, (8, TILE), 0)
    splats = block_words(word, row_chunk)
    for row_block in range(2):
        for col_block in range(2):
            lanes = slice(col_block * TILE, (col_block + 1) * TILE)
            for group in range(TILE // GROUP):
                first = row_block * TILE + group * GROUP
                halves = []
                for half in range(first, first + GROUP, 8):
                    i, j = row + half, lane + col_block * TILE
                    low, high = jnp.minimum(i, j) % TILE, jnp.maximum(i, j) % TILE
                    shift = 31 - (8 * (low // 32) + high // 16)
                    seen = jnp.left_shift(splats[col_block][row_block], shift) < 0
                    value = pl.reciprocal(distance[half : half + 8, lanes], approx=True)
                    halves.append(jnp.where(seen, value, 0.0))
                out_ref[first : first + GROUP, lanes] = jnp.concatenate(halves).astype(
                    jnp.bfloat16
                )


def read_extra(rows):
    extra = rows.astype(jnp.float32)
    value = extra[12:16].astype(jnp.int32)
    word = value[0:1]
    for place in range(1, 4):
        word = jnp.bitwise_or(word, jnp.left_shift(value[place : place + 1], 8 * place))
    return extra[0:3] + extra[3:6] + extra[6:9], word


def form_all(blocks, me, row_terms, col_terms, words, fields, start, refs, finish_row):
    kernel_ref, distance = refs
    held = {}

    def measure(place):
        t, v = blocks[place]
        distance[place % 2] = times(row_terms[t], col_terms[v])

    def add(place):
        t, v = blocks[place]
        term = times_transpose(fields(v), kernel_ref[place])
        held[t] = (held[t] if t in held else start(t)) + term
        if place + 1 == len(blocks) or blocks[place + 1][0] != t:
            finish_row(t, held[t])

    measure(0)
    for place, (t, v) in enumerate(blocks):
        if place + 1 < len(blocks):
            measure(place + 1)
        slot, out_ref = distance.at[place % 2], kernel_ref.at[place]
        row_chunk = jnp.bitwise_xor(me, FAR * t)
        if t == 0 and v == 0:
            form_own(row_chunk, slot, words[v], out_ref)
        else:
            form_block(row_chunk, jnp.bitwise_xor(me, STEP * v), slot, words[v], out_ref)
        if place:
            add(place - 1)
    add(len(blocks) - 1)


def column_terms(refs, rhs_count, terms, col_terms):
    words = {}
    for at, (v, ref) in enumerate(refs.items()):
        position, words[v] = read_extra(ref[rhs_count:])
        distance_terms(position, terms.at[at], False)
        col_terms[v] = terms[at].astype(jnp.bfloat16)
    return words


def grid_near(scale, me_ref, far_ref, seed_hbm, area_hbm, *refs):
    count = len(FIRST)
    lines = dict(zip(FIRST, refs[:count]))
    kernel_ref, partial_ref, row_terms, terms, col_terms, distance, seed_ref, area_ref, sems = refs[
        count:
    ]
    copies = [
        pltpu.make_async_copy(seed_hbm, seed_ref, sems.at[0]),
        pltpu.make_async_copy(area_hbm, area_ref, sems.at[1]),
    ]
    for copy in copies:
        copy.start()
    rhs_count = seed_ref.shape[0]
    own, _ = read_extra(lines[0][rhs_count:])
    for t, value in enumerate((own, far_ref[...])):
        slot = terms.at[count + t]
        distance_terms(value, slot, True)
        row_terms[t] = jnp.transpose(slot[...]).astype(jnp.bfloat16)
    words = column_terms(lines, rhs_count, terms, col_terms)

    def finish_row(t, value):
        partial_ref[t] = value

    form_all(
        NEAR,
        me_ref[0],
        row_terms,
        col_terms,
        words,
        lambda v: lines[v][:rhs_count],
        lambda t: 0.0,
        (kernel_ref, distance),
        finish_row,
    )
    for copy in copies:
        copy.wait()
    partial_ref[0] = partial_ref[0] + seed_ref[...] * (1.0 / (area_ref[...] * scale))


def grid_rest(me_ref, own_ref, before_ref, row_terms, *refs):
    count = len(THEN)
    lines = dict(zip(THEN, refs[:count]))
    kernel_ref, partial_ref, sent_ref, terms, col_terms, distance = refs[count:]
    rhs_count = before_ref.shape[1]
    words = column_terms(lines, rhs_count, terms, col_terms)

    def finish_row(t, value):
        partial_ref[t] = value
        sent_ref[t * rhs_count : (t + 1) * rhs_count] = value.astype(jnp.bfloat16)

    form_all(
        REST,
        me_ref[0],
        row_terms,
        col_terms,
        words,
        lambda v: lines[v][:rhs_count],
        lambda t: before_ref[t],
        (kernel_ref, distance),
        finish_row,
    )
    sent_ref[2 * rhs_count :] = own_ref[rhs_count:]


def product(scaled_ref, kernel_ref, places):
    return times(scaled_ref[0], kernel_ref[places[0]]) + times(
        scaled_ref[1], kernel_ref[places[1]]
    )


def grid_second(near_ref, partial_ref, own_ref, far_ref, scaled_ref, *out_refs):
    rhs_count = partial_ref.shape[1]
    extras = (own_ref[rhs_count:], far_ref[2 * rhs_count :, :])
    for t in range(2):
        terms = extras[t].astype(jnp.float32)
        factor = terms[9:10] + terms[10:11] + terms[11:12]
        start = (1 - t) * rhs_count
        total = partial_ref[t] + far_ref[start : start + rhs_count].astype(jnp.float32)
        scaled_ref[t] = (factor * total).astype(jnp.bfloat16)
    for v, ref in zip(FIRST[1:], out_refs):
        places = [NEAR.index((t, v)) for t in range(2)]
        ref[...] = product(scaled_ref, near_ref, places).astype(jnp.bfloat16)


def grid_third(near_ref, rest_ref, scaled_ref, own_ref, *out_refs):
    for v, ref in zip(THEN, out_refs):
        places = [REST.index((t, v)) for t in range(2)]
        ref[...] = product(scaled_ref, rest_ref, places).astype(jnp.bfloat16)
    own_ref[...] = product(scaled_ref, near_ref, [NEAR.index((t, 0)) for t in range(2)])


def grid_last(scale, *refs):
    total = refs[LINE - 1][...]
    for ref in refs[: LINE - 1]:
        total = total + ref[...].astype(jnp.float32)
    finish(scale, total, *refs[LINE:])


def on_grid(adjoint_seed, radiosity, emission, reflectance, area, position, visibility):
    rhs_count, own_width = adjoint_seed.shape
    devices = GRID
    my_index = lax.axis_index("row").astype(jnp.int32).reshape(1)
    scale = 1.0 / math.sqrt(own_width * devices)
    area = area.reshape(1, own_width)
    reflectance = reflectance.reshape(1, own_width)
    smem = pl.BlockSpec(memory_space=pltpu.SMEM)
    vmem = pl.BlockSpec(memory_space=pltpu.VMEM)
    params = pltpu.CompilerParams(vmem_limit_bytes=GRID_BYTES)
    shaped = jax.ShapeDtypeStruct
    field = (rhs_count, own_width)

    def send(value, step):
        return lax.ppermute(value, "row", [(at, at ^ step) for at in range(devices)])

    hbm = pl.BlockSpec(memory_space=pltpu.HBM)
    arguments = [
        pltpu.with_memory_space_constraint(value, pltpu.HBM)
        for value in (position, visibility, area, reflectance, adjoint_seed)
    ]

    def call(body, name, operands, in_specs, out_shape, scratch_shapes=()):
        return pl.pallas_call(
            body,
            in_specs=in_specs,
            out_specs=[vmem] * len(out_shape),
            out_shape=out_shape,
            scratch_shapes=scratch_shapes,
            compiler_params=params,
            name=name,
        )(*operands)

    packed_rows = rhs_count + EXTRA
    own, spot = call(
        functools.partial(prepare, scale),
        "prepare",
        arguments,
        [hbm] * 5,
        [
            shaped((packed_rows, own_width), jnp.bfloat16),
            shaped(position.shape, jnp.float32),
        ],
        [pltpu.VMEM((EXTRA, own_width), jnp.float32)]
        + [pltpu.VMEM(value.shape, value.dtype) for value in arguments]
        + [pltpu.SemaphoreType.DMA((5,))],
    )
    lines = {v: send(own, STEP * v) for v in FIRST[1:] + THEN}
    lines[0] = own
    far_spot = send(position, FAR)
    terms = (TERMS, own_width)
    pair = shaped((2,) + field, jnp.float32)
    bfloat16 = shaped(field, jnp.bfloat16)

    def blocks(places):
        return shaped((len(places), own_width, own_width), jnp.bfloat16)

    def scratch(count):
        return [
            pltpu.VMEM((count,) + terms, jnp.float32),
            pltpu.VMEM((LINE,) + terms, jnp.bfloat16),
            pltpu.VMEM((2, own_width, own_width), jnp.float32),
        ]

    near, partial, row_terms = call(
        functools.partial(grid_near, scale),
        "grid_near",
        (my_index, far_spot, arguments[4], arguments[2], *[lines[v] for v in FIRST]),
        [smem, vmem, hbm, hbm] + [vmem] * len(FIRST),
        [blocks(NEAR), pair, shaped((2, own_width, TERMS), jnp.bfloat16)],
        scratch(len(FIRST) + 2)
        + [
            pltpu.VMEM(field, jnp.float32),
            pltpu.VMEM((1, own_width), jnp.float32),
            pltpu.SemaphoreType.DMA((2,)),
        ],
    )
    rest, partial, sent = call(
        grid_rest,
        "grid_rest",
        (my_index, own, partial, row_terms, *[lines[v] for v in THEN]),
        [smem] + [vmem] * (3 + len(THEN)),
        [blocks(REST), pair, shaped((2 * rhs_count + EXTRA, own_width), jnp.bfloat16)],
        scratch(len(THEN)),
    )
    scaled, *sums = call(
        grid_second,
        "grid_second",
        (near, partial, own, send(sent, FAR)),
        [vmem] * 4,
        [shaped((2,) + field, jnp.bfloat16)] + [bfloat16] * (len(FIRST) - 1),
    )
    lines = [send(value, STEP * v) for v, value in zip(FIRST[1:], sums)]
    own_sum, *sums = call(
        grid_third,
        "grid_third",
        (near, rest, scaled),
        [vmem] * 3,
        [shaped(field, jnp.float32)] + [bfloat16] * len(THEN),
    )
    lines += [send(value, STEP * v) for v, value in zip(THEN, sums)]
    adjoint, grad = call(
        functools.partial(grid_last, scale),
        "grid_last",
        (*lines, own_sum, adjoint_seed, area, reflectance, radiosity, emission),
        [vmem] * (LINE + 5),
        [shaped(field, jnp.float32), shaped((1, own_width), jnp.float32)],
    )
    return adjoint, grad.reshape(own_width)


def spread_rows(pos_ref, spread):
    for coord in range(3):
        for block in range(spread.shape[1]):
            line = pos_ref[coord : coord + 1, block * TILE : (block + 1) * TILE]
            spread[coord, block] = jnp.transpose(jnp.broadcast_to(line, (TILE, TILE)))


def inverse_square(spread, pos_ref, at, own_block, rows, other_block):
    lanes = pl.ds(other_block * TILE, TILE)
    total = 1.0
    for coord in range(3):
        delta = spread[coord, own_block, rows, :] - pos_ref[at, coord : coord + 1, lanes]
        total = total + delta * delta
    return 1.0 / total


def form_part(me, at, part, words_ref, pos_ref, spread, kernel_ref):
    blocks = spread.shape[1]
    lane = lax.broadcasted_iota(jnp.int32, (GROUP, TILE), 1)
    for own_block in range(blocks):
        row_block = me * blocks + own_block
        for other_block in range(blocks):
            col_block = part * blocks + other_block
            word = words_ref[own_block, col_block]
            direct = row_block < col_block
            for group in range(TILE // GROUP):
                rows = slice(group * GROUP, (group + 1) * GROUP)
                bit = jnp.where(direct, 8 * (group // 2) + lane // 16, 8 * (lane // 32) + group)
                seen = (jnp.right_shift(word, bit) & 1) != 0
                value = inverse_square(spread, pos_ref, at, own_block, rows, other_block)
                value = jnp.where(seen, value, 0.0).astype(jnp.bfloat16)
                kernel_ref[
                    at,
                    own_block * TILE + group * GROUP : own_block * TILE + (group + 1) * GROUP,
                    other_block * TILE : (other_block + 1) * TILE,
                ] = value


def form_diagonal(me, at, words_ref, pos_ref, spread, kernel_ref):
    blocks = spread.shape[1]
    lane = lax.broadcasted_iota(jnp.int32, (TILE, TILE), 1)
    row = lax.broadcasted_iota(jnp.int32, (TILE, TILE), 0)
    low, high = jnp.minimum(row, lane), jnp.maximum(row, lane)
    bit = 8 * (low // 32) + high // 16
    for block in range(blocks):
        word = words_ref[block, me * blocks + block]
        seen = (jnp.right_shift(word, bit) & 1) != 0
        value = inverse_square(spread, pos_ref, at, block, slice(0, TILE), block)
        value = jnp.where(seen, value, 0.0).astype(jnp.bfloat16)
        kernel_ref[
            at, block * TILE : (block + 1) * TILE, block * TILE : (block + 1) * TILE
        ] = value


def gather_sum(every_ref, kernel_ref):
    total = times_transpose(every_ref[0], kernel_ref[0])
    for at in range(1, every_ref.shape[0]):
        total += times_transpose(every_ref[at], kernel_ref[at])
    return total


def first_sweep(
    scale,
    me_ref,
    words_ref,
    own_pos_ref,
    pos_ref,
    every_ref,
    seed_ref,
    area_ref,
    reflectance_ref,
    kernel_ref,
    scaled_ref,
    spread,
    total,
):
    step = pl.program_id(0)
    chunk = pos_ref.shape[0]
    me = me_ref[0]

    @pl.when(step == 0)
    def _():
        spread_rows(own_pos_ref, spread)
        total[...] = jnp.zeros_like(total)

    def form(at, carry):
        form_part(me, at, step * chunk + at, words_ref, pos_ref, spread, kernel_ref)
        return carry

    lax.fori_loop(0, chunk, form, 0)

    @pl.when((me >= step * chunk) & (me < (step + 1) * chunk))
    def _():
        form_diagonal(me, me - step * chunk, words_ref, pos_ref, spread, kernel_ref)

    total[...] += gather_sum(every_ref, kernel_ref)

    @pl.when(step == pl.num_programs(0) - 1)
    def _():
        adjoint = seed_ref[...] + (area_ref[...] * scale) * total[...]
        scaled_ref[...] = (reflectance_ref[...] * adjoint).astype(jnp.bfloat16)


def last_sweep(
    scale,
    kernel_ref,
    every_ref,
    seed_ref,
    area_ref,
    reflectance_ref,
    radiosity_ref,
    emission_ref,
    adjoint_ref,
    grad_ref,
    total,
):
    step = pl.program_id(0)

    @pl.when(step == 0)
    def _():
        total[...] = jnp.zeros_like(total)

    total[...] += gather_sum(every_ref, kernel_ref)

    @pl.when(step == pl.num_programs(0) - 1)
    def _():
        finish(
            scale,
            total[...],
            seed_ref,
            area_ref,
            reflectance_ref,
            radiosity_ref,
            emission_ref,
            adjoint_ref,
            grad_ref,
        )


def whole(shape):
    return pl.BlockSpec(shape, lambda step: (0,) * len(shape))


def parts(chunk, shape):
    return pl.BlockSpec((chunk,) + shape, lambda step: (step,) + (0,) * len(shape))


def on_rows(adjoint_seed, radiosity, emission, reflectance, area, position, visibility):
    rhs_count, own_width = adjoint_seed.shape
    devices = lax.axis_size("row")
    my_index = lax.axis_index("row").astype(jnp.int32).reshape(1)
    local_blocks = own_width // TILE
    scale = 1.0 / math.sqrt(own_width * devices)
    chunk = math.gcd(devices, 16)
    area = area.reshape(1, own_width)
    reflectance = reflectance.reshape(1, own_width)
    smem = pl.BlockSpec(memory_space=pltpu.SMEM)
    params = pltpu.CompilerParams(
        dimension_semantics=("arbitrary",), vmem_limit_bytes=VMEM_BYTES
    )

    all_pos = lax.all_gather(position, "row")
    every = lax.all_gather((reflectance * adjoint_seed).astype(jnp.bfloat16), "row")
    kernel, scaled = pl.pallas_call(
        functools.partial(first_sweep, scale),
        grid=(devices // chunk,),
        in_specs=[
            smem,
            smem,
            whole((3, own_width)),
            parts(chunk, (3, own_width)),
            parts(chunk, (rhs_count, own_width)),
            whole((rhs_count, own_width)),
            whole((1, own_width)),
            whole((1, own_width)),
        ],
        out_specs=[parts(chunk, (own_width, own_width)), whole((rhs_count, own_width))],
        out_shape=[
            jax.ShapeDtypeStruct((devices, own_width, own_width), jnp.bfloat16),
            jax.ShapeDtypeStruct((rhs_count, own_width), jnp.bfloat16),
        ],
        scratch_shapes=[
            pltpu.VMEM((3, local_blocks, TILE, TILE), jnp.float32),
            pltpu.VMEM((rhs_count, own_width), jnp.float32),
        ],
        compiler_params=params,
        name="first_sweep",
    )(my_index, visibility, position, all_pos, every, adjoint_seed, area, reflectance)

    every = lax.all_gather(scaled, "row")
    adjoint, grad = pl.pallas_call(
        functools.partial(last_sweep, scale),
        grid=(devices // chunk,),
        in_specs=[
            parts(chunk, (own_width, own_width)),
            parts(chunk, (rhs_count, own_width)),
            whole((rhs_count, own_width)),
            whole((1, own_width)),
            whole((1, own_width)),
            whole((rhs_count, own_width)),
            whole((rhs_count, own_width)),
        ],
        out_specs=[whole((rhs_count, own_width)), whole((1, own_width))],
        out_shape=[
            jax.ShapeDtypeStruct((rhs_count, own_width), jnp.float32),
            jax.ShapeDtypeStruct((1, own_width), jnp.float32),
        ],
        scratch_shapes=[pltpu.VMEM((rhs_count, own_width), jnp.float32)],
        compiler_params=params,
        name="last_sweep",
    )(kernel, every, adjoint_seed, area, reflectance, radiosity, emission)
    return adjoint, grad.reshape(own_width)


def on_device(adjoint_seed, *rest):
    on_grid_shape = lax.axis_size("row") == GRID and adjoint_seed.shape[1] == 2 * TILE
    return (on_grid if on_grid_shape else on_rows)(adjoint_seed, *rest)


def solution(mesh):
    placed = (
        P(None, ("scene", "row")),
        P(None, ("scene", "row")),
        P(None, ("scene", "row")),
        P(("scene", "row")),
        P(("scene", "row")),
        P(None, ("scene", "row")),
        P(("scene", "row"), None),
    )
    return jax.shard_map(
        on_device,
        mesh=mesh,
        in_specs=placed,
        out_specs=(P(None, ("scene", "row")), P(("scene", "row"))),
        check_vma=False,
    )
```

```python
import functools
import math

import jax
import jax.numpy as jnp
from jax import lax
from jax.experimental import pallas as pl
from jax.experimental.pallas import tpu as pltpu
from jax.sharding import PartitionSpec as P

TILE = 128
SWEEPS = 2
GROUP = 16
LINE = 4
GRID = 16
STEP = 4
FAR = 2
EXTRA = 16
TERMS = 32
VMEM_BYTES = 48 * 1024 * 1024
GRID_BYTES = 8 * 1024 * 1024


NEAR = [(t, v, 0) for t in range(2) for v in range(LINE)]
REST = [(t, v, 1) for t in range(2) for v in range(LINE)]


def three_terms(value):
    high = value.astype(jnp.bfloat16).astype(jnp.float32)
    rest = value - high
    middle = rest.astype(jnp.bfloat16).astype(jnp.float32)
    return high, middle, rest - middle


def times_transpose(values, kernel):
    return lax.dot_general(
        values, kernel, (((1,), (1,)), ((), ())), preferred_element_type=jnp.float32
    )


def times(values, kernel):
    return jnp.dot(values, kernel, preferred_element_type=jnp.float32)


def finish(
    scale, total, seed_ref, area_ref, reflectance_ref, radiosity_ref, emission_ref, adjoint_ref, grad_ref
):
    adjoint = seed_ref[...] + (area_ref[...] * scale) * total
    adjoint_ref[...] = adjoint
    change = radiosity_ref[...].astype(jnp.float32) - emission_ref[...].astype(jnp.float32)
    grad_ref[...] = jnp.sum(adjoint * change, axis=0, keepdims=True) / reflectance_ref[...]


def prepare(scale, *refs):
    arguments, (packed_ref, spot_ref, rows, *held, sems) = refs[:5], refs[5:]
    copies = [
        pltpu.make_async_copy(argument, ref, sems.at[at])
        for at, (argument, ref) in enumerate(zip(arguments, held))
    ]
    for copy in copies[::-1]:
        copy.start()
    rows[...] = jnp.zeros_like(rows)
    for copy in copies[:-1]:
        copy.wait()
    pos_ref, words_ref, area_ref, reflectance_ref, seed_ref = held
    rhs_count = seed_ref.shape[0]
    for term, value in enumerate(three_terms(pos_ref[...])):
        rows[3 * term : 3 * term + 3, :] = value
    weight = area_ref[...] * scale
    for term, value in enumerate(three_terms(weight * reflectance_ref[...])):
        rows[9 + term : 10 + term, :] = value
    count = words_ref.shape[1]
    for place in range(4):
        part = (jnp.right_shift(words_ref[...], 8 * place) & 255).astype(jnp.float32)
        for local in range(words_ref.shape[0]):
            start = local * TILE
            rows[12 + place : 13 + place, start : start + count] = part[local : local + 1]
    packed_ref[rhs_count:] = rows[...].astype(jnp.bfloat16)
    copies[-1].wait()
    packed_ref[:rhs_count] = (reflectance_ref[...] * seed_ref[...]).astype(jnp.bfloat16)
    spot_ref[...] = pos_ref[...]


def distance_terms(position, terms, as_rows):
    high, middle, low = three_terms(position)
    norm = jnp.sum(position * position, axis=0, keepdims=True)
    terms[...] = jnp.zeros_like(terms)
    if as_rows:
        for at, value in enumerate((high, high, high, middle, middle, low)):
            terms[3 * at : 3 * at + 3, :] = -2.0 * value
        ones, norms, norm = 21, 18, norm + 1.0
    else:
        for at, value in enumerate((high, middle, low, high, middle, high)):
            terms[3 * at : 3 * at + 3, :] = value
        ones, norms = 18, 21
    terms[ones : ones + 3, :] = jnp.ones_like(high)
    for at, value in enumerate(three_terms(norm)):
        terms[norms + at : norms + at + 1, :] = value


def shift_up(direct, group, lane):
    return 31 - jnp.where(direct, 8 * (group // 2) + lane // 16, 8 * (lane // 32) + group)


def block_words(word, row_chunk):
    splats = []
    for col_block in range(2):
        lanes = jnp.broadcast_to(word[:, col_block * TILE : (col_block + 1) * TILE], (8, TILE))
        lanes = pltpu.roll(lanes, TILE - 2 * row_chunk, 1)
        splats.append(
            [jnp.broadcast_to(lanes[:, at : at + 1], (8, TILE)) for at in range(2)]
        )
    return splats


def form_block(row_chunk, col_chunk, distance, word, out_ref):
    lane = lax.broadcasted_iota(jnp.int32, (8, TILE), 1)
    direct = row_chunk < col_chunk
    shifts = [shift_up(direct, group, lane) for group in range(TILE // GROUP)]
    splats = block_words(word, row_chunk)
    for row_block in range(2):
        for col_block in range(2):
            lanes = slice(col_block * TILE, (col_block + 1) * TILE)
            for group, shift in enumerate(shifts):
                first = row_block * TILE + group * GROUP
                seen = jnp.left_shift(splats[col_block][row_block], shift) < 0
                halves = []
                for half in range(first, first + GROUP, 8):
                    value = pl.reciprocal(distance[half : half + 8, lanes], approx=True)
                    halves.append(jnp.where(seen, value, 0.0))
                out_ref[first : first + GROUP, lanes] = jnp.concatenate(halves).astype(
                    jnp.bfloat16
                )


def form_own(row_chunk, distance, word, out_ref):
    lane = lax.broadcasted_iota(jnp.int32, (8, TILE), 1)
    row = lax.broadcasted_iota(jnp.int32, (8, TILE), 0)
    splats = block_words(word, row_chunk)
    for row_block in range(2):
        for col_block in range(2):
            lanes = slice(col_block * TILE, (col_block + 1) * TILE)
            for group in range(TILE // GROUP):
                first = row_block * TILE + group * GROUP
                halves = []
                for half in range(first, first + GROUP, 8):
                    i, j = row + half, lane + col_block * TILE
                    low, high = jnp.minimum(i, j) % TILE, jnp.maximum(i, j) % TILE
                    shift = 31 - (8 * (low // 32) + high // 16)
                    seen = jnp.left_shift(splats[col_block][row_block], shift) < 0
                    value = pl.reciprocal(distance[half : half + 8, lanes], approx=True)
                    halves.append(jnp.where(seen, value, 0.0))
                out_ref[first : first + GROUP, lanes] = jnp.concatenate(halves).astype(
                    jnp.bfloat16
                )


def read_extra(rows):
    extra = rows.astype(jnp.float32)
    value = extra[12:16].astype(jnp.int32)
    word = value[0:1]
    for place in range(1, 4):
        word = jnp.bitwise_or(word, jnp.left_shift(value[place : place + 1], 8 * place))
    return extra[0:3] + extra[3:6] + extra[6:9], word


def form_all(blocks, me, row_terms, col_terms, words, fields, start, refs, finish_row):
    kernel_ref, distance = refs
    held = {}

    def measure(place):
        t, v, w = blocks[place]
        distance[place % 2] = times(row_terms[t], col_terms[v])

    def add(place):
        t, v, w = blocks[place]
        term = times_transpose(fields(v), kernel_ref[place])
        held[t] = (held[t] if t in held else start(t)) + term
        if place + 1 == len(blocks) or blocks[place + 1][0] != t:
            finish_row(t, held[t])

    measure(0)
    for place, (t, v, w) in enumerate(blocks):
        if place + 1 < len(blocks):
            measure(place + 1)
        slot, out_ref = distance.at[place % 2], kernel_ref.at[place]
        row_chunk = jnp.bitwise_xor(me, FAR * t)
        if t == 0 and v == 0 and w == 0:
            form_own(row_chunk, slot, words[v], out_ref)
        else:
            form_block(row_chunk, jnp.bitwise_xor(me, STEP * v + w), slot, words[v], out_ref)
        if place:
            add(place - 1)
    add(len(blocks) - 1)


def column_terms(rows, terms, col_terms):
    words = []
    for v in range(LINE):
        position, word = read_extra(rows(v))
        words.append(word)
        distance_terms(position, terms.at[v], False)
        col_terms[v] = terms[v].astype(jnp.bfloat16)
    return words


def grid_pack(v0_ref, v1_ref, v2_ref, v3_ref, out_ref):
    for v, ref in enumerate((v0_ref, v1_ref, v2_ref, v3_ref)):
        out_ref[v] = ref[...]


def grid_near(
    scale,
    me_ref,
    packed_ref,
    far_ref,
    seed_hbm,
    area_hbm,
    kernel_ref,
    partial_ref,
    row_terms,
    terms,
    col_terms,
    distance,
    seed_ref,
    area_ref,
    sems,
):
    copies = [
        pltpu.make_async_copy(seed_hbm, seed_ref, sems.at[0]),
        pltpu.make_async_copy(area_hbm, area_ref, sems.at[1]),
    ]
    for copy in copies:
        copy.start()
    rhs_count = seed_ref.shape[0]
    me = me_ref[0]
    words = column_terms(lambda v: packed_ref[v, rhs_count:], terms, col_terms)
    own, _ = read_extra(packed_ref[0, rhs_count:])
    for t, value in enumerate((own, far_ref[...])):
        slot = terms.at[LINE + t]
        distance_terms(value, slot, True)
        row_terms[t] = jnp.transpose(slot[...]).astype(jnp.bfloat16)

    def finish_row(t, value):
        partial_ref[t] = value

    form_all(
        NEAR,
        me,
        row_terms,
        col_terms,
        words,
        lambda v: packed_ref[v, :rhs_count],
        lambda t: 0.0,
        (kernel_ref, distance),
        finish_row,
    )
    for copy in copies:
        copy.wait()
    partial_ref[0] = partial_ref[0] + seed_ref[...] * (1.0 / (area_ref[...] * scale))


def grid_rest(
    me_ref,
    packed_ref,
    core_ref,
    before_ref,
    row_terms,
    kernel_ref,
    partial_ref,
    sent_ref,
    terms,
    col_terms,
    distance,
):
    rhs_count = before_ref.shape[1]
    words = column_terms(lambda v: core_ref[v, rhs_count:], terms, col_terms)

    def finish_row(t, value):
        partial_ref[t] = value
        sent_ref[t * rhs_count : (t + 1) * rhs_count] = value.astype(jnp.bfloat16)

    form_all(
        REST,
        me_ref[0],
        row_terms,
        col_terms,
        words,
        lambda v: core_ref[v, :rhs_count],
        lambda t: before_ref[t],
        (kernel_ref, distance),
        finish_row,
    )
    sent_ref[2 * rhs_count :] = packed_ref[0, rhs_count:]


def product(scaled_ref, kernel_ref, v):
    return times(scaled_ref[0], kernel_ref[v]) + times(scaled_ref[1], kernel_ref[LINE + v])


def grid_second(me_ref, rest_ref, partial_ref, packed_ref, both_ref, scaled_ref, sent_ref):
    rhs_count = partial_ref.shape[1]
    far_ref = both_ref.at[1 - me_ref[0] // FAR % 2]
    extras = (packed_ref[0, rhs_count:], far_ref[2 * rhs_count :, :])
    for t in range(2):
        terms = extras[t].astype(jnp.float32)
        factor = terms[9:10] + terms[10:11] + terms[11:12]
        start = (1 - t) * rhs_count
        total = partial_ref[t] + far_ref[start : start + rhs_count].astype(jnp.float32)
        scaled_ref[t] = (factor * total).astype(jnp.bfloat16)
    for v in range(LINE):
        sent_ref[v] = product(scaled_ref, rest_ref, v).astype(jnp.bfloat16)


def grid_third(near_ref, scaled_ref, sum_ref):
    for v in range(LINE):
        sum_ref[v] = product(scaled_ref, near_ref, v)


def grid_fourth(sum_ref, core_ref, q0_ref, q1_ref, q2_ref, q3_ref):
    for v, ref in enumerate((q0_ref, q1_ref, q2_ref, q3_ref)):
        ref[...] = (sum_ref[v] + core_ref[v].astype(jnp.float32)).astype(ref.dtype)


def grid_last(scale, q3_ref, q2_ref, q1_ref, q0_ref, *rest):
    total = q0_ref[...]
    for ref in (q1_ref, q2_ref, q3_ref):
        total = total + ref[...].astype(jnp.float32)
    finish(scale, total, *rest)


def on_grid(adjoint_seed, radiosity, emission, reflectance, area, position, visibility):
    rhs_count, own_width = adjoint_seed.shape
    devices = GRID
    my_index = lax.axis_index("row").astype(jnp.int32).reshape(1)
    scale = 1.0 / math.sqrt(own_width * devices)
    area = area.reshape(1, own_width)
    reflectance = reflectance.reshape(1, own_width)
    smem = pl.BlockSpec(memory_space=pltpu.SMEM)
    vmem = pl.BlockSpec(memory_space=pltpu.VMEM)
    params = pltpu.CompilerParams(vmem_limit_bytes=GRID_BYTES)
    shaped = jax.ShapeDtypeStruct
    field = (rhs_count, own_width)

    def send(value, step):
        return lax.ppermute(value, "row", [(at, at ^ step) for at in range(devices)])

    hbm = pl.BlockSpec(memory_space=pltpu.HBM)
    arguments = [
        pltpu.with_memory_space_constraint(value, pltpu.HBM)
        for value in (position, visibility, area, reflectance, adjoint_seed)
    ]

    def call(body, name, operands, in_specs, out_shape, scratch_shapes=()):
        return pl.pallas_call(
            body,
            in_specs=in_specs,
            out_specs=[vmem] * len(out_shape),
            out_shape=out_shape,
            scratch_shapes=scratch_shapes,
            compiler_params=params,
            name=name,
        )(*operands)

    packed_rows = rhs_count + EXTRA
    own, spot = call(
        functools.partial(prepare, scale),
        "prepare",
        arguments,
        [hbm] * 5,
        [
            shaped((packed_rows, own_width), jnp.bfloat16),
            shaped(position.shape, jnp.float32),
        ],
        [pltpu.VMEM((EXTRA, own_width), jnp.float32)]
        + [pltpu.VMEM(value.shape, value.dtype) for value in arguments]
        + [pltpu.SemaphoreType.DMA((5,))],
    )
    lines = [send(own, STEP * v) for v in range(1, LINE)]
    far_spot = send(spot, FAR)
    first, far_spot = lax.optimization_barrier((own, far_spot))
    packed_shape = shaped((LINE, packed_rows, own_width), jnp.bfloat16)
    (packed,) = call(grid_pack, "grid_pack", (first, *lines), [vmem] * LINE, [packed_shape])
    core = send(packed, 1)
    terms = (TERMS, own_width)
    blocks = shaped((2 * LINE, own_width, own_width), jnp.bfloat16)
    pair = shaped((2,) + field, jnp.float32)
    scratch = [
        pltpu.VMEM((LINE + 2,) + terms, jnp.float32),
        pltpu.VMEM((LINE,) + terms, jnp.bfloat16),
        pltpu.VMEM((2, own_width, own_width), jnp.float32),
    ]
    near, partial, row_terms = call(
        functools.partial(grid_near, scale),
        "grid_near",
        (my_index, packed, far_spot, arguments[4], arguments[2]),
        [smem] + [vmem] * 2 + [hbm] * 2,
        [blocks, pair, shaped((2, own_width, TERMS), jnp.bfloat16)],
        scratch
        + [
            pltpu.VMEM(field, jnp.float32),
            pltpu.VMEM((1, own_width), jnp.float32),
            pltpu.SemaphoreType.DMA((2,)),
        ],
    )
    rest, partial, sent = call(
        grid_rest,
        "grid_rest",
        (my_index, packed, core, partial, row_terms),
        [smem] + [vmem] * 4,
        [blocks, pair, shaped((2 * rhs_count + EXTRA, own_width), jnp.bfloat16)],
        scratch,
    )
    four = (LINE,) + field
    pairs = [[at, at + FAR] for at in range(devices) if at // FAR % 2 == 0]
    both = lax.all_gather(sent, "row", axis_index_groups=pairs)
    scaled, sent = call(
        grid_second,
        "grid_second",
        (my_index, rest, partial, packed, both),
        [smem] + [vmem] * 4,
        [shaped((2,) + field, jnp.bfloat16), shaped(four, jnp.bfloat16)],
    )
    other = send(sent, 1)
    (sums,) = call(
        grid_third, "grid_third", (near, scaled), [vmem] * 2, [shaped(four, jnp.float32)]
    )
    sums = call(
        grid_fourth,
        "grid_fourth",
        (sums, other),
        [vmem] * 2,
        [shaped(field, jnp.float32)] + [shaped(field, jnp.bfloat16)] * 3,
    )
    lines = [send(sums[v], STEP * v) for v in range(1, LINE)]
    adjoint, grad = call(
        functools.partial(grid_last, scale),
        "grid_last",
        (*lines[::-1], sums[0], adjoint_seed, area, reflectance, radiosity, emission),
        [vmem] * 9,
        [shaped(field, jnp.float32), shaped((1, own_width), jnp.float32)],
    )
    return adjoint, grad.reshape(own_width)


def spread_rows(pos_ref, spread):
    for coord in range(3):
        for block in range(spread.shape[1]):
            line = pos_ref[coord : coord + 1, block * TILE : (block + 1) * TILE]
            spread[coord, block] = jnp.transpose(jnp.broadcast_to(line, (TILE, TILE)))


def inverse_square(spread, pos_ref, at, own_block, rows, other_block):
    lanes = pl.ds(other_block * TILE, TILE)
    total = 1.0
    for coord in range(3):
        delta = spread[coord, own_block, rows, :] - pos_ref[at, coord : coord + 1, lanes]
        total = total + delta * delta
    return 1.0 / total


def form_part(me, at, part, words_ref, pos_ref, spread, kernel_ref):
    blocks = spread.shape[1]
    lane = lax.broadcasted_iota(jnp.int32, (GROUP, TILE), 1)
    for own_block in range(blocks):
        row_block = me * blocks + own_block
        for other_block in range(blocks):
            col_block = part * blocks + other_block
            word = words_ref[own_block, col_block]
            direct = row_block < col_block
            for group in range(TILE // GROUP):
                rows = slice(group * GROUP, (group + 1) * GROUP)
                bit = jnp.where(direct, 8 * (group // 2) + lane // 16, 8 * (lane // 32) + group)
                seen = (jnp.right_shift(word, bit) & 1) != 0
                value = inverse_square(spread, pos_ref, at, own_block, rows, other_block)
                value = jnp.where(seen, value, 0.0).astype(jnp.bfloat16)
                kernel_ref[
                    at,
                    own_block * TILE + group * GROUP : own_block * TILE + (group + 1) * GROUP,
                    other_block * TILE : (other_block + 1) * TILE,
                ] = value


def form_diagonal(me, at, words_ref, pos_ref, spread, kernel_ref):
    blocks = spread.shape[1]
    lane = lax.broadcasted_iota(jnp.int32, (TILE, TILE), 1)
    row = lax.broadcasted_iota(jnp.int32, (TILE, TILE), 0)
    low, high = jnp.minimum(row, lane), jnp.maximum(row, lane)
    bit = 8 * (low // 32) + high // 16
    for block in range(blocks):
        word = words_ref[block, me * blocks + block]
        seen = (jnp.right_shift(word, bit) & 1) != 0
        value = inverse_square(spread, pos_ref, at, block, slice(0, TILE), block)
        value = jnp.where(seen, value, 0.0).astype(jnp.bfloat16)
        kernel_ref[
            at, block * TILE : (block + 1) * TILE, block * TILE : (block + 1) * TILE
        ] = value


def gather_sum(every_ref, kernel_ref):
    total = times_transpose(every_ref[0], kernel_ref[0])
    for at in range(1, every_ref.shape[0]):
        total += times_transpose(every_ref[at], kernel_ref[at])
    return total


def first_sweep(
    scale,
    me_ref,
    words_ref,
    own_pos_ref,
    pos_ref,
    every_ref,
    seed_ref,
    area_ref,
    reflectance_ref,
    kernel_ref,
    scaled_ref,
    spread,
    total,
):
    step = pl.program_id(0)
    chunk = pos_ref.shape[0]
    me = me_ref[0]

    @pl.when(step == 0)
    def _():
        spread_rows(own_pos_ref, spread)
        total[...] = jnp.zeros_like(total)

    def form(at, carry):
        form_part(me, at, step * chunk + at, words_ref, pos_ref, spread, kernel_ref)
        return carry

    lax.fori_loop(0, chunk, form, 0)

    @pl.when((me >= step * chunk) & (me < (step + 1) * chunk))
    def _():
        form_diagonal(me, me - step * chunk, words_ref, pos_ref, spread, kernel_ref)

    total[...] += gather_sum(every_ref, kernel_ref)

    @pl.when(step == pl.num_programs(0) - 1)
    def _():
        adjoint = seed_ref[...] + (area_ref[...] * scale) * total[...]
        scaled_ref[...] = (reflectance_ref[...] * adjoint).astype(jnp.bfloat16)


def last_sweep(
    scale,
    kernel_ref,
    every_ref,
    seed_ref,
    area_ref,
    reflectance_ref,
    radiosity_ref,
    emission_ref,
    adjoint_ref,
    grad_ref,
    total,
):
    step = pl.program_id(0)

    @pl.when(step == 0)
    def _():
        total[...] = jnp.zeros_like(total)

    total[...] += gather_sum(every_ref, kernel_ref)

    @pl.when(step == pl.num_programs(0) - 1)
    def _():
        finish(
            scale,
            total[...],
            seed_ref,
            area_ref,
            reflectance_ref,
            radiosity_ref,
            emission_ref,
            adjoint_ref,
            grad_ref,
        )


def whole(shape):
    return pl.BlockSpec(shape, lambda step: (0,) * len(shape))


def parts(chunk, shape):
    return pl.BlockSpec((chunk,) + shape, lambda step: (step,) + (0,) * len(shape))


def on_rows(adjoint_seed, radiosity, emission, reflectance, area, position, visibility):
    rhs_count, own_width = adjoint_seed.shape
    devices = lax.axis_size("row")
    my_index = lax.axis_index("row").astype(jnp.int32).reshape(1)
    local_blocks = own_width // TILE
    scale = 1.0 / math.sqrt(own_width * devices)
    chunk = math.gcd(devices, 16)
    area = area.reshape(1, own_width)
    reflectance = reflectance.reshape(1, own_width)
    smem = pl.BlockSpec(memory_space=pltpu.SMEM)
    params = pltpu.CompilerParams(
        dimension_semantics=("arbitrary",), vmem_limit_bytes=VMEM_BYTES
    )

    all_pos = lax.all_gather(position, "row")
    every = lax.all_gather((reflectance * adjoint_seed).astype(jnp.bfloat16), "row")
    kernel, scaled = pl.pallas_call(
        functools.partial(first_sweep, scale),
        grid=(devices // chunk,),
        in_specs=[
            smem,
            smem,
            whole((3, own_width)),
            parts(chunk, (3, own_width)),
            parts(chunk, (rhs_count, own_width)),
            whole((rhs_count, own_width)),
            whole((1, own_width)),
            whole((1, own_width)),
        ],
        out_specs=[parts(chunk, (own_width, own_width)), whole((rhs_count, own_width))],
        out_shape=[
            jax.ShapeDtypeStruct((devices, own_width, own_width), jnp.bfloat16),
            jax.ShapeDtypeStruct((rhs_count, own_width), jnp.bfloat16),
        ],
        scratch_shapes=[
            pltpu.VMEM((3, local_blocks, TILE, TILE), jnp.float32),
            pltpu.VMEM((rhs_count, own_width), jnp.float32),
        ],
        compiler_params=params,
        name="first_sweep",
    )(my_index, visibility, position, all_pos, every, adjoint_seed, area, reflectance)

    every = lax.all_gather(scaled, "row")
    adjoint, grad = pl.pallas_call(
        functools.partial(last_sweep, scale),
        grid=(devices // chunk,),
        in_specs=[
            parts(chunk, (own_width, own_width)),
            parts(chunk, (rhs_count, own_width)),
            whole((rhs_count, own_width)),
            whole((1, own_width)),
            whole((1, own_width)),
            whole((rhs_count, own_width)),
            whole((rhs_count, own_width)),
        ],
        out_specs=[whole((rhs_count, own_width)), whole((1, own_width))],
        out_shape=[
            jax.ShapeDtypeStruct((rhs_count, own_width), jnp.float32),
            jax.ShapeDtypeStruct((1, own_width), jnp.float32),
        ],
        scratch_shapes=[pltpu.VMEM((rhs_count, own_width), jnp.float32)],
        compiler_params=params,
        name="last_sweep",
    )(kernel, every, adjoint_seed, area, reflectance, radiosity, emission)
    return adjoint, grad.reshape(own_width)


def on_device(adjoint_seed, *rest):
    on_grid_shape = lax.axis_size("row") == GRID and adjoint_seed.shape[1] == 2 * TILE
    return (on_grid if on_grid_shape else on_rows)(adjoint_seed, *rest)


def solution(mesh):
    placed = (
        P(None, ("scene", "row")),
        P(None, ("scene", "row")),
        P(None, ("scene", "row")),
        P(("scene", "row")),
        P(("scene", "row")),
        P(None, ("scene", "row")),
        P(("scene", "row"), None),
    )
    return jax.shard_map(
        on_device,
        mesh=mesh,
        in_specs=placed,
        out_specs=(P(None, ("scene", "row")), P(("scene", "row"))),
        check_vma=False,
    )
```

```python
import functools
import math

import jax
import jax.numpy as jnp
from jax import lax
from jax.experimental import pallas as pl
from jax.experimental.pallas import tpu as pltpu
from jax.sharding import PartitionSpec as P

TILE = 128
SWEEPS = 2
GROUP = 16
LINE = 4
GRID = 16
STEP = 4
FAR = 2
EXTRA = 16
TERMS = 32
VMEM_BYTES = 48 * 1024 * 1024
GRID_BYTES = 8 * 1024 * 1024


NEAR = [(t, v, 0) for t in range(2) for v in range(LINE)]
REST = [(t, v, 1) for t in range(2) for v in range(LINE)]


def three_terms(value):
    high = value.astype(jnp.bfloat16).astype(jnp.float32)
    rest = value - high
    middle = rest.astype(jnp.bfloat16).astype(jnp.float32)
    return high, middle, rest - middle


def times_transpose(values, kernel):
    return lax.dot_general(
        values, kernel, (((1,), (1,)), ((), ())), preferred_element_type=jnp.float32
    )


def times(values, kernel):
    return jnp.dot(values, kernel, preferred_element_type=jnp.float32)


def finish(
    scale, total, seed_ref, area_ref, reflectance_ref, radiosity_ref, emission_ref, adjoint_ref, grad_ref
):
    adjoint = seed_ref[...] + (area_ref[...] * scale) * total
    adjoint_ref[...] = adjoint
    change = radiosity_ref[...].astype(jnp.float32) - emission_ref[...].astype(jnp.float32)
    grad_ref[...] = jnp.sum(adjoint * change, axis=0, keepdims=True) / reflectance_ref[...]


def prepare(scale, *refs):
    arguments, (packed_ref, spot_ref, rows, *held, sems) = refs[:5], refs[5:]
    copies = [
        pltpu.make_async_copy(argument, ref, sems.at[at])
        for at, (argument, ref) in enumerate(zip(arguments, held))
    ]
    for copy in copies[::-1]:
        copy.start()
    rows[...] = jnp.zeros_like(rows)
    for copy in copies[:-1]:
        copy.wait()
    pos_ref, words_ref, area_ref, reflectance_ref, seed_ref = held
    rhs_count = seed_ref.shape[0]
    for term, value in enumerate(three_terms(pos_ref[...])):
        rows[3 * term : 3 * term + 3, :] = value
    weight = area_ref[...] * scale
    for term, value in enumerate(three_terms(weight * reflectance_ref[...])):
        rows[9 + term : 10 + term, :] = value
    count = words_ref.shape[1]
    for place in range(4):
        part = (jnp.right_shift(words_ref[...], 8 * place) & 255).astype(jnp.float32)
        for local in range(words_ref.shape[0]):
            start = local * TILE
            rows[12 + place : 13 + place, start : start + count] = part[local : local + 1]
    packed_ref[rhs_count:] = rows[...].astype(jnp.bfloat16)
    copies[-1].wait()
    packed_ref[:rhs_count] = (reflectance_ref[...] * seed_ref[...]).astype(jnp.bfloat16)
    spot_ref[...] = pos_ref[...]


def distance_terms(position, terms, as_rows):
    high, middle, low = three_terms(position)
    norm = jnp.sum(position * position, axis=0, keepdims=True)
    terms[...] = jnp.zeros_like(terms)
    if as_rows:
        for at, value in enumerate((high, high, high, middle, middle, low)):
            terms[3 * at : 3 * at + 3, :] = -2.0 * value
        ones, norms, norm = 21, 18, norm + 1.0
    else:
        for at, value in enumerate((high, middle, low, high, middle, high)):
            terms[3 * at : 3 * at + 3, :] = value
        ones, norms = 18, 21
    terms[ones : ones + 3, :] = jnp.ones_like(high)
    for at, value in enumerate(three_terms(norm)):
        terms[norms + at : norms + at + 1, :] = value


def shift_up(direct, group, lane):
    return 31 - jnp.where(direct, 8 * (group // 2) + lane // 16, 8 * (lane // 32) + group)


def block_words(word, row_chunk):
    splats = []
    for col_block in range(2):
        lanes = jnp.broadcast_to(word[:, col_block * TILE : (col_block + 1) * TILE], (8, TILE))
        lanes = pltpu.roll(lanes, TILE - 2 * row_chunk, 1)
        splats.append(
            [jnp.broadcast_to(lanes[:, at : at + 1], (8, TILE)) for at in range(2)]
        )
    return splats


def form_block(row_chunk, col_chunk, distance, word, out_ref):
    lane = lax.broadcasted_iota(jnp.int32, (8, TILE), 1)
    direct = row_chunk < col_chunk
    shifts = [shift_up(direct, group, lane) for group in range(TILE // GROUP)]
    splats = block_words(word, row_chunk)
    for row_block in range(2):
        values = distance(row_block)
        for col_block in range(2):
            lanes = slice(col_block * TILE, (col_block + 1) * TILE)
            for group, shift in enumerate(shifts):
                first = group * GROUP
                seen = jnp.left_shift(splats[col_block][row_block], shift) < 0
                halves = []
                for half in range(first, first + GROUP, 8):
                    value = pl.reciprocal(values[half : half + 8, lanes], approx=True)
                    halves.append(jnp.where(seen, value, 0.0))
                rows = slice(row_block * TILE + first, row_block * TILE + first + GROUP)
                out_ref[rows, lanes] = jnp.concatenate(halves).astype(jnp.bfloat16)


def form_own(row_chunk, distance, word, out_ref):
    lane = lax.broadcasted_iota(jnp.int32, (8, TILE), 1)
    row = lax.broadcasted_iota(jnp.int32, (8, TILE), 0)
    splats = block_words(word, row_chunk)
    for row_block in range(2):
        values = distance(row_block)
        for col_block in range(2):
            lanes = slice(col_block * TILE, (col_block + 1) * TILE)
            for group in range(TILE // GROUP):
                first = group * GROUP
                halves = []
                for half in range(first, first + GROUP, 8):
                    i, j = row + half + row_block * TILE, lane + col_block * TILE
                    low, high = jnp.minimum(i, j) % TILE, jnp.maximum(i, j) % TILE
                    shift = 31 - (8 * (low // 32) + high // 16)
                    seen = jnp.left_shift(splats[col_block][row_block], shift) < 0
                    value = pl.reciprocal(values[half : half + 8, lanes], approx=True)
                    halves.append(jnp.where(seen, value, 0.0))
                rows = slice(row_block * TILE + first, row_block * TILE + first + GROUP)
                out_ref[rows, lanes] = jnp.concatenate(halves).astype(jnp.bfloat16)


def read_extra(rows):
    extra = rows.astype(jnp.float32)
    value = extra[12:16].astype(jnp.int32)
    word = value[0:1]
    for place in range(1, 4):
        word = jnp.bitwise_or(word, jnp.left_shift(value[place : place + 1], 8 * place))
    return extra[0:3] + extra[3:6] + extra[6:9], word


def form_all(blocks, me, row_terms, col_terms, words, fields, start, kernel_ref, finish_row):
    held = {}

    def add(place):
        t, v, w = blocks[place]
        term = times_transpose(fields(v), kernel_ref[place])
        held[t] = (held[t] if t in held else start(t)) + term
        if place + 1 == len(blocks) or blocks[place + 1][0] != t:
            finish_row(t, held[t])

    for place, (t, v, w) in enumerate(blocks):

        def distance(row_block):
            rows = slice(row_block * TILE, (row_block + 1) * TILE)
            return times(row_terms[t, rows, :], col_terms[v])

        out_ref = kernel_ref.at[place]
        row_chunk = jnp.bitwise_xor(me, FAR * t)
        if t == 0 and v == 0 and w == 0:
            form_own(row_chunk, distance, words[v], out_ref)
        else:
            form_block(
                row_chunk, jnp.bitwise_xor(me, STEP * v + w), distance, words[v], out_ref
            )
        if place:
            add(place - 1)
    add(len(blocks) - 1)


def column_terms(rows, terms, col_terms):
    words = []
    for v in range(LINE):
        position, word = read_extra(rows(v))
        words.append(word)
        distance_terms(position, terms.at[v], False)
        col_terms[v] = terms[v].astype(jnp.bfloat16)
    return words


def grid_pack(v0_ref, v1_ref, v2_ref, v3_ref, out_ref):
    for v, ref in enumerate((v0_ref, v1_ref, v2_ref, v3_ref)):
        out_ref[v] = ref[...]


def grid_near(
    scale,
    me_ref,
    packed_ref,
    far_ref,
    seed_hbm,
    area_hbm,
    kernel_ref,
    partial_ref,
    row_terms,
    terms,
    col_terms,
    seed_ref,
    area_ref,
    sems,
):
    copies = [
        pltpu.make_async_copy(seed_hbm, seed_ref, sems.at[0]),
        pltpu.make_async_copy(area_hbm, area_ref, sems.at[1]),
    ]
    for copy in copies:
        copy.start()
    rhs_count = seed_ref.shape[0]
    me = me_ref[0]
    words = column_terms(lambda v: packed_ref[v, rhs_count:], terms, col_terms)
    own, _ = read_extra(packed_ref[0, rhs_count:])
    for t, value in enumerate((own, far_ref[...])):
        slot = terms.at[LINE + t]
        distance_terms(value, slot, True)
        row_terms[t] = jnp.transpose(slot[...]).astype(jnp.bfloat16)

    def finish_row(t, value):
        partial_ref[t] = value

    form_all(
        NEAR,
        me,
        row_terms,
        col_terms,
        words,
        lambda v: packed_ref[v, :rhs_count],
        lambda t: 0.0,
        kernel_ref,
        finish_row,
    )
    for copy in copies:
        copy.wait()
    partial_ref[0] = partial_ref[0] + seed_ref[...] * (1.0 / (area_ref[...] * scale))


def grid_rest(
    me_ref,
    packed_ref,
    core_ref,
    before_ref,
    row_terms,
    kernel_ref,
    partial_ref,
    sent_ref,
    terms,
    col_terms,
):
    rhs_count = before_ref.shape[1]
    words = column_terms(lambda v: core_ref[v, rhs_count:], terms, col_terms)

    def finish_row(t, value):
        partial_ref[t] = value
        sent_ref[t * rhs_count : (t + 1) * rhs_count] = value.astype(jnp.bfloat16)

    form_all(
        REST,
        me_ref[0],
        row_terms,
        col_terms,
        words,
        lambda v: core_ref[v, :rhs_count],
        lambda t: before_ref[t],
        kernel_ref,
        finish_row,
    )
    sent_ref[2 * rhs_count :] = packed_ref[0, rhs_count:]


def product(scaled_ref, kernel_ref, v):
    return times(scaled_ref[0], kernel_ref[v]) + times(scaled_ref[1], kernel_ref[LINE + v])


def grid_second(rest_ref, partial_ref, packed_ref, far_ref, scaled_ref, sent_ref):
    rhs_count = partial_ref.shape[1]
    extras = (packed_ref[0, rhs_count:], far_ref[2 * rhs_count :, :])
    for t in range(2):
        terms = extras[t].astype(jnp.float32)
        factor = terms[9:10] + terms[10:11] + terms[11:12]
        start = (1 - t) * rhs_count
        total = partial_ref[t] + far_ref[start : start + rhs_count].astype(jnp.float32)
        scaled_ref[t] = (factor * total).astype(jnp.bfloat16)
    for v in range(LINE):
        sent_ref[v] = product(scaled_ref, rest_ref, v).astype(jnp.bfloat16)


def grid_third(near_ref, scaled_ref, sum_ref):
    for v in range(LINE):
        sum_ref[v] = product(scaled_ref, near_ref, v)


def grid_fourth(sum_ref, core_ref, q0_ref, q1_ref, q2_ref, q3_ref):
    for v, ref in enumerate((q0_ref, q1_ref, q2_ref, q3_ref)):
        ref[...] = (sum_ref[v] + core_ref[v].astype(jnp.float32)).astype(ref.dtype)


def grid_last(scale, q3_ref, q2_ref, q1_ref, q0_ref, *rest):
    total = q0_ref[...]
    for ref in (q1_ref, q2_ref, q3_ref):
        total = total + ref[...].astype(jnp.float32)
    finish(scale, total, *rest)


def on_grid(adjoint_seed, radiosity, emission, reflectance, area, position, visibility):
    rhs_count, own_width = adjoint_seed.shape
    devices = GRID
    my_index = lax.axis_index("row").astype(jnp.int32).reshape(1)
    scale = 1.0 / math.sqrt(own_width * devices)
    area = area.reshape(1, own_width)
    reflectance = reflectance.reshape(1, own_width)
    smem = pl.BlockSpec(memory_space=pltpu.SMEM)
    vmem = pl.BlockSpec(memory_space=pltpu.VMEM)
    params = pltpu.CompilerParams(vmem_limit_bytes=GRID_BYTES)
    shaped = jax.ShapeDtypeStruct
    field = (rhs_count, own_width)

    def send(value, step):
        return lax.ppermute(value, "row", [(at, at ^ step) for at in range(devices)])

    hbm = pl.BlockSpec(memory_space=pltpu.HBM)
    arguments = [
        pltpu.with_memory_space_constraint(value, pltpu.HBM)
        for value in (position, visibility, area, reflectance, adjoint_seed)
    ]

    def call(body, name, operands, in_specs, out_shape, scratch_shapes=()):
        return pl.pallas_call(
            body,
            in_specs=in_specs,
            out_specs=[vmem] * len(out_shape),
            out_shape=out_shape,
            scratch_shapes=scratch_shapes,
            compiler_params=params,
            name=name,
        )(*operands)

    packed_rows = rhs_count + EXTRA
    own, spot = call(
        functools.partial(prepare, scale),
        "prepare",
        arguments,
        [hbm] * 5,
        [
            shaped((packed_rows, own_width), jnp.bfloat16),
            shaped(position.shape, jnp.float32),
        ],
        [pltpu.VMEM((EXTRA, own_width), jnp.float32)]
        + [pltpu.VMEM(value.shape, value.dtype) for value in arguments]
        + [pltpu.SemaphoreType.DMA((5,))],
    )
    lines = [send(own, STEP * v) for v in range(1, LINE)]
    far_spot = send(spot, FAR)
    first, far_spot = lax.optimization_barrier((own, far_spot))
    packed_shape = shaped((LINE, packed_rows, own_width), jnp.bfloat16)
    (packed,) = call(grid_pack, "grid_pack", (first, *lines), [vmem] * LINE, [packed_shape])
    core = send(packed, 1)
    terms = (TERMS, own_width)
    blocks = shaped((2 * LINE, own_width, own_width), jnp.bfloat16)
    pair = shaped((2,) + field, jnp.float32)
    scratch = [
        pltpu.VMEM((LINE + 2,) + terms, jnp.float32),
        pltpu.VMEM((LINE,) + terms, jnp.bfloat16),
    ]
    near, partial, row_terms = call(
        functools.partial(grid_near, scale),
        "grid_near",
        (my_index, packed, far_spot, arguments[4], arguments[2]),
        [smem] + [vmem] * 2 + [hbm] * 2,
        [blocks, pair, shaped((2, own_width, TERMS), jnp.bfloat16)],
        scratch
        + [
            pltpu.VMEM(field, jnp.float32),
            pltpu.VMEM((1, own_width), jnp.float32),
            pltpu.SemaphoreType.DMA((2,)),
        ],
    )
    rest, partial, sent = call(
        grid_rest,
        "grid_rest",
        (my_index, packed, core, partial, row_terms),
        [smem] + [vmem] * 4,
        [blocks, pair, shaped((2 * rhs_count + EXTRA, own_width), jnp.bfloat16)],
        scratch,
    )
    four = (LINE,) + field
    scaled, sent = call(
        grid_second,
        "grid_second",
        (rest, partial, packed, send(sent, FAR)),
        [vmem] * 4,
        [shaped((2,) + field, jnp.bfloat16), shaped(four, jnp.bfloat16)],
    )
    other = send(sent, 1)
    (sums,) = call(
        grid_third, "grid_third", (near, scaled), [vmem] * 2, [shaped(four, jnp.float32)]
    )
    sums = call(
        grid_fourth,
        "grid_fourth",
        (sums, other),
        [vmem] * 2,
        [shaped(field, jnp.float32)] + [shaped(field, jnp.bfloat16)] * 3,
    )
    lines = [send(sums[v], STEP * v) for v in range(1, LINE)]
    adjoint, grad = call(
        functools.partial(grid_last, scale),
        "grid_last",
        (*lines[::-1], sums[0], adjoint_seed, area, reflectance, radiosity, emission),
        [vmem] * 9,
        [shaped(field, jnp.float32), shaped((1, own_width), jnp.float32)],
    )
    return adjoint, grad.reshape(own_width)


def spread_rows(pos_ref, spread):
    for coord in range(3):
        for block in range(spread.shape[1]):
            line = pos_ref[coord : coord + 1, block * TILE : (block + 1) * TILE]
            spread[coord, block] = jnp.transpose(jnp.broadcast_to(line, (TILE, TILE)))


def inverse_square(spread, pos_ref, at, own_block, rows, other_block):
    lanes = pl.ds(other_block * TILE, TILE)
    total = 1.0
    for coord in range(3):
        delta = spread[coord, own_block, rows, :] - pos_ref[at, coord : coord + 1, lanes]
        total = total + delta * delta
    return 1.0 / total


def form_part(me, at, part, words_ref, pos_ref, spread, kernel_ref):
    blocks = spread.shape[1]
    lane = lax.broadcasted_iota(jnp.int32, (GROUP, TILE), 1)
    for own_block in range(blocks):
        row_block = me * blocks + own_block
        for other_block in range(blocks):
            col_block = part * blocks + other_block
            word = words_ref[own_block, col_block]
            direct = row_block < col_block
            for group in range(TILE // GROUP):
                rows = slice(group * GROUP, (group + 1) * GROUP)
                bit = jnp.where(direct, 8 * (group // 2) + lane // 16, 8 * (lane // 32) + group)
                seen = (jnp.right_shift(word, bit) & 1) != 0
                value = inverse_square(spread, pos_ref, at, own_block, rows, other_block)
                value = jnp.where(seen, value, 0.0).astype(jnp.bfloat16)
                kernel_ref[
                    at,
                    own_block * TILE + group * GROUP : own_block * TILE + (group + 1) * GROUP,
                    other_block * TILE : (other_block + 1) * TILE,
                ] = value


def form_diagonal(me, at, words_ref, pos_ref, spread, kernel_ref):
    blocks = spread.shape[1]
    lane = lax.broadcasted_iota(jnp.int32, (TILE, TILE), 1)
    row = lax.broadcasted_iota(jnp.int32, (TILE, TILE), 0)
    low, high = jnp.minimum(row, lane), jnp.maximum(row, lane)
    bit = 8 * (low // 32) + high // 16
    for block in range(blocks):
        word = words_ref[block, me * blocks + block]
        seen = (jnp.right_shift(word, bit) & 1) != 0
        value = inverse_square(spread, pos_ref, at, block, slice(0, TILE), block)
        value = jnp.where(seen, value, 0.0).astype(jnp.bfloat16)
        kernel_ref[
            at, block * TILE : (block + 1) * TILE, block * TILE : (block + 1) * TILE
        ] = value


def gather_sum(every_ref, kernel_ref):
    total = times_transpose(every_ref[0], kernel_ref[0])
    for at in range(1, every_ref.shape[0]):
        total += times_transpose(every_ref[at], kernel_ref[at])
    return total


def first_sweep(
    scale,
    me_ref,
    words_ref,
    own_pos_ref,
    pos_ref,
    every_ref,
    seed_ref,
    area_ref,
    reflectance_ref,
    kernel_ref,
    scaled_ref,
    spread,
    total,
):
    step = pl.program_id(0)
    chunk = pos_ref.shape[0]
    me = me_ref[0]

    @pl.when(step == 0)
    def _():
        spread_rows(own_pos_ref, spread)
        total[...] = jnp.zeros_like(total)

    def form(at, carry):
        form_part(me, at, step * chunk + at, words_ref, pos_ref, spread, kernel_ref)
        return carry

    lax.fori_loop(0, chunk, form, 0)

    @pl.when((me >= step * chunk) & (me < (step + 1) * chunk))
    def _():
        form_diagonal(me, me - step * chunk, words_ref, pos_ref, spread, kernel_ref)

    total[...] += gather_sum(every_ref, kernel_ref)

    @pl.when(step == pl.num_programs(0) - 1)
    def _():
        adjoint = seed_ref[...] + (area_ref[...] * scale) * total[...]
        scaled_ref[...] = (reflectance_ref[...] * adjoint).astype(jnp.bfloat16)


def last_sweep(
    scale,
    kernel_ref,
    every_ref,
    seed_ref,
    area_ref,
    reflectance_ref,
    radiosity_ref,
    emission_ref,
    adjoint_ref,
    grad_ref,
    total,
):
    step = pl.program_id(0)

    @pl.when(step == 0)
    def _():
        total[...] = jnp.zeros_like(total)

    total[...] += gather_sum(every_ref, kernel_ref)

    @pl.when(step == pl.num_programs(0) - 1)
    def _():
        finish(
            scale,
            total[...],
            seed_ref,
            area_ref,
            reflectance_ref,
            radiosity_ref,
            emission_ref,
            adjoint_ref,
            grad_ref,
        )


def whole(shape):
    return pl.BlockSpec(shape, lambda step: (0,) * len(shape))


def parts(chunk, shape):
    return pl.BlockSpec((chunk,) + shape, lambda step: (step,) + (0,) * len(shape))


def on_rows(adjoint_seed, radiosity, emission, reflectance, area, position, visibility):
    rhs_count, own_width = adjoint_seed.shape
    devices = lax.axis_size("row")
    my_index = lax.axis_index("row").astype(jnp.int32).reshape(1)
    local_blocks = own_width // TILE
    scale = 1.0 / math.sqrt(own_width * devices)
    chunk = math.gcd(devices, 16)
    area = area.reshape(1, own_width)
    reflectance = reflectance.reshape(1, own_width)
    smem = pl.BlockSpec(memory_space=pltpu.SMEM)
    params = pltpu.CompilerParams(
        dimension_semantics=("arbitrary",), vmem_limit_bytes=VMEM_BYTES
    )

    all_pos = lax.all_gather(position, "row")
    every = lax.all_gather((reflectance * adjoint_seed).astype(jnp.bfloat16), "row")
    kernel, scaled = pl.pallas_call(
        functools.partial(first_sweep, scale),
        grid=(devices // chunk,),
        in_specs=[
            smem,
            smem,
            whole((3, own_width)),
            parts(chunk, (3, own_width)),
            parts(chunk, (rhs_count, own_width)),
            whole((rhs_count, own_width)),
            whole((1, own_width)),
            whole((1, own_width)),
        ],
        out_specs=[parts(chunk, (own_width, own_width)), whole((rhs_count, own_width))],
        out_shape=[
            jax.ShapeDtypeStruct((devices, own_width, own_width), jnp.bfloat16),
            jax.ShapeDtypeStruct((rhs_count, own_width), jnp.bfloat16),
        ],
        scratch_shapes=[
            pltpu.VMEM((3, local_blocks, TILE, TILE), jnp.float32),
            pltpu.VMEM((rhs_count, own_width), jnp.float32),
        ],
        compiler_params=params,
        name="first_sweep",
    )(my_index, visibility, position, all_pos, every, adjoint_seed, area, reflectance)

    every = lax.all_gather(scaled, "row")
    adjoint, grad = pl.pallas_call(
        functools.partial(last_sweep, scale),
        grid=(devices // chunk,),
        in_specs=[
            parts(chunk, (own_width, own_width)),
            parts(chunk, (rhs_count, own_width)),
            whole((rhs_count, own_width)),
            whole((1, own_width)),
            whole((1, own_width)),
            whole((rhs_count, own_width)),
            whole((rhs_count, own_width)),
        ],
        out_specs=[whole((rhs_count, own_width)), whole((1, own_width))],
        out_shape=[
            jax.ShapeDtypeStruct((rhs_count, own_width), jnp.float32),
            jax.ShapeDtypeStruct((1, own_width), jnp.float32),
        ],
        scratch_shapes=[pltpu.VMEM((rhs_count, own_width), jnp.float32)],
        compiler_params=params,
        name="last_sweep",
    )(kernel, every, adjoint_seed, area, reflectance, radiosity, emission)
    return adjoint, grad.reshape(own_width)


def on_device(adjoint_seed, *rest):
    on_grid_shape = lax.axis_size("row") == GRID and adjoint_seed.shape[1] == 2 * TILE
    return (on_grid if on_grid_shape else on_rows)(adjoint_seed, *rest)


def solution(mesh):
    placed = (
        P(None, ("scene", "row")),
        P(None, ("scene", "row")),
        P(None, ("scene", "row")),
        P(("scene", "row")),
        P(("scene", "row")),
        P(None, ("scene", "row")),
        P(("scene", "row"), None),
    )
    return jax.shard_map(
        on_device,
        mesh=mesh,
        in_specs=placed,
        out_specs=(P(None, ("scene", "row")), P(("scene", "row"))),
        check_vma=False,
    )
```

```python
import functools
import math

import jax
import jax.numpy as jnp
from jax import lax
from jax.experimental import pallas as pl
from jax.experimental.pallas import tpu as pltpu
from jax.sharding import PartitionSpec as P

TILE = 128
SWEEPS = 2
GROUP = 16
LINE = 4
GRID = 16
STEP = 4
FAR = 2
EXTRA = 16
TERMS = 32
VMEM_BYTES = 48 * 1024 * 1024
GRID_BYTES = 8 * 1024 * 1024


NEAR = [(t, v, 0) for t in range(2) for v in range(LINE)]
REST = [(t, v, 1) for t in range(2) for v in range(LINE)]


def three_terms(value):
    high = value.astype(jnp.bfloat16).astype(jnp.float32)
    rest = value - high
    middle = rest.astype(jnp.bfloat16).astype(jnp.float32)
    return high, middle, rest - middle


def times_transpose(values, kernel):
    return lax.dot_general(
        values, kernel, (((1,), (1,)), ((), ())), preferred_element_type=jnp.float32
    )


def times(values, kernel):
    return jnp.dot(values, kernel, preferred_element_type=jnp.float32)


def finish(
    scale, total, seed_ref, area_ref, reflectance_ref, radiosity_ref, emission_ref, adjoint_ref, grad_ref
):
    adjoint = seed_ref[...] + (area_ref[...] * scale) * total
    adjoint_ref[...] = adjoint
    change = radiosity_ref[...].astype(jnp.float32) - emission_ref[...].astype(jnp.float32)
    grad_ref[...] = jnp.sum(adjoint * change, axis=0, keepdims=True) / reflectance_ref[...]


def prepare(scale, *refs):
    arguments, (packed_ref, spot_ref, rows, *held, sems) = refs[:5], refs[5:]
    copies = [
        pltpu.make_async_copy(argument, ref, sems.at[at])
        for at, (argument, ref) in enumerate(zip(arguments, held))
    ]
    for copy in copies[::-1]:
        copy.start()
    rows[...] = jnp.zeros_like(rows)
    for copy in copies[:-1]:
        copy.wait()
    pos_ref, words_ref, area_ref, reflectance_ref, seed_ref = held
    rhs_count = seed_ref.shape[0]
    for term, value in enumerate(three_terms(pos_ref[...])):
        rows[3 * term : 3 * term + 3, :] = value
    weight = area_ref[...] * scale
    for term, value in enumerate(three_terms(weight * reflectance_ref[...])):
        rows[9 + term : 10 + term, :] = value
    count = words_ref.shape[1]
    for place in range(4):
        part = (jnp.right_shift(words_ref[...], 8 * place) & 255).astype(jnp.float32)
        for local in range(words_ref.shape[0]):
            start = local * TILE
            rows[12 + place : 13 + place, start : start + count] = part[local : local + 1]
    packed_ref[rhs_count:] = rows[...].astype(jnp.bfloat16)
    copies[-1].wait()
    packed_ref[:rhs_count] = (reflectance_ref[...] * seed_ref[...]).astype(jnp.bfloat16)
    spot_ref[...] = pos_ref[...]


def distance_terms(position, terms, as_rows):
    high, middle, low = three_terms(position)
    norm = jnp.sum(position * position, axis=0, keepdims=True)
    terms[...] = jnp.zeros_like(terms)
    if as_rows:
        for at, value in enumerate((high, high, high, middle, middle, low)):
            terms[3 * at : 3 * at + 3, :] = -2.0 * value
        ones, norms, norm = 21, 18, norm + 1.0
    else:
        for at, value in enumerate((high, middle, low, high, middle, high)):
            terms[3 * at : 3 * at + 3, :] = value
        ones, norms = 18, 21
    terms[ones : ones + 3, :] = jnp.ones_like(high)
    for at, value in enumerate(three_terms(norm)):
        terms[norms + at : norms + at + 1, :] = value


def shift_up(direct, group, lane):
    return 31 - jnp.where(direct, 8 * (group // 2) + lane // 16, 8 * (lane // 32) + group)


def block_words(word, row_chunk):
    splats = []
    for col_block in range(2):
        lanes = jnp.broadcast_to(word[:, col_block * TILE : (col_block + 1) * TILE], (8, TILE))
        lanes = pltpu.roll(lanes, TILE - 2 * row_chunk, 1)
        splats.append(
            [jnp.broadcast_to(lanes[:, at : at + 1], (8, TILE)) for at in range(2)]
        )
    return splats


def form_block(row_chunk, col_chunk, distance, word, out_ref):
    lane = lax.broadcasted_iota(jnp.int32, (8, TILE), 1)
    direct = row_chunk < col_chunk
    shifts = [shift_up(direct, group, lane) for group in range(TILE // GROUP)]
    splats = block_words(word, row_chunk)
    for row_block in range(2):
        for col_block in range(2):
            lanes = slice(col_block * TILE, (col_block + 1) * TILE)
            for group, shift in enumerate(shifts):
                first = row_block * TILE + group * GROUP
                seen = jnp.left_shift(splats[col_block][row_block], shift) < 0
                halves = []
                for half in range(first, first + GROUP, 8):
                    value = pl.reciprocal(distance[half : half + 8, lanes], approx=True)
                    halves.append(jnp.where(seen, value, 0.0))
                out_ref[first : first + GROUP, lanes] = jnp.concatenate(halves).astype(
                    jnp.bfloat16
                )


def form_own(row_chunk, distance, word, out_ref):
    lane = lax.broadcasted_iota(jnp.int32, (8, TILE), 1)
    row = lax.broadcasted_iota(jnp.int32, (8, TILE), 0)
    splats = block_words(word, row_chunk)
    for row_block in range(2):
        for col_block in range(2):
            lanes = slice(col_block * TILE, (col_block + 1) * TILE)
            for group in range(TILE // GROUP):
                first = row_block * TILE + group * GROUP
                halves = []
                for half in range(first, first + GROUP, 8):
                    i, j = row + half, lane + col_block * TILE
                    low, high = jnp.minimum(i, j) % TILE, jnp.maximum(i, j) % TILE
                    shift = 31 - (8 * (low // 32) + high // 16)
                    seen = jnp.left_shift(splats[col_block][row_block], shift) < 0
                    value = pl.reciprocal(distance[half : half + 8, lanes], approx=True)
                    halves.append(jnp.where(seen, value, 0.0))
                out_ref[first : first + GROUP, lanes] = jnp.concatenate(halves).astype(
                    jnp.bfloat16
                )


def read_extra(rows):
    extra = rows.astype(jnp.float32)
    value = extra[12:16].astype(jnp.int32)
    word = value[0:1]
    for place in range(1, 4):
        word = jnp.bitwise_or(word, jnp.left_shift(value[place : place + 1], 8 * place))
    return extra[0:3] + extra[3:6] + extra[6:9], word


def form_all(blocks, me, row_terms, col_terms, words, fields, start, refs, finish_row):
    kernel_ref, distance = refs
    held = {}

    def measure(place):
        t, v, w = blocks[place]
        distance[place % 2] = times(row_terms[t], col_terms[v])

    def add(place):
        t, v, w = blocks[place]
        term = times_transpose(fields(v), kernel_ref[place])
        held[t] = (held[t] if t in held else start(t)) + term
        if place + 1 == len(blocks) or blocks[place + 1][0] != t:
            finish_row(t, held[t])

    measure(0)
    for place, (t, v, w) in enumerate(blocks):
        if place + 1 < len(blocks):
            measure(place + 1)
        slot, out_ref = distance.at[place % 2], kernel_ref.at[place]
        row_chunk = jnp.bitwise_xor(me, FAR * t)
        if t == 0 and v == 0 and w == 0:
            form_own(row_chunk, slot, words[v], out_ref)
        else:
            form_block(row_chunk, jnp.bitwise_xor(me, STEP * v + w), slot, words[v], out_ref)
        if place:
            add(place - 1)
    add(len(blocks) - 1)


def column_terms(rows, terms, col_terms):
    words = []
    for v in range(LINE):
        position, word = read_extra(rows(v))
        words.append(word)
        distance_terms(position, terms.at[v], False)
        col_terms[v] = terms[v].astype(jnp.bfloat16)
    return words


def grid_pack(v0_ref, v1_ref, v2_ref, v3_ref, out_ref):
    for v, ref in enumerate((v0_ref, v1_ref, v2_ref, v3_ref)):
        out_ref[v] = ref[...]


def grid_rows(own_ref, far_ref, row_terms, terms):
    own, _ = read_extra(own_ref[-EXTRA:, :])
    for t, value in enumerate((own, far_ref[...])):
        distance_terms(value, terms.at[t], True)
        row_terms[t] = jnp.transpose(terms[t]).astype(jnp.bfloat16)


def grid_near(
    scale,
    me_ref,
    packed_ref,
    row_terms,
    seed_hbm,
    area_hbm,
    kernel_ref,
    partial_ref,
    terms,
    col_terms,
    distance,
    seed_ref,
    area_ref,
    sems,
):
    copies = [
        pltpu.make_async_copy(seed_hbm, seed_ref, sems.at[0]),
        pltpu.make_async_copy(area_hbm, area_ref, sems.at[1]),
    ]
    for copy in copies:
        copy.start()
    rhs_count = seed_ref.shape[0]
    me = me_ref[0]
    words = column_terms(lambda v: packed_ref[v, rhs_count:], terms, col_terms)

    def finish_row(t, value):
        partial_ref[t] = value

    form_all(
        NEAR,
        me,
        row_terms,
        col_terms,
        words,
        lambda v: packed_ref[v, :rhs_count],
        lambda t: 0.0,
        (kernel_ref, distance),
        finish_row,
    )
    for copy in copies:
        copy.wait()
    partial_ref[0] = partial_ref[0] + seed_ref[...] * (1.0 / (area_ref[...] * scale))


def grid_rest(
    me_ref,
    packed_ref,
    core_ref,
    before_ref,
    row_terms,
    kernel_ref,
    partial_ref,
    sent_ref,
    terms,
    col_terms,
    distance,
):
    rhs_count = before_ref.shape[1]
    words = column_terms(lambda v: core_ref[v, rhs_count:], terms, col_terms)

    def finish_row(t, value):
        partial_ref[t] = value
        sent_ref[t * rhs_count : (t + 1) * rhs_count] = value.astype(jnp.bfloat16)

    form_all(
        REST,
        me_ref[0],
        row_terms,
        col_terms,
        words,
        lambda v: core_ref[v, :rhs_count],
        lambda t: before_ref[t],
        (kernel_ref, distance),
        finish_row,
    )
    sent_ref[2 * rhs_count :] = packed_ref[0, rhs_count:]


def product(scaled_ref, kernel_ref, v):
    return times(scaled_ref[0], kernel_ref[v]) + times(scaled_ref[1], kernel_ref[LINE + v])


def grid_second(rest_ref, partial_ref, packed_ref, far_ref, scaled_ref, sent_ref):
    rhs_count = partial_ref.shape[1]
    extras = (packed_ref[0, rhs_count:], far_ref[2 * rhs_count :, :])
    for t in range(2):
        terms = extras[t].astype(jnp.float32)
        factor = terms[9:10] + terms[10:11] + terms[11:12]
        start = (1 - t) * rhs_count
        total = partial_ref[t] + far_ref[start : start + rhs_count].astype(jnp.float32)
        scaled_ref[t] = (factor * total).astype(jnp.bfloat16)
    for v in range(LINE):
        sent_ref[v] = product(scaled_ref, rest_ref, v).astype(jnp.bfloat16)


def grid_third(near_ref, scaled_ref, sum_ref):
    for v in range(LINE):
        sum_ref[v] = product(scaled_ref, near_ref, v)


def grid_fourth(sum_ref, core_ref, q0_ref, q1_ref, q2_ref, q3_ref):
    for v, ref in enumerate((q0_ref, q1_ref, q2_ref, q3_ref)):
        ref[...] = (sum_ref[v] + core_ref[v].astype(jnp.float32)).astype(ref.dtype)


def grid_last(scale, q3_ref, q2_ref, q1_ref, q0_ref, *rest):
    total = q0_ref[...]
    for ref in (q1_ref, q2_ref, q3_ref):
        total = total + ref[...].astype(jnp.float32)
    finish(scale, total, *rest)


def on_grid(adjoint_seed, radiosity, emission, reflectance, area, position, visibility):
    rhs_count, own_width = adjoint_seed.shape
    devices = GRID
    my_index = lax.axis_index("row").astype(jnp.int32).reshape(1)
    scale = 1.0 / math.sqrt(own_width * devices)
    area = area.reshape(1, own_width)
    reflectance = reflectance.reshape(1, own_width)
    smem = pl.BlockSpec(memory_space=pltpu.SMEM)
    vmem = pl.BlockSpec(memory_space=pltpu.VMEM)
    params = pltpu.CompilerParams(vmem_limit_bytes=GRID_BYTES)
    shaped = jax.ShapeDtypeStruct
    field = (rhs_count, own_width)

    def send(value, step):
        return lax.ppermute(value, "row", [(at, at ^ step) for at in range(devices)])

    hbm = pl.BlockSpec(memory_space=pltpu.HBM)
    arguments = [
        pltpu.with_memory_space_constraint(value, pltpu.HBM)
        for value in (position, visibility, area, reflectance, adjoint_seed)
    ]

    def call(body, name, operands, in_specs, out_shape, scratch_shapes=()):
        return pl.pallas_call(
            body,
            in_specs=in_specs,
            out_specs=[vmem] * len(out_shape),
            out_shape=out_shape,
            scratch_shapes=scratch_shapes,
            compiler_params=params,
            name=name,
        )(*operands)

    packed_rows = rhs_count + EXTRA
    own, spot = call(
        functools.partial(prepare, scale),
        "prepare",
        arguments,
        [hbm] * 5,
        [
            shaped((packed_rows, own_width), jnp.bfloat16),
            shaped(position.shape, jnp.float32),
        ],
        [pltpu.VMEM((EXTRA, own_width), jnp.float32)]
        + [pltpu.VMEM(value.shape, value.dtype) for value in arguments]
        + [pltpu.SemaphoreType.DMA((5,))],
    )
    lines = [send(own, STEP * v) for v in range(1, LINE)]
    terms = (TERMS, own_width)
    (row_terms,) = call(
        grid_rows,
        "grid_rows",
        (own, send(spot, FAR)),
        [vmem] * 2,
        [shaped((2, own_width, TERMS), jnp.bfloat16)],
        [pltpu.VMEM((2,) + terms, jnp.float32)],
    )
    first, row_terms = lax.optimization_barrier((own, row_terms))
    packed_shape = shaped((LINE, packed_rows, own_width), jnp.bfloat16)
    (packed,) = call(grid_pack, "grid_pack", (first, *lines), [vmem] * LINE, [packed_shape])
    core = send(packed, 1)
    blocks = shaped((2 * LINE, own_width, own_width), jnp.bfloat16)
    pair = shaped((2,) + field, jnp.float32)
    scratch = [
        pltpu.VMEM((LINE,) + terms, jnp.float32),
        pltpu.VMEM((LINE,) + terms, jnp.bfloat16),
        pltpu.VMEM((2, own_width, own_width), jnp.float32),
    ]
    near, partial = call(
        functools.partial(grid_near, scale),
        "grid_near",
        (my_index, packed, row_terms, arguments[4], arguments[2]),
        [smem] + [vmem] * 2 + [hbm] * 2,
        [blocks, pair],
        scratch
        + [
            pltpu.VMEM(field, jnp.float32),
            pltpu.VMEM((1, own_width), jnp.float32),
            pltpu.SemaphoreType.DMA((2,)),
        ],
    )
    rest, partial, sent = call(
        grid_rest,
        "grid_rest",
        (my_index, packed, core, partial, row_terms),
        [smem] + [vmem] * 4,
        [blocks, pair, shaped((2 * rhs_count + EXTRA, own_width), jnp.bfloat16)],
        scratch,
    )
    four = (LINE,) + field
    scaled, sent = call(
        grid_second,
        "grid_second",
        (rest, partial, packed, send(sent, FAR)),
        [vmem] * 4,
        [shaped((2,) + field, jnp.bfloat16), shaped(four, jnp.bfloat16)],
    )
    other = send(sent, 1)
    (sums,) = call(
        grid_third, "grid_third", (near, scaled), [vmem] * 2, [shaped(four, jnp.float32)]
    )
    sums = call(
        grid_fourth,
        "grid_fourth",
        (sums, other),
        [vmem] * 2,
        [shaped(field, jnp.float32)] + [shaped(field, jnp.bfloat16)] * 3,
    )
    lines = [send(sums[v], STEP * v) for v in range(1, LINE)]
    adjoint, grad = call(
        functools.partial(grid_last, scale),
        "grid_last",
        (*lines[::-1], sums[0], adjoint_seed, area, reflectance, radiosity, emission),
        [vmem] * 9,
        [shaped(field, jnp.float32), shaped((1, own_width), jnp.float32)],
    )
    return adjoint, grad.reshape(own_width)


def spread_rows(pos_ref, spread):
    for coord in range(3):
        for block in range(spread.shape[1]):
            line = pos_ref[coord : coord + 1, block * TILE : (block + 1) * TILE]
            spread[coord, block] = jnp.transpose(jnp.broadcast_to(line, (TILE, TILE)))


def inverse_square(spread, pos_ref, at, own_block, rows, other_block):
    lanes = pl.ds(other_block * TILE, TILE)
    total = 1.0
    for coord in range(3):
        delta = spread[coord, own_block, rows, :] - pos_ref[at, coord : coord + 1, lanes]
        total = total + delta * delta
    return 1.0 / total


def form_part(me, at, part, words_ref, pos_ref, spread, kernel_ref):
    blocks = spread.shape[1]
    lane = lax.broadcasted_iota(jnp.int32, (GROUP, TILE), 1)
    for own_block in range(blocks):
        row_block = me * blocks + own_block
        for other_block in range(blocks):
            col_block = part * blocks + other_block
            word = words_ref[own_block, col_block]
            direct = row_block < col_block
            for group in range(TILE // GROUP):
                rows = slice(group * GROUP, (group + 1) * GROUP)
                bit = jnp.where(direct, 8 * (group // 2) + lane // 16, 8 * (lane // 32) + group)
                seen = (jnp.right_shift(word, bit) & 1) != 0
                value = inverse_square(spread, pos_ref, at, own_block, rows, other_block)
                value = jnp.where(seen, value, 0.0).astype(jnp.bfloat16)
                kernel_ref[
                    at,
                    own_block * TILE + group * GROUP : own_block * TILE + (group + 1) * GROUP,
                    other_block * TILE : (other_block + 1) * TILE,
                ] = value


def form_diagonal(me, at, words_ref, pos_ref, spread, kernel_ref):
    blocks = spread.shape[1]
    lane = lax.broadcasted_iota(jnp.int32, (TILE, TILE), 1)
    row = lax.broadcasted_iota(jnp.int32, (TILE, TILE), 0)
    low, high = jnp.minimum(row, lane), jnp.maximum(row, lane)
    bit = 8 * (low // 32) + high // 16
    for block in range(blocks):
        word = words_ref[block, me * blocks + block]
        seen = (jnp.right_shift(word, bit) & 1) != 0
        value = inverse_square(spread, pos_ref, at, block, slice(0, TILE), block)
        value = jnp.where(seen, value, 0.0).astype(jnp.bfloat16)
        kernel_ref[
            at, block * TILE : (block + 1) * TILE, block * TILE : (block + 1) * TILE
        ] = value


def gather_sum(every_ref, kernel_ref):
    total = times_transpose(every_ref[0], kernel_ref[0])
    for at in range(1, every_ref.shape[0]):
        total += times_transpose(every_ref[at], kernel_ref[at])
    return total


def first_sweep(
    scale,
    me_ref,
    words_ref,
    own_pos_ref,
    pos_ref,
    every_ref,
    seed_ref,
    area_ref,
    reflectance_ref,
    kernel_ref,
    scaled_ref,
    spread,
    total,
):
    step = pl.program_id(0)
    chunk = pos_ref.shape[0]
    me = me_ref[0]

    @pl.when(step == 0)
    def _():
        spread_rows(own_pos_ref, spread)
        total[...] = jnp.zeros_like(total)

    def form(at, carry):
        form_part(me, at, step * chunk + at, words_ref, pos_ref, spread, kernel_ref)
        return carry

    lax.fori_loop(0, chunk, form, 0)

    @pl.when((me >= step * chunk) & (me < (step + 1) * chunk))
    def _():
        form_diagonal(me, me - step * chunk, words_ref, pos_ref, spread, kernel_ref)

    total[...] += gather_sum(every_ref, kernel_ref)

    @pl.when(step == pl.num_programs(0) - 1)
    def _():
        adjoint = seed_ref[...] + (area_ref[...] * scale) * total[...]
        scaled_ref[...] = (reflectance_ref[...] * adjoint).astype(jnp.bfloat16)


def last_sweep(
    scale,
    kernel_ref,
    every_ref,
    seed_ref,
    area_ref,
    reflectance_ref,
    radiosity_ref,
    emission_ref,
    adjoint_ref,
    grad_ref,
    total,
):
    step = pl.program_id(0)

    @pl.when(step == 0)
    def _():
        total[...] = jnp.zeros_like(total)

    total[...] += gather_sum(every_ref, kernel_ref)

    @pl.when(step == pl.num_programs(0) - 1)
    def _():
        finish(
            scale,
            total[...],
            seed_ref,
            area_ref,
            reflectance_ref,
            radiosity_ref,
            emission_ref,
            adjoint_ref,
            grad_ref,
        )


def whole(shape):
    return pl.BlockSpec(shape, lambda step: (0,) * len(shape))


def parts(chunk, shape):
    return pl.BlockSpec((chunk,) + shape, lambda step: (step,) + (0,) * len(shape))


def on_rows(adjoint_seed, radiosity, emission, reflectance, area, position, visibility):
    rhs_count, own_width = adjoint_seed.shape
    devices = lax.axis_size("row")
    my_index = lax.axis_index("row").astype(jnp.int32).reshape(1)
    local_blocks = own_width // TILE
    scale = 1.0 / math.sqrt(own_width * devices)
    chunk = math.gcd(devices, 16)
    area = area.reshape(1, own_width)
    reflectance = reflectance.reshape(1, own_width)
    smem = pl.BlockSpec(memory_space=pltpu.SMEM)
    params = pltpu.CompilerParams(
        dimension_semantics=("arbitrary",), vmem_limit_bytes=VMEM_BYTES
    )

    all_pos = lax.all_gather(position, "row")
    every = lax.all_gather((reflectance * adjoint_seed).astype(jnp.bfloat16), "row")
    kernel, scaled = pl.pallas_call(
        functools.partial(first_sweep, scale),
        grid=(devices // chunk,),
        in_specs=[
            smem,
            smem,
            whole((3, own_width)),
            parts(chunk, (3, own_width)),
            parts(chunk, (rhs_count, own_width)),
            whole((rhs_count, own_width)),
            whole((1, own_width)),
            whole((1, own_width)),
        ],
        out_specs=[parts(chunk, (own_width, own_width)), whole((rhs_count, own_width))],
        out_shape=[
            jax.ShapeDtypeStruct((devices, own_width, own_width), jnp.bfloat16),
            jax.ShapeDtypeStruct((rhs_count, own_width), jnp.bfloat16),
        ],
        scratch_shapes=[
            pltpu.VMEM((3, local_blocks, TILE, TILE), jnp.float32),
            pltpu.VMEM((rhs_count, own_width), jnp.float32),
        ],
        compiler_params=params,
        name="first_sweep",
    )(my_index, visibility, position, all_pos, every, adjoint_seed, area, reflectance)

    every = lax.all_gather(scaled, "row")
    adjoint, grad = pl.pallas_call(
        functools.partial(last_sweep, scale),
        grid=(devices // chunk,),
        in_specs=[
            parts(chunk, (own_width, own_width)),
            parts(chunk, (rhs_count, own_width)),
            whole((rhs_count, own_width)),
            whole((1, own_width)),
            whole((1, own_width)),
            whole((rhs_count, own_width)),
            whole((rhs_count, own_width)),
        ],
        out_specs=[whole((rhs_count, own_width)), whole((1, own_width))],
        out_shape=[
            jax.ShapeDtypeStruct((rhs_count, own_width), jnp.float32),
            jax.ShapeDtypeStruct((1, own_width), jnp.float32),
        ],
        scratch_shapes=[pltpu.VMEM((rhs_count, own_width), jnp.float32)],
        compiler_params=params,
        name="last_sweep",
    )(kernel, every, adjoint_seed, area, reflectance, radiosity, emission)
    return adjoint, grad.reshape(own_width)


def on_device(adjoint_seed, *rest):
    on_grid_shape = lax.axis_size("row") == GRID and adjoint_seed.shape[1] == 2 * TILE
    return (on_grid if on_grid_shape else on_rows)(adjoint_seed, *rest)


def solution(mesh):
    placed = (
        P(None, ("scene", "row")),
        P(None, ("scene", "row")),
        P(None, ("scene", "row")),
        P(("scene", "row")),
        P(("scene", "row")),
        P(None, ("scene", "row")),
        P(("scene", "row"), None),
    )
    return jax.shard_map(
        on_device,
        mesh=mesh,
        in_specs=placed,
        out_specs=(P(None, ("scene", "row")), P(("scene", "row"))),
        check_vma=False,
    )
```

```python
import functools
import math

import jax
import jax.numpy as jnp
from jax import lax
from jax.experimental import pallas as pl
from jax.experimental.pallas import tpu as pltpu
from jax.sharding import PartitionSpec as P

TILE = 128
SWEEPS = 2
GROUP = 16
LINE = 4
GRID = 16
STEP = 4
FAR = 2
EXTRA = 16
TERMS = 32
VMEM_BYTES = 48 * 1024 * 1024
GRID_BYTES = 8 * 1024 * 1024


NEAR = [(t, v, 0) for t in range(2) for v in range(LINE)]
REST = [(t, v, 1) for t in range(2) for v in range(LINE)]


def three_terms(value):
    high = value.astype(jnp.bfloat16).astype(jnp.float32)
    rest = value - high
    middle = rest.astype(jnp.bfloat16).astype(jnp.float32)
    return high, middle, rest - middle


def times_transpose(values, kernel):
    return lax.dot_general(
        values, kernel, (((1,), (1,)), ((), ())), preferred_element_type=jnp.float32
    )


def times(values, kernel):
    return jnp.dot(values, kernel, preferred_element_type=jnp.float32)


def finish(
    scale, total, seed_ref, area_ref, reflectance_ref, radiosity_ref, emission_ref, adjoint_ref, grad_ref
):
    adjoint = seed_ref[...] + (area_ref[...] * scale) * total
    adjoint_ref[...] = adjoint
    change = radiosity_ref[...].astype(jnp.float32) - emission_ref[...].astype(jnp.float32)
    grad_ref[...] = jnp.sum(adjoint * change, axis=0, keepdims=True) / reflectance_ref[...]


def prepare(scale, *refs):
    arguments, (packed_ref, spot_ref, rows, *held, sems) = refs[:5], refs[5:]
    copies = [
        pltpu.make_async_copy(argument, ref, sems.at[at])
        for at, (argument, ref) in enumerate(zip(arguments, held))
    ]
    for copy in copies[::-1]:
        copy.start()
    rows[...] = jnp.zeros_like(rows)
    for copy in copies[:-1]:
        copy.wait()
    pos_ref, words_ref, area_ref, reflectance_ref, seed_ref = held
    rhs_count = seed_ref.shape[0]
    for term, value in enumerate(three_terms(pos_ref[...])):
        rows[3 * term : 3 * term + 3, :] = value
    weight = area_ref[...] * scale
    for term, value in enumerate(three_terms(weight * reflectance_ref[...])):
        rows[9 + term : 10 + term, :] = value
    count = words_ref.shape[1]
    for place in range(4):
        part = (jnp.right_shift(words_ref[...], 8 * place) & 255).astype(jnp.float32)
        for local in range(words_ref.shape[0]):
            start = local * TILE
            rows[12 + place : 13 + place, start : start + count] = part[local : local + 1]
    packed_ref[rhs_count:] = rows[...].astype(jnp.bfloat16)
    copies[-1].wait()
    packed_ref[:rhs_count] = (reflectance_ref[...] * seed_ref[...]).astype(jnp.bfloat16)
    spot_ref[...] = pos_ref[...]


def distance_terms(position, terms, as_rows):
    high, middle, low = three_terms(position)
    norm = jnp.sum(position * position, axis=0, keepdims=True)
    terms[...] = jnp.zeros_like(terms)
    if as_rows:
        for at, value in enumerate((high, high, high, middle, middle, low)):
            terms[3 * at : 3 * at + 3, :] = -2.0 * value
        ones, norms, norm = 21, 18, norm + 1.0
    else:
        for at, value in enumerate((high, middle, low, high, middle, high)):
            terms[3 * at : 3 * at + 3, :] = value
        ones, norms = 18, 21
    terms[ones : ones + 3, :] = jnp.ones_like(high)
    for at, value in enumerate(three_terms(norm)):
        terms[norms + at : norms + at + 1, :] = value


def shift_up(direct, group, lane):
    return 31 - jnp.where(direct, 8 * (group // 2) + lane // 16, 8 * (lane // 32) + group)


def block_words(word, row_chunk):
    splats = []
    for col_block in range(2):
        lanes = jnp.broadcast_to(word[:, col_block * TILE : (col_block + 1) * TILE], (8, TILE))
        lanes = pltpu.roll(lanes, TILE - 2 * row_chunk, 1)
        splats.append(
            [jnp.broadcast_to(lanes[:, at : at + 1], (8, TILE)) for at in range(2)]
        )
    return splats


def form_block(row_chunk, col_chunk, distance, word, out_ref):
    lane = lax.broadcasted_iota(jnp.int32, (8, TILE), 1)
    direct = row_chunk < col_chunk
    shifts = [shift_up(direct, group, lane) for group in range(TILE // GROUP)]
    splats = block_words(word, row_chunk)
    for row_block in range(2):
        for col_block in range(2):
            lanes = slice(col_block * TILE, (col_block + 1) * TILE)
            for group, shift in enumerate(shifts):
                first = row_block * TILE + group * GROUP
                seen = jnp.left_shift(splats[col_block][row_block], shift) < 0
                halves = []
                for half in range(first, first + GROUP, 8):
                    value = pl.reciprocal(distance[half : half + 8, lanes], approx=True)
                    halves.append(jnp.where(seen, value, 0.0))
                out_ref[first : first + GROUP, lanes] = jnp.concatenate(halves).astype(
                    jnp.bfloat16
                )


def form_own(row_chunk, distance, word, out_ref):
    lane = lax.broadcasted_iota(jnp.int32, (8, TILE), 1)
    row = lax.broadcasted_iota(jnp.int32, (8, TILE), 0)
    splats = block_words(word, row_chunk)
    for row_block in range(2):
        for col_block in range(2):
            lanes = slice(col_block * TILE, (col_block + 1) * TILE)
            for group in range(TILE // GROUP):
                first = row_block * TILE + group * GROUP
                halves = []
                for half in range(first, first + GROUP, 8):
                    i, j = row + half, lane + col_block * TILE
                    low, high = jnp.minimum(i, j) % TILE, jnp.maximum(i, j) % TILE
                    shift = 31 - (8 * (low // 32) + high // 16)
                    seen = jnp.left_shift(splats[col_block][row_block], shift) < 0
                    value = pl.reciprocal(distance[half : half + 8, lanes], approx=True)
                    halves.append(jnp.where(seen, value, 0.0))
                out_ref[first : first + GROUP, lanes] = jnp.concatenate(halves).astype(
                    jnp.bfloat16
                )


def read_extra(rows):
    extra = rows.astype(jnp.float32)
    value = extra[12:16].astype(jnp.int32)
    word = value[0:1]
    for place in range(1, 4):
        word = jnp.bitwise_or(word, jnp.left_shift(value[place : place + 1], 8 * place))
    return extra[0:3] + extra[3:6] + extra[6:9], word


def form_all(blocks, me, row_terms, col_terms, words, fields, start, refs, finish_row):
    kernel_ref, distance = refs
    held = {}

    def measure(place):
        t, v, w = blocks[place]
        distance[place % 2] = times(row_terms[t], col_terms[v])

    def add(place):
        t, v, w = blocks[place]
        term = times_transpose(fields(v), kernel_ref[place])
        held[t] = (held[t] if t in held else start(t)) + term
        if place + 1 == len(blocks) or blocks[place + 1][0] != t:
            finish_row(t, held[t])

    measure(0)
    for place, (t, v, w) in enumerate(blocks):
        if place + 1 < len(blocks):
            measure(place + 1)
        slot, out_ref = distance.at[place % 2], kernel_ref.at[place]
        row_chunk = jnp.bitwise_xor(me, FAR * t)
        if t == 0 and v == 0 and w == 0:
            form_own(row_chunk, slot, words[v], out_ref)
        else:
            form_block(row_chunk, jnp.bitwise_xor(me, STEP * v + w), slot, words[v], out_ref)
        if place:
            add(place - 1)
    add(len(blocks) - 1)


def column_terms(rows, terms, col_terms):
    words = []
    for v in range(LINE):
        position, word = read_extra(rows(v))
        words.append(word)
        distance_terms(position, terms.at[v], False)
        col_terms[v] = terms[v].astype(jnp.bfloat16)
    return words


def grid_pack(v0_ref, v1_ref, v2_ref, v3_ref, out_ref):
    for v, ref in enumerate((v0_ref, v1_ref, v2_ref, v3_ref)):
        out_ref[v] = ref[...]


def grid_rows(own_ref, far_ref, row_terms, terms):
    own, _ = read_extra(own_ref[-EXTRA:, :])
    for t, value in enumerate((own, far_ref[...])):
        distance_terms(value, terms.at[t], True)
        row_terms[t] = jnp.transpose(terms[t]).astype(jnp.bfloat16)


def grid_near(
    me_ref, packed_ref, row_terms, boost_ref, kernel_ref, partial_ref, terms, col_terms, distance
):
    rhs_count = boost_ref.shape[0]
    me = me_ref[0]
    words = column_terms(lambda v: packed_ref[v, rhs_count:], terms, col_terms)

    def finish_row(t, value):
        partial_ref[t] = value

    form_all(
        NEAR,
        me,
        row_terms,
        col_terms,
        words,
        lambda v: packed_ref[v, :rhs_count],
        lambda t: 0.0 if t else boost_ref[...],
        (kernel_ref, distance),
        finish_row,
    )


def grid_rest(
    me_ref,
    packed_ref,
    core_ref,
    before_ref,
    row_terms,
    kernel_ref,
    partial_ref,
    sent_ref,
    terms,
    col_terms,
    distance,
):
    rhs_count = before_ref.shape[1]
    words = column_terms(lambda v: core_ref[v, rhs_count:], terms, col_terms)

    def finish_row(t, value):
        partial_ref[t] = value
        sent_ref[t * rhs_count : (t + 1) * rhs_count] = value.astype(jnp.bfloat16)

    form_all(
        REST,
        me_ref[0],
        row_terms,
        col_terms,
        words,
        lambda v: core_ref[v, :rhs_count],
        lambda t: before_ref[t],
        (kernel_ref, distance),
        finish_row,
    )
    sent_ref[2 * rhs_count :] = packed_ref[0, rhs_count:]


def product(scaled_ref, kernel_ref, v):
    return times(scaled_ref[0], kernel_ref[v]) + times(scaled_ref[1], kernel_ref[LINE + v])


def grid_second(rest_ref, partial_ref, packed_ref, far_ref, scaled_ref, sent_ref):
    rhs_count = partial_ref.shape[1]
    extras = (packed_ref[0, rhs_count:], far_ref[2 * rhs_count :, :])
    for t in range(2):
        terms = extras[t].astype(jnp.float32)
        factor = terms[9:10] + terms[10:11] + terms[11:12]
        start = (1 - t) * rhs_count
        total = partial_ref[t] + far_ref[start : start + rhs_count].astype(jnp.float32)
        scaled_ref[t] = (factor * total).astype(jnp.bfloat16)
    for v in range(LINE):
        sent_ref[v] = product(scaled_ref, rest_ref, v).astype(jnp.bfloat16)


def grid_third(near_ref, scaled_ref, sum_ref):
    for v in range(LINE):
        sum_ref[v] = product(scaled_ref, near_ref, v)


def grid_fourth(sum_ref, core_ref, q0_ref, q1_ref, q2_ref, q3_ref):
    for v, ref in enumerate((q0_ref, q1_ref, q2_ref, q3_ref)):
        ref[...] = (sum_ref[v] + core_ref[v].astype(jnp.float32)).astype(ref.dtype)


def grid_last(scale, q3_ref, q2_ref, q1_ref, q0_ref, *rest):
    total = q0_ref[...]
    for ref in (q1_ref, q2_ref, q3_ref):
        total = total + ref[...].astype(jnp.float32)
    finish(scale, total, *rest)


def on_grid(adjoint_seed, radiosity, emission, reflectance, area, position, visibility):
    rhs_count, own_width = adjoint_seed.shape
    devices = GRID
    my_index = lax.axis_index("row").astype(jnp.int32).reshape(1)
    scale = 1.0 / math.sqrt(own_width * devices)
    area = area.reshape(1, own_width)
    reflectance = reflectance.reshape(1, own_width)
    smem = pl.BlockSpec(memory_space=pltpu.SMEM)
    vmem = pl.BlockSpec(memory_space=pltpu.VMEM)
    params = pltpu.CompilerParams(vmem_limit_bytes=GRID_BYTES)
    shaped = jax.ShapeDtypeStruct
    field = (rhs_count, own_width)

    def send(value, step):
        return lax.ppermute(value, "row", [(at, at ^ step) for at in range(devices)])

    hbm = pl.BlockSpec(memory_space=pltpu.HBM)
    arguments = [
        pltpu.with_memory_space_constraint(value, pltpu.HBM)
        for value in (position, visibility, area, reflectance, adjoint_seed)
    ]

    def call(body, name, operands, in_specs, out_shape, scratch_shapes=()):
        return pl.pallas_call(
            body,
            in_specs=in_specs,
            out_specs=[vmem] * len(out_shape),
            out_shape=out_shape,
            scratch_shapes=scratch_shapes,
            compiler_params=params,
            name=name,
        )(*operands)

    packed_rows = rhs_count + EXTRA
    own, spot = call(
        functools.partial(prepare, scale),
        "prepare",
        arguments,
        [hbm] * 5,
        [
            shaped((packed_rows, own_width), jnp.bfloat16),
            shaped(position.shape, jnp.float32),
        ],
        [pltpu.VMEM((EXTRA, own_width), jnp.float32)]
        + [pltpu.VMEM(value.shape, value.dtype) for value in arguments]
        + [pltpu.SemaphoreType.DMA((5,))],
    )
    lines = [send(own, STEP * v) for v in range(1, LINE)]
    terms = (TERMS, own_width)
    (row_terms,) = call(
        grid_rows,
        "grid_rows",
        (own, send(spot, FAR)),
        [vmem] * 2,
        [shaped((2, own_width, TERMS), jnp.bfloat16)],
        [pltpu.VMEM((2,) + terms, jnp.float32)],
    )
    boost = adjoint_seed * (1.0 / (area * scale))
    first, row_terms, boost = lax.optimization_barrier((own, row_terms, boost))
    packed_shape = shaped((LINE, packed_rows, own_width), jnp.bfloat16)
    (packed,) = call(grid_pack, "grid_pack", (first, *lines), [vmem] * LINE, [packed_shape])
    core = send(packed, 1)
    blocks = shaped((2 * LINE, own_width, own_width), jnp.bfloat16)
    pair = shaped((2,) + field, jnp.float32)
    scratch = [
        pltpu.VMEM((LINE,) + terms, jnp.float32),
        pltpu.VMEM((LINE,) + terms, jnp.bfloat16),
        pltpu.VMEM((2, own_width, own_width), jnp.float32),
    ]
    near, partial = call(
        grid_near,
        "grid_near",
        (my_index, packed, row_terms, boost),
        [smem] + [vmem] * 3,
        [blocks, pair],
        scratch,
    )
    rest, partial, sent = call(
        grid_rest,
        "grid_rest",
        (my_index, packed, core, partial, row_terms),
        [smem] + [vmem] * 4,
        [blocks, pair, shaped((2 * rhs_count + EXTRA, own_width), jnp.bfloat16)],
        scratch,
    )
    four = (LINE,) + field
    scaled, sent = call(
        grid_second,
        "grid_second",
        (rest, partial, packed, send(sent, FAR)),
        [vmem] * 4,
        [shaped((2,) + field, jnp.bfloat16), shaped(four, jnp.bfloat16)],
    )
    other = send(sent, 1)
    (sums,) = call(
        grid_third, "grid_third", (near, scaled), [vmem] * 2, [shaped(four, jnp.float32)]
    )
    sums = call(
        grid_fourth,
        "grid_fourth",
        (sums, other),
        [vmem] * 2,
        [shaped(field, jnp.float32)] + [shaped(field, jnp.bfloat16)] * 3,
    )
    lines = [send(sums[v], STEP * v) for v in range(1, LINE)]
    adjoint, grad = call(
        functools.partial(grid_last, scale),
        "grid_last",
        (*lines[::-1], sums[0], adjoint_seed, area, reflectance, radiosity, emission),
        [vmem] * 9,
        [shaped(field, jnp.float32), shaped((1, own_width), jnp.float32)],
    )
    return adjoint, grad.reshape(own_width)


def spread_rows(pos_ref, spread):
    for coord in range(3):
        for block in range(spread.shape[1]):
            line = pos_ref[coord : coord + 1, block * TILE : (block + 1) * TILE]
            spread[coord, block] = jnp.transpose(jnp.broadcast_to(line, (TILE, TILE)))


def inverse_square(spread, pos_ref, at, own_block, rows, other_block):
    lanes = pl.ds(other_block * TILE, TILE)
    total = 1.0
    for coord in range(3):
        delta = spread[coord, own_block, rows, :] - pos_ref[at, coord : coord + 1, lanes]
        total = total + delta * delta
    return 1.0 / total


def form_part(me, at, part, words_ref, pos_ref, spread, kernel_ref):
    blocks = spread.shape[1]
    lane = lax.broadcasted_iota(jnp.int32, (GROUP, TILE), 1)
    for own_block in range(blocks):
        row_block = me * blocks + own_block
        for other_block in range(blocks):
            col_block = part * blocks + other_block
            word = words_ref[own_block, col_block]
            direct = row_block < col_block
            for group in range(TILE // GROUP):
                rows = slice(group * GROUP, (group + 1) * GROUP)
                bit = jnp.where(direct, 8 * (group // 2) + lane // 16, 8 * (lane // 32) + group)
                seen = (jnp.right_shift(word, bit) & 1) != 0
                value = inverse_square(spread, pos_ref, at, own_block, rows, other_block)
                value = jnp.where(seen, value, 0.0).astype(jnp.bfloat16)
                kernel_ref[
                    at,
                    own_block * TILE + group * GROUP : own_block * TILE + (group + 1) * GROUP,
                    other_block * TILE : (other_block + 1) * TILE,
                ] = value


def form_diagonal(me, at, words_ref, pos_ref, spread, kernel_ref):
    blocks = spread.shape[1]
    lane = lax.broadcasted_iota(jnp.int32, (TILE, TILE), 1)
    row = lax.broadcasted_iota(jnp.int32, (TILE, TILE), 0)
    low, high = jnp.minimum(row, lane), jnp.maximum(row, lane)
    bit = 8 * (low // 32) + high // 16
    for block in range(blocks):
        word = words_ref[block, me * blocks + block]
        seen = (jnp.right_shift(word, bit) & 1) != 0
        value = inverse_square(spread, pos_ref, at, block, slice(0, TILE), block)
        value = jnp.where(seen, value, 0.0).astype(jnp.bfloat16)
        kernel_ref[
            at, block * TILE : (block + 1) * TILE, block * TILE : (block + 1) * TILE
        ] = value


def gather_sum(every_ref, kernel_ref):
    total = times_transpose(every_ref[0], kernel_ref[0])
    for at in range(1, every_ref.shape[0]):
        total += times_transpose(every_ref[at], kernel_ref[at])
    return total


def first_sweep(
    scale,
    me_ref,
    words_ref,
    own_pos_ref,
    pos_ref,
    every_ref,
    seed_ref,
    area_ref,
    reflectance_ref,
    kernel_ref,
    scaled_ref,
    spread,
    total,
):
    step = pl.program_id(0)
    chunk = pos_ref.shape[0]
    me = me_ref[0]

    @pl.when(step == 0)
    def _():
        spread_rows(own_pos_ref, spread)
        total[...] = jnp.zeros_like(total)

    def form(at, carry):
        form_part(me, at, step * chunk + at, words_ref, pos_ref, spread, kernel_ref)
        return carry

    lax.fori_loop(0, chunk, form, 0)

    @pl.when((me >= step * chunk) & (me < (step + 1) * chunk))
    def _():
        form_diagonal(me, me - step * chunk, words_ref, pos_ref, spread, kernel_ref)

    total[...] += gather_sum(every_ref, kernel_ref)

    @pl.when(step == pl.num_programs(0) - 1)
    def _():
        adjoint = seed_ref[...] + (area_ref[...] * scale) * total[...]
        scaled_ref[...] = (reflectance_ref[...] * adjoint).astype(jnp.bfloat16)


def last_sweep(
    scale,
    kernel_ref,
    every_ref,
    seed_ref,
    area_ref,
    reflectance_ref,
    radiosity_ref,
    emission_ref,
    adjoint_ref,
    grad_ref,
    total,
):
    step = pl.program_id(0)

    @pl.when(step == 0)
    def _():
        total[...] = jnp.zeros_like(total)

    total[...] += gather_sum(every_ref, kernel_ref)

    @pl.when(step == pl.num_programs(0) - 1)
    def _():
        finish(
            scale,
            total[...],
            seed_ref,
            area_ref,
            reflectance_ref,
            radiosity_ref,
            emission_ref,
            adjoint_ref,
            grad_ref,
        )


def whole(shape):
    return pl.BlockSpec(shape, lambda step: (0,) * len(shape))


def parts(chunk, shape):
    return pl.BlockSpec((chunk,) + shape, lambda step: (step,) + (0,) * len(shape))


def on_rows(adjoint_seed, radiosity, emission, reflectance, area, position, visibility):
    rhs_count, own_width = adjoint_seed.shape
    devices = lax.axis_size("row")
    my_index = lax.axis_index("row").astype(jnp.int32).reshape(1)
    local_blocks = own_width // TILE
    scale = 1.0 / math.sqrt(own_width * devices)
    chunk = math.gcd(devices, 16)
    area = area.reshape(1, own_width)
    reflectance = reflectance.reshape(1, own_width)
    smem = pl.BlockSpec(memory_space=pltpu.SMEM)
    params = pltpu.CompilerParams(
        dimension_semantics=("arbitrary",), vmem_limit_bytes=VMEM_BYTES
    )

    all_pos = lax.all_gather(position, "row")
    every = lax.all_gather((reflectance * adjoint_seed).astype(jnp.bfloat16), "row")
    kernel, scaled = pl.pallas_call(
        functools.partial(first_sweep, scale),
        grid=(devices // chunk,),
        in_specs=[
            smem,
            smem,
            whole((3, own_width)),
            parts(chunk, (3, own_width)),
            parts(chunk, (rhs_count, own_width)),
            whole((rhs_count, own_width)),
            whole((1, own_width)),
            whole((1, own_width)),
        ],
        out_specs=[parts(chunk, (own_width, own_width)), whole((rhs_count, own_width))],
        out_shape=[
            jax.ShapeDtypeStruct((devices, own_width, own_width), jnp.bfloat16),
            jax.ShapeDtypeStruct((rhs_count, own_width), jnp.bfloat16),
        ],
        scratch_shapes=[
            pltpu.VMEM((3, local_blocks, TILE, TILE), jnp.float32),
            pltpu.VMEM((rhs_count, own_width), jnp.float32),
        ],
        compiler_params=params,
        name="first_sweep",
    )(my_index, visibility, position, all_pos, every, adjoint_seed, area, reflectance)

    every = lax.all_gather(scaled, "row")
    adjoint, grad = pl.pallas_call(
        functools.partial(last_sweep, scale),
        grid=(devices // chunk,),
        in_specs=[
            parts(chunk, (own_width, own_width)),
            parts(chunk, (rhs_count, own_width)),
            whole((rhs_count, own_width)),
            whole((1, own_width)),
            whole((1, own_width)),
            whole((rhs_count, own_width)),
            whole((rhs_count, own_width)),
        ],
        out_specs=[whole((rhs_count, own_width)), whole((1, own_width))],
        out_shape=[
            jax.ShapeDtypeStruct((rhs_count, own_width), jnp.float32),
            jax.ShapeDtypeStruct((1, own_width), jnp.float32),
        ],
        scratch_shapes=[pltpu.VMEM((rhs_count, own_width), jnp.float32)],
        compiler_params=params,
        name="last_sweep",
    )(kernel, every, adjoint_seed, area, reflectance, radiosity, emission)
    return adjoint, grad.reshape(own_width)


def on_device(adjoint_seed, *rest):
    on_grid_shape = lax.axis_size("row") == GRID and adjoint_seed.shape[1] == 2 * TILE
    return (on_grid if on_grid_shape else on_rows)(adjoint_seed, *rest)


def solution(mesh):
    placed = (
        P(None, ("scene", "row")),
        P(None, ("scene", "row")),
        P(None, ("scene", "row")),
        P(("scene", "row")),
        P(("scene", "row")),
        P(None, ("scene", "row")),
        P(("scene", "row"), None),
    )
    return jax.shard_map(
        on_device,
        mesh=mesh,
        in_specs=placed,
        out_specs=(P(None, ("scene", "row")), P(("scene", "row"))),
        check_vma=False,
    )
```
